32 devices in a mesh: blk: 8 (over z, y), gz: 4 (over x, core).
Axes of the slice: x: 2, y: 2, z: 4, core: 2. Of those that a mesh axis runs over, the one named last changes fastest.
Arguments:
- adjoint: float32 [4, 64, 19, 16, 256], P('gz', 'blk'), may hold values from -6 to 6
- velocity: float32 [4, 64, 3, 16, 256], P('gz', 'blk'), may hold values from -0.32 to 0.32
- porosity: float32 [4, 64, 16, 256], P('gz', 'blk'), may hold values from 0 to 1
- block_x: int32 [4, 64], P('gz'), may hold values from 0 to 7, as said below
- neighbours: int32 [4, 64, 6], P('gz'), may hold values from -1 to 63, as said below
- owner_map: int32 [8], replicated, may hold values from 1 to 24, 64 in all
Outputs:
- adjoint_out: float32 [4, 64, 19, 16, 256], P('gz', 'blk')
- smoothed: float32 [4, 8, 48, 16, 128], P('gz', 'blk')
The draws below stay inside these ranges and needn't reach their ends.
Inputs may be any that keep to these rules, and one draw needn't show every extreme that they name: `block_x`: in every layer, block row k holds 8 blocks, one on each device of blk at that device's slot k (slot = device * 8 + k); the columns of one row of one layer are all different. `neighbours`: the entries name the blocks beside a slot in the same row (-x, +x), in the rows k - 1 and k + 1 (-y, +y) and at the same row and column in the layer below and above (-z, +z), as slots of that layer; -1 beyond the window's faces. Design slab j of every layer holds the 2 * owner_map[j] cell rows after those of slabs 0 to j - 1; the entries sum to 64.
All inputs are finite; a program needn't handle non-finite values.
Results may differ from the reference program's by a relative error of at most 0.0001.
Values sent between devices are 32-bit elements; how exact they have to be, the bound alone decides.
No kernel may reach another device: no remote copies, remote signals or barrier semaphores. Data moves between devices by JAX's collectives and lax.ppermute only.
A program may use at most 128 MiB of HBM per device.

```python
import math
import jax
import jax.numpy as jnp
import numpy as np
from jax import lax

B = 16
K = 8
STEPS = 2
LAYERS = 4
COLS = 8
SLOTS = 64
UNITS = 64
MOSTU = 24
ROWS = 48


def layout_columns(key):
    base = jax.random.fold_in(key, 7)
    keys_all = jax.random.split(base, LAYERS * K)
    orders = jax.vmap(lambda single: jax.random.permutation(single, COLS))(keys_all)
    return orders.reshape(LAYERS, K, COLS).astype(jnp.int32)


def draw_block_x(key, part):
    orders = layout_columns(key)
    inverse = jnp.argsort(orders, axis=-1).astype(jnp.int32)
    return jnp.transpose(inverse, (0, 2, 1)).reshape(LAYERS, SLOTS)


def draw_neighbours(key, part):
    orders = layout_columns(key)
    row_ids = jnp.arange(K, dtype=jnp.int32)[None, :, None]
    slot_grid = orders * K + row_ids
    empty_col = jnp.full((LAYERS, K, 1), -1, jnp.int32)
    empty_row = jnp.full((LAYERS, 1, COLS), -1, jnp.int32)
    empty_layer = jnp.full((1, K, COLS), -1, jnp.int32)
    minus_x = jnp.concatenate([empty_col, slot_grid[:, :, :-1]], axis=2)
    plus_x = jnp.concatenate([slot_grid[:, :, 1:], empty_col], axis=2)
    minus_y = jnp.concatenate([empty_row, slot_grid[:, :-1, :]], axis=1)
    plus_y = jnp.concatenate([slot_grid[:, 1:, :], empty_row], axis=1)
    minus_z = jnp.concatenate([empty_layer, slot_grid[:-1]], axis=0)
    plus_z = jnp.concatenate([slot_grid[1:], empty_layer], axis=0)
    grid_table = jnp.stack([minus_x, plus_x, minus_y, plus_y, minus_z, plus_z], axis=-1)
    inverse = jnp.argsort(orders, axis=-1).astype(jnp.int32)
    by_device = jnp.take_along_axis(grid_table, inverse[..., None], axis=2)
    return jnp.transpose(by_device, (0, 2, 1, 3)).reshape(LAYERS, SLOTS, 6).astype(jnp.int32)


def block_scale(own_key, extent, cuts, smallest, top_value):
    def one(dim, shards_of):
        steps = jax.random.uniform(jax.random.fold_in(jax.random.fold_in(own_key, 6), dim), (shards_of,), jnp.float32, smallest / len(cuts), top_value / len(cuts))
        return jnp.repeat(jnp.exp(steps), extent[dim] // shards_of).reshape((-1,) + (1,) * (len(extent) - dim - 1))

    gain = one(*cuts[0])
    for cut in cuts[1:]:
        gain = gain * one(*cut)
    return gain


def profile(count, total, most, lean):
    weights = [(1 << 20) // math.isqrt(grade ** lean) + 1 for grade in range(2, count + 1)]
    surplus, given = total - most - (count - 1), [1] * (count - 1)
    while surplus > 0:
        free = [i for i in range(count - 1) if given[i] < most]
        whole, left = sum([weights[i] for i in free]), surplus
        for i in free:
            more = min(most - given[i], max(1, left * weights[i] // whole), surplus)
            given[i] = given[i] + more
            surplus = surplus - more
    return np.array([most] + given)


def ragged(key, count, total, bound, skew):
    if count == 2:
        one = jax.random.randint(key, (), max(1, total - bound), min(bound, total - 1) + 1)
        return jnp.stack([one, total - one])
    sizes = jnp.asarray(profile(count, total, bound, skew), jnp.int32)
    couples = (count - 1) // 2
    giver, taker = sizes[1:1 + 2 * couples:2], sizes[2:2 + 2 * couples:2]
    slack = jnp.minimum(giver - 1, bound - taker)
    moved = jax.random.randint(jax.random.fold_in(key, 1), (couples,), 0, 1 << 20) % (slack + 1)
    sizes = sizes.at[1:1 + 2 * couples:2].set(giver - moved).at[2:2 + 2 * couples:2].set(taker + moved)
    return sizes[jax.random.permutation(jax.random.fold_in(key, 2), count)]


def normal_values(stream_key, shape, scale, limit, cuts=(), kind=jnp.bfloat16):
    factor_of = block_scale(stream_key, shape, cuts, -0.22, 0.18) if cuts else 1.0
    drawn = jax.random.normal(stream_key, shape, jnp.float32) * scale * factor_of
    return jnp.minimum(jnp.maximum(drawn, -limit), limit).astype(kind)


def setup_inputs(seed: int = 0) -> dict:
    seeds = jax.random.split(jax.random.key(seed), 7)
    adjoint = normal_values(seeds[0], (LAYERS, SLOTS, 19, B, B * B), 1.0, 6.0, ((0, 4), (1, 8)), jnp.float32)
    velocity = normal_values(seeds[1], (LAYERS, SLOTS, 3, B, B * B), 0.08, 0.32, ((0, 4), (1, 8)), jnp.float32)
    porosity = jnp.clip(1.0 * jax.random.uniform(seeds[2], (LAYERS, SLOTS, B, B * B), jnp.float32) ** block_scale(seeds[2], (LAYERS, SLOTS, B, B * B), ((0, 4), (1, 8)), -0.2, 0.2), 0.0, 1.0)
    block_x = draw_block_x(jax.random.fold_in(seeds[6], 71), 0)
    neighbours = draw_neighbours(jax.random.fold_in(seeds[6], 71), 0)
    owner_map = ragged(seeds[5], COLS, UNITS, MOSTU, 2).astype(jnp.int32)
    return {"adjoint": adjoint, "velocity": velocity, "porosity": porosity, "block_x": block_x, "neighbours": neighbours, "owner_map": owner_map}


VELOCITIES = np.array([[0, 0, 0], [1, 0, 0], [-1, 0, 0], [0, 1, 0], [0, -1, 0], [0, 0, 1], [0, 0, -1], [1, 1, 0], [-1, -1, 0], [1, -1, 0], [-1, 1, 0], [1, 0, 1], [-1, 0, -1], [1, 0, -1], [-1, 0, 1], [0, 1, 1], [0, -1, -1], [0, 1, -1], [0, -1, 1]], dtype=np.float32)
WEIGHTS = np.array([1.0 / 3.0] + [1.0 / 18.0] * 6 + [1.0 / 36.0] * 12, dtype=np.float32)
EAST_POPS = [1, 7, 9, 11, 13]
WEST_POPS = [2, 8, 10, 12, 14]
NORTH_POPS = [3, 7, 10, 15, 17]
SOUTH_POPS = [4, 8, 9, 16, 18]
UPPER_POPS = [5, 11, 14, 15, 18]
LOWER_POPS = [6, 12, 13, 16, 17]
RELAX_RATE = 1.25
DRAG_RATE = 0.3
FILTER_TAPS = [1.0 / 3.0, 2.0 / 3.0, 1.0, 2.0 / 3.0, 1.0 / 3.0]


def pop_table(values, rank_count, pop_axis):
    shape = [1] * rank_count
    shape[pop_axis] = values.shape[0]
    return jnp.asarray(values).reshape(shape)


def collide(state, velocity, porosity, pop_axis):
    rank_count = state.ndim
    components = [lax.index_in_dim(velocity, c, pop_axis, keepdims=True) for c in range(3)]
    lattice = [pop_table(VELOCITIES[:, c], rank_count, pop_axis) for c in range(3)]
    weights = pop_table(WEIGHTS, rank_count, pop_axis)
    speed_sq = components[0] * components[0] + components[1] * components[1] + components[2] * components[2]
    along = lattice[0] * components[0] + lattice[1] * components[1] + lattice[2] * components[2]
    weighted = weights * state
    scalar = jnp.sum(weighted * (1.0 + 3.0 * along + 4.5 * along * along - 1.5 * speed_sq), axis=pop_axis, keepdims=True)
    weight_total = jnp.sum(weighted, axis=pop_axis, keepdims=True)
    grown = weighted * (3.0 + 9.0 * along)
    vector_part = [jnp.sum(grown * lattice[c], axis=pop_axis, keepdims=True) - 3.0 * components[c] * weight_total for c in range(3)]
    momentum = [jnp.sum(lattice[c] * state, axis=pop_axis, keepdims=True) for c in range(3)]
    sens_step = components[0] * momentum[0] + components[1] * momentum[1] + components[2] * momentum[2]
    relative = [lattice[c] - components[c] for c in range(3)]
    project_vector = relative[0] * vector_part[0] + relative[1] * vector_part[1] + relative[2] * vector_part[2]
    project_momentum = relative[0] * momentum[0] + relative[1] * momentum[1] + relative[2] * momentum[2]
    collided = (1.0 - RELAX_RATE) * state + RELAX_RATE * (scalar + project_vector) - DRAG_RATE * porosity * project_momentum
    return collided, sens_step


def smooth_axis(field, axis_pos):
    length = field.shape[axis_pos]
    widths = [(0, 0)] * field.ndim
    widths[axis_pos] = (2, 2)
    padded = jnp.pad(field, widths)
    result = FILTER_TAPS[0] * lax.slice_in_dim(padded, 0, length, axis=axis_pos)
    for offset in range(1, 5):
        result = result + FILTER_TAPS[offset] * lax.slice_in_dim(padded, offset, offset + length, axis=axis_pos)
    return result


def take_slots(face, slot_index):
    count = face.shape[1]
    padded = jnp.concatenate([face, jnp.zeros_like(face[:, :1])], axis=1)
    safe = jnp.where(slot_index < 0, count, slot_index).astype(jnp.int32)
    return jax.vmap(lambda layer, picks: layer[picks])(padded, safe)


def stream(collided, neighbours):
    moved = collided
    group = moved[:, :, EAST_POPS]
    incoming = take_slots(group[..., :1], neighbours[:, :, 1])
    moved = moved.at[:, :, EAST_POPS].set(jnp.concatenate([group[..., 1:], incoming], axis=-1))
    group = moved[:, :, WEST_POPS]
    incoming = take_slots(group[..., -1:], neighbours[:, :, 0])
    moved = moved.at[:, :, WEST_POPS].set(jnp.concatenate([incoming, group[..., :-1]], axis=-1))
    group = moved[:, :, NORTH_POPS]
    incoming = take_slots(group[..., :1, :], neighbours[:, :, 3])
    moved = moved.at[:, :, NORTH_POPS].set(jnp.concatenate([group[..., 1:, :], incoming], axis=-2))
    group = moved[:, :, SOUTH_POPS]
    incoming = take_slots(group[..., -1:, :], neighbours[:, :, 2])
    moved = moved.at[:, :, SOUTH_POPS].set(jnp.concatenate([incoming, group[..., :-1, :]], axis=-2))
    group = moved[:, :, UPPER_POPS]
    face = group[..., :1, :, :]
    source = jnp.concatenate([face[1:], jnp.zeros_like(face[:1])], axis=0)
    incoming = take_slots(source, neighbours[:, :, 5])
    moved = moved.at[:, :, UPPER_POPS].set(jnp.concatenate([group[..., 1:, :, :], incoming], axis=-3))
    group = moved[:, :, LOWER_POPS]
    face = group[..., -1:, :, :]
    source = jnp.concatenate([jnp.zeros_like(face[:1]), face[:-1]], axis=0)
    incoming = take_slots(source, neighbours[:, :, 4])
    moved = moved.at[:, :, LOWER_POPS].set(jnp.concatenate([incoming, group[..., :-1, :, :]], axis=-3))
    return moved


def reference(adjoint, velocity, porosity, block_x, neighbours, owner_map):
    state = adjoint.reshape(LAYERS, SLOTS, 19, B, B, B)
    flow = velocity.reshape(LAYERS, SLOTS, 3, B, B, B)
    design = porosity.reshape(LAYERS, SLOTS, 1, B, B, B)
    sens_total = jnp.zeros((LAYERS, SLOTS, B, B, B), jnp.float32)
    for iteration in range(STEPS):
        collided, sens_step = collide(state, flow, design, 2)
        sens_total = sens_total + sens_step[:, :, 0]
        state = stream(collided, neighbours)
    columns = block_x.reshape(LAYERS, COLS, K)
    hits = columns[..., None] == jnp.arange(COLS, dtype=jnp.int32)
    holder = jnp.sum(jnp.where(hits, jnp.arange(COLS, dtype=jnp.int32)[None, :, None, None], 0), axis=1).astype(jnp.int32)
    per_device = sens_total.reshape(LAYERS, COLS, K, B, B, B)
    row_ids = jnp.arange(K, dtype=jnp.int32)[:, None]
    placed = jax.vmap(lambda source, picks: source[picks, row_ids])(per_device, holder)
    field = placed.transpose(0, 3, 1, 4, 2, 5).reshape(LAYERS * B, K * B, COLS * B)
    filtered = smooth_axis(smooth_axis(smooth_axis(field, 1), 2), 0)
    band_rows = 2 * owner_map
    band_start = jnp.cumsum(band_rows) - band_rows
    offsets = jnp.arange(ROWS, dtype=jnp.int32)
    wanted = band_start[:, None] + offsets[None, :]
    present = offsets[None, :] < band_rows[:, None]
    picked = jnp.take(filtered, jnp.clip(wanted, 0, K * B - 1).reshape(-1), axis=1)
    picked = picked.reshape(LAYERS * B, COLS, ROWS, COLS * B)
    picked = jnp.where(present[None, :, :, None], picked, jnp.zeros_like(picked))
    smoothed = picked.reshape(LAYERS, B, COLS, ROWS, COLS * B).transpose(0, 2, 3, 1, 4)
    return state.reshape(adjoint.shape), smoothed
```

```python
import functools

import jax
import jax.numpy as jnp
import numpy as np
from jax import lax
from jax.experimental import pallas as pl
from jax.experimental.pallas import tpu as pltpu
from jax.sharding import PartitionSpec as P

STEPS = 2
VELOCITIES = [
    (0, 0, 0),
    (1, 0, 0),
    (-1, 0, 0),
    (0, 1, 0),
    (0, -1, 0),
    (0, 0, 1),
    (0, 0, -1),
    (1, 1, 0),
    (-1, -1, 0),
    (1, -1, 0),
    (-1, 1, 0),
    (1, 0, 1),
    (-1, 0, -1),
    (1, 0, -1),
    (-1, 0, 1),
    (0, 1, 1),
    (0, -1, -1),
    (0, 1, -1),
    (0, -1, 1),
]
POPS = 19
EAST_POPS = [1, 7, 9, 11, 13]
WEST_POPS = [2, 8, 10, 12, 14]
NORTH_POPS = [3, 7, 10, 15, 17]
SOUTH_POPS = [4, 8, 9, 16, 18]
UPPER_POPS = [5, 11, 14, 15, 18]
LOWER_POPS = [6, 12, 13, 16, 17]
RELAX_RATE = 1.25
DRAG_RATE = 0.3
TAP_EDGE, TAP_NEAR = 1.0 / 3.0, 2.0 / 3.0

FACE_ROWS = 48


def dev_of(slot, blocks):
    return lax.div(jnp.maximum(slot, 0), jnp.int32(blocks))


def shift(value, amount, axis=1):
    amount = amount % value.shape[axis]
    return value if amount == 0 else pltpu.roll(value, amount, axis)


def lanes(shape):
    return lax.broadcasted_iota(jnp.int32, shape, len(shape) - 1)


def collide_cells(f, u, porosity):
    total, gap = {}, {}
    for i in range(1, POPS, 2):
        total[i], gap[i] = f[i] + f[i + 1], f[i] - f[i + 1]
    ux, uy, uz = u
    mx = gap[1] + gap[7] + gap[9] + gap[11] + gap[13]
    my = gap[3] + gap[7] - gap[9] + gap[15] + gap[17]
    mz = gap[5] + gap[11] - gap[13] + gap[15] - gap[17]
    xy_sum, xz_sum, yz_sum = total[7] + total[9], total[11] + total[13], total[15] + total[17]
    xx = 2.0 * total[1] + xy_sum + xz_sum
    yy = 2.0 * total[3] + xy_sum + yz_sum
    zz = 2.0 * total[5] + xz_sum + yz_sum
    xy, xz, yz = total[7] - total[9], total[11] - total[13], total[15] - total[17]
    mass = 12.0 * f[0] + 2.0 * (total[1] + total[3] + total[5]) + (xy_sum + xz_sum + yz_sum)
    speed_sq = ux * ux + uy * uy + uz * uz
    qx = xx * ux + xy * uy + xz * uz
    qy = xy * ux + yy * uy + yz * uz
    qz = xz * ux + yz * uy + zz * uz
    sens = ux * mx + uy * my + uz * mz
    drag = DRAG_RATE * porosity
    scale = RELAX_RATE / 36.0
    quad = ux * qx + uy * qy + uz * qz
    base = scale * (mass + 1.5 * (speed_sq * mass) - 4.5 * quad) + drag * sens
    gx = (3.0 * scale) * (mx + gap[1] + 3.0 * qx - ux * mass) - drag * mx
    gy = (3.0 * scale) * (my + gap[3] + 3.0 * qy - uy * mass) - drag * my
    gz = (3.0 * scale) * (mz + gap[5] + 3.0 * qz - uz * mass) - drag * mz
    along = {1: gx, 3: gy, 5: gz, 7: gx + gy, 9: gx - gy, 11: gx + gz, 13: gx - gz, 15: gy + gz, 17: gy - gz}
    keep = 1.0 - RELAX_RATE
    post = [base + keep * f[0]]
    for i in range(1, POPS, 2):
        post.append(base + along[i] + keep * f[i])
        post.append(base - along[i] + keep * f[i + 1])
    return post, sens


def collide_block(read, velocity_ref, porosity_ref, post_ref, edge, plane):
    parts = {}
    for low in range(0, edge, 8):
        for left in range(0, plane, 128):
            zs, cells = pl.ds(low, 8), pl.ds(left, 128)
            post, sens = collide_cells(
                [read(p, zs, cells) for p in range(POPS)],
                [velocity_ref[c, zs, cells] for c in range(3)],
                porosity_ref[zs, cells],
            )
            for p in range(POPS):
                post_ref[p, zs, cells] = post[p]
            parts[low, left] = sens
    return parts


def pack_faces(block, blocks, post_ref, faces_ref, edge, plane):
    slot = lanes((edge, plane)) % edge
    x_tile = jnp.zeros((edge, plane), jnp.float32)
    for s, p in enumerate(EAST_POPS):
        x_tile = jnp.where(slot == s, shift(post_ref[p], s), x_tile)
    for s, p in enumerate(WEST_POPS):
        x_tile = jnp.where(slot == 5 + s, shift(post_ref[p], 5 + s - (edge - 1)), x_tile)
    faces_ref[block, 0:16, :] = x_tile
    for i in range(5):
        faces_ref[block, 32 + i : 33 + i, :] = post_ref[UPPER_POPS[i], 0:1, :]
        faces_ref[block, 40 + i : 41 + i, :] = post_ref[LOWER_POPS[i], edge - 1 : edge, :]
    faces_ref[block, 37:38, :] = x_tile[0:1]
    faces_ref[block, 45:46, :] = x_tile[edge - 1 : edge]
    group = lanes((edge, 128)) // edge
    north = jnp.zeros((edge, 128), jnp.float32)
    south = jnp.zeros((edge, 128), jnp.float32)
    for q in range(5):
        north = jnp.where(group == q, shift(post_ref[NORTH_POPS[q], :, 0:128], q * edge), north)
        south = jnp.where(
            group == q, shift(post_ref[SOUTH_POPS[q], :, plane - 128 : plane], (q + 1) * edge - 128), south
        )

    @pl.when(block > 0)
    def _():
        faces_ref[block - 1, 16:32, 0:128] = north
        faces_ref[block - 1, 38:39, 0:128] = north[0:1]
        faces_ref[block - 1, 46:47, 0:128] = north[edge - 1 : edge]

    @pl.when(block < blocks - 1)
    def _():
        faces_ref[block + 1, 16:32, 128:256] = south
        faces_ref[block + 1, 38:39, 128:256] = south[0:1]
        faces_ref[block + 1, 46:47, 128:256] = south[edge - 1 : edge]


def stream_pop(p, source, halo_ref, edge, plane):
    cx, cy, cz = VELOCITIES[p]
    lane = lanes((edge, plane))
    value = shift(source, -(cx + edge * cy))
    if cx != 0:
        face = edge - 1 if cx > 0 else 0
        s = EAST_POPS.index(p) if cx > 0 else 5 + WEST_POPS.index(p)
        arrived = shift(halo_ref[0, 0:16, :], face - s - edge * cy)
        value = jnp.where(lane % edge == face, arrived, value)
    if cy != 0:
        face = edge - 1 if cy > 0 else 0
        start = NORTH_POPS.index(p) * edge if cy > 0 else 128 + SOUTH_POPS.index(p) * edge
        arrived = shift(halo_ref[0, 16:32, :], face * edge - start)
        value = jnp.where(lane // edge == face, arrived, value)
    if cz != 0:
        face = edge - 1 if cz > 0 else 0
        row = 32 + UPPER_POPS.index(p) if cz > 0 else 40 + LOWER_POPS.index(p)
        arrived = halo_ref[0, row : row + 1, :]
        depth = lax.broadcasted_iota(jnp.int32, (edge, plane), 0)
        value = jnp.where(depth == face, arrived, shift(value, -cz, 0))
    return value


def first_kernel(blocks, state_ref, velocity_ref, porosity_ref, post_ref, sens_ref, faces_ref):
    block = pl.program_id(0)
    edge, plane = porosity_ref.shape[1:]
    parts = collide_block(
        lambda p, zs, cells: state_ref[0, p, zs, cells],
        velocity_ref.at[0],
        porosity_ref.at[0],
        post_ref.at[0],
        edge,
        plane,
    )
    for (low, left), sens in parts.items():
        sens_ref[0, pl.ds(low, 8), pl.ds(left, 128)] = sens
    pack_faces(block, blocks, post_ref.at[0], faces_ref, edge, plane)


def slab_start(owner_ref, slab, devices):
    start = jnp.int32(0)
    for j in range(devices):
        start = start + jnp.where(j < slab, 2 * owner_ref[j], 0)
    return start


def second_kernel(
    blocks,
    devices,
    chunks,
    owner_ref,
    before_ref,
    halo_ref,
    velocity_ref,
    porosity_ref,
    sens_ref,
    post_ref,
    faces_ref,
    rows_ref,
    state_ref,
    field_ref,
):
    block = pl.program_id(0)
    edge, plane = porosity_ref.shape[1:]
    for p in range(POPS):
        state_ref[p] = stream_pop(p, before_ref[0, p], halo_ref, edge, plane)
    parts = collide_block(
        lambda p, zs, cells: state_ref[p, zs, cells],
        velocity_ref.at[0],
        porosity_ref.at[0],
        post_ref.at[0],
        edge,
        plane,
    )
    for (low, left), sens in parts.items():
        field_ref[block * (plane // 128) + left // 128, pl.ds(low, 8), :] = (
            sens_ref[0, pl.ds(low, 8), pl.ds(left, 128)] + sens
        )
    pack_faces(block, blocks, post_ref.at[0], faces_ref, edge, plane)

    @pl.when(block == blocks - 1)
    def _():
        held = blocks * (plane // 128)
        start = jnp.int32(0)
        for j in range(devices):
            first = lax.div(start + 6, jnp.int32(8)) - 1
            for i in range(chunks):
                rows_ref[j, i] = field_ref[jnp.clip(first + i, 0, held - 1)]
            start = start + 2 * owner_ref[j]


def last_kernel(before_ref, halo_ref, out_ref):
    edge, plane = out_ref.shape[2:]
    for p in range(POPS):
        out_ref[0, p] = stream_pop(p, before_ref[0, p], halo_ref, edge, plane)


def route_kernel(blocks, devices, table_ref, row_ref, faces_ref, above_ref, below_ref, halo_ref):
    row = row_ref[0]
    edge, plane = 16, faces_ref.shape[2]
    slot = lanes((edge, plane)) % edge
    lane = lanes((edge, 128))
    line = lanes((1, plane))
    dev = functools.partial(dev_of, blocks=blocks)

    def beside(slot_id, face):
        return jnp.where(slot_id < 0, -1, table_ref[jnp.maximum(slot_id, 0), face])

    def one(d, carry):
        here = d * blocks + row
        west, east, south, north, below, above = [table_ref[here, face] for face in range(6)]
        zero = jnp.float32(0.0)
        halo_ref[d, 0:16, :] = jnp.where(
            slot < 5,
            jnp.where(east >= 0, faces_ref[dev(east), 0:16, :], zero),
            jnp.where(west >= 0, faces_ref[dev(west), 0:16, :], zero),
        )

        def y_face(where_from, left, east_q, west_q):
            far_east, far_west = beside(where_from, 1), beside(where_from, 0)

            def tile(slot_id):
                return jnp.where(slot_id >= 0, faces_ref[dev(slot_id), 16:32, left : left + 128], zero)

            own = tile(where_from)
            e, w = east_q * edge, west_q * edge
            moved = jnp.where((lane >= e) & (lane < e + edge), shift(own, -1), own)
            moved = jnp.where(lane == e + edge - 1, shift(tile(far_east), edge - 1), moved)
            moved = jnp.where((lane >= w) & (lane < w + edge), shift(own, 1), moved)
            return jnp.where(lane == w, shift(tile(far_west), 1 - edge), moved)

        halo_ref[d, 16:32, 0:128] = y_face(north, 0, 1, 2)
        halo_ref[d, 16:32, 128:256] = y_face(south, 128, 2, 1)

        def z_face(ref, where_from, face, pops, row0):
            def rows(slot_id, r):
                return jnp.where(slot_id >= 0, ref[dev(slot_id), r : r + 1, :], zero)

            from_x = {1: rows(beside(east, face), 5), -1: rows(beside(west, face), 5)}
            from_y = {1: rows(beside(north, face), 6), -1: rows(beside(south, face), 6)}
            for i, p in enumerate(pops):
                cx, cy, _ = VELOCITIES[p]
                value = shift(rows(where_from, i), -(cx + edge * cy))
                if cx != 0:
                    at = edge - 1 if cx > 0 else 0
                    s = EAST_POPS.index(p) if cx > 0 else 5 + WEST_POPS.index(p)
                    value = jnp.where(line % edge == at, shift(from_x[cx], at - s), value)
                if cy != 0:
                    at = edge - 1 if cy > 0 else 0
                    start = NORTH_POPS.index(p) * edge if cy > 0 else 128 + SOUTH_POPS.index(p) * edge
                    value = jnp.where(line // edge == at, shift(from_y[cy], at * edge - start), value)
                halo_ref[d, row0 + i : row0 + i + 1, :] = value

        z_face(above_ref, above, 5, UPPER_POPS, 32)
        z_face(below_ref, below, 4, LOWER_POPS, 40)
        return carry

    lax.fori_loop(0, devices, one, 0)


def slab_kernel(
    blocks, devices, chunks, owner_ref, column_ref, slab_ref, rows_ref, out_ref, low_ref, high_ref, field_ref
):
    slab = slab_ref[0]
    count, edge, width = out_ref.shape
    start = slab_start(owner_ref, slab, devices)
    first = lax.div(start + 6, jnp.int32(8)) - 1
    lane = lanes((edge, width))
    group = lane // edge
    per_block = 256 // 128
    held = blocks * per_block

    def chunk(i, carry):
        at = first + i
        inside = (at >= 0) & (at < held)
        block_row = lax.div(jnp.clip(at, 0, held - 1), jnp.int32(per_block))
        tiles = [jnp.zeros((edge, width), jnp.float32) for _ in range(8)]
        for e in range(devices):
            column = column_ref[0, e * blocks + block_row]
            value = rows_ref[e, i]
            turned = pltpu.roll(value, lax.rem(column, jnp.int32(8)) * edge, 1)
            hit = (group == column) & inside
            for r in range(8):
                part = shift(turned, -r * edge)
                if width > 128:
                    part = jnp.concatenate([part] * (width // 128), axis=1)
                tiles[r] = jnp.where(hit, part, tiles[r])
        for r in range(8):
            field_ref[i * 8 + r] = tiles[r]
        return carry

    lax.fori_loop(0, chunks, chunk, 0)
    offset = start - 2 - 8 * first

    def row(r, carry):
        at = offset + r
        mixed = TAP_EDGE * (field_ref[at] + field_ref[at + 4]) + (
            TAP_NEAR * (field_ref[at + 1] + field_ref[at + 3]) + field_ref[at + 2]
        )
        value = mixed
        for step, tap in ((1, TAP_NEAR), (2, TAP_EDGE)):
            left = jnp.where(lane >= step, shift(mixed, step), 0.0)
            right = jnp.where(lane < width - step, shift(mixed, -step), 0.0)
            value = value + tap * (left + right)
        out_ref[r] = value
        for z in range(2):
            low_ref[z, pl.ds(r, 1), :] = value[z : z + 1]
            high_ref[z, pl.ds(r, 1), :] = value[edge - 2 + z : edge - 1 + z]
        return carry

    lax.fori_loop(0, count, row, 0)


def depth_kernel(owner_ref, slab_ref, rows_ref, below_ref, above_ref, out_ref):
    count, edge, width = out_ref.shape
    own_rows = 2 * owner_ref[slab_ref[0]]
    depth = lax.broadcasted_iota(jnp.int32, (edge, width), 0)

    def row(r, carry):
        value = rows_ref[r]
        b0, b1 = [below_ref[z, pl.ds(r, 1), :] for z in range(2)]
        a0, a1 = [above_ref[z, pl.ds(r, 1), :] for z in range(2)]
        down = jnp.where(depth == 0, b1, shift(value, 1, 0))
        up = jnp.where(depth == edge - 1, a0, shift(value, -1, 0))
        down_2 = jnp.where(depth == 0, b0, jnp.where(depth == 1, b1, shift(value, 2, 0)))
        up_2 = jnp.where(depth == edge - 1, a1, jnp.where(depth == edge - 2, a0, shift(value, -2, 0)))
        total = value + TAP_NEAR * (down + up) + TAP_EDGE * (down_2 + up_2)
        out_ref[r] = jnp.where(r < own_rows, total, 0.0)
        return carry

    lax.fori_loop(0, count, row, 0)


SMEM = pl.BlockSpec(memory_space=pltpu.SMEM)
VMEM = pl.BlockSpec(memory_space=pltpu.VMEM)


def by_block(shape):
    rest = len(shape) - 1
    return pl.BlockSpec((1,) + tuple(shape[1:]), lambda b: (b,) + (0,) * rest)


def whole(shape):
    return pl.BlockSpec(tuple(shape), lambda b: (0,) * len(shape))


def f32(*shape):
    return jax.ShapeDtypeStruct(shape, jnp.float32)


def local(adjoint, velocity, porosity, block_x, neighbours, owner_map):
    blocks, _, edge, plane = adjoint.shape[1:]
    devices, layers = lax.axis_size("blk"), lax.axis_size("gz")
    my_index = lax.axis_index("blk").astype(jnp.int32)
    row_id = jnp.minimum(my_index, blocks - 1).reshape(1)
    slab_id = my_index.reshape(1)
    state, flow, design, table = adjoint[0], velocity[0], porosity[0], neighbours[0]
    rows_cap = 2 * (3 * (blocks * edge // 2) // devices)
    chunks = -(-(rows_cap + 10) // 8)
    width = devices * edge
    upward = [(g, g + 1) for g in range(layers - 1)]
    downward = [(g + 1, g) for g in range(layers - 1)]
    faces_shape = (devices, FACE_ROWS, plane)
    params = pltpu.CompilerParams(vmem_limit_bytes=32 * 1024 * 1024)

    def to_halo(faces):
        gathered = lax.all_to_all(faces, "blk", 0, 0, tiled=True)
        above = lax.ppermute(gathered[:, 32:40], "gz", downward)
        below = lax.ppermute(gathered[:, 40:48], "gz", upward)
        halo = pl.pallas_call(
            functools.partial(route_kernel, blocks, devices),
            out_shape=f32(*faces_shape),
            in_specs=[SMEM, SMEM, VMEM, VMEM, VMEM],
            out_specs=VMEM,
            compiler_params=params,
            name="route",
        )(table, row_id, gathered, above, below)
        return lax.all_to_all(halo, "blk", 0, 0, tiled=True)

    post, sens, faces = pl.pallas_call(
        functools.partial(first_kernel, blocks),
        grid=(blocks,),
        out_shape=(f32(*state.shape), f32(*design.shape), f32(*faces_shape)),
        in_specs=[by_block(state.shape), by_block(flow.shape), by_block(design.shape)],
        out_specs=(by_block(state.shape), by_block(design.shape), whole(faces_shape)),
        compiler_params=params,
        name="collide_first",
    )(state, flow, design)
    halo = to_halo(faces)
    rows_shape = (devices, chunks, edge, 128)
    post, faces, rows = pl.pallas_call(
        functools.partial(second_kernel, blocks, devices, chunks),
        grid=(blocks,),
        out_shape=(f32(*state.shape), f32(*faces_shape), f32(*rows_shape)),
        in_specs=[
            SMEM,
            by_block(state.shape),
            by_block(faces_shape),
            by_block(flow.shape),
            by_block(design.shape),
            by_block(design.shape),
        ],
        out_specs=(by_block(state.shape), whole(faces_shape), whole(rows_shape)),
        scratch_shapes=[
            pltpu.VMEM((POPS, edge, plane), jnp.float32),
            pltpu.VMEM((blocks * plane // 128, edge, 128), jnp.float32),
        ],
        compiler_params=params,
        name="stream_collide",
    )(owner_map, post, halo, flow, design, sens)
    halo = to_halo(faces)
    rows = lax.all_to_all(rows, "blk", 0, 0, tiled=True)
    ends = (2, rows_cap, width)
    slab, low, high = pl.pallas_call(
        functools.partial(slab_kernel, blocks, devices, chunks),
        out_shape=(f32(rows_cap, edge, width), f32(*ends), f32(*ends)),
        in_specs=[SMEM, SMEM, SMEM, VMEM],
        out_specs=(VMEM, VMEM, VMEM),
        scratch_shapes=[pltpu.VMEM((chunks * 8, edge, width), jnp.float32)],
        compiler_params=params,
        name="slab_rows",
    )(owner_map, block_x, slab_id, rows)
    below = lax.ppermute(high, "gz", upward)
    above = lax.ppermute(low, "gz", downward)
    smoothed = pl.pallas_call(
        depth_kernel,
        out_shape=f32(rows_cap, edge, width),
        in_specs=[SMEM, SMEM, VMEM, VMEM, VMEM],
        out_specs=VMEM,
        compiler_params=params,
        name="slab_depth",
    )(owner_map, slab_id, slab, below, above)
    moved = pl.pallas_call(
        last_kernel,
        grid=(blocks,),
        out_shape=f32(*state.shape),
        in_specs=[by_block(state.shape), by_block(faces_shape)],
        out_specs=by_block(state.shape),
        compiler_params=params,
        name="stream_last",
    )(post, halo)
    return (moved[None], smoothed[None, None])


def solution(mesh):
    placed = (
        P("gz", "blk", None, None, None),
        P("gz", "blk", None, None, None),
        P("gz", "blk", None, None),
        P("gz", None),
        P("gz", None, None),
        P(),
    )
    return jax.shard_map(
        local,
        mesh=mesh,
        in_specs=placed,
        out_specs=(P("gz", "blk", None, None, None), P("gz", "blk", None, None, None)),
        check_vma=False,
    )
```

```python
import functools

import jax
import jax.numpy as jnp
import numpy as np
from jax import lax
from jax.experimental import pallas as pl
from jax.experimental.pallas import tpu as pltpu
from jax.sharding import PartitionSpec as P

STEPS = 2
VELOCITIES = [
    (0, 0, 0),
    (1, 0, 0),
    (-1, 0, 0),
    (0, 1, 0),
    (0, -1, 0),
    (0, 0, 1),
    (0, 0, -1),
    (1, 1, 0),
    (-1, -1, 0),
    (1, -1, 0),
    (-1, 1, 0),
    (1, 0, 1),
    (-1, 0, -1),
    (1, 0, -1),
    (-1, 0, 1),
    (0, 1, 1),
    (0, -1, -1),
    (0, 1, -1),
    (0, -1, 1),
]
POPS = 19
EAST_POPS = [1, 7, 9, 11, 13]
WEST_POPS = [2, 8, 10, 12, 14]
NORTH_POPS = [7, 10, 15, 17]
SOUTH_POPS = [8, 9, 16, 18]
UPPER_POPS = [5, 11, 14, 15, 18]
LOWER_POPS = [6, 12, 13, 16, 17]
RELAX_RATE = 1.25
DRAG_RATE = 0.3
TAP_EDGE, TAP_NEAR = 1.0 / 3.0, 2.0 / 3.0

FACE_ROWS = 40
FIRST, SECOND = 24, 32
SOUTH = 64


def dev_of(slot, blocks):
    return lax.div(jnp.maximum(slot, 0), jnp.int32(blocks))


def shift(value, amount, axis=1):
    amount = amount % value.shape[axis]
    return value if amount == 0 else pltpu.roll(value, amount, axis)


def lanes(shape):
    return lax.broadcasted_iota(jnp.int32, shape, len(shape) - 1)


def collide_cells(f, u, porosity):
    total, gap = {}, {}
    for i in range(1, POPS, 2):
        total[i], gap[i] = f[i] + f[i + 1], f[i] - f[i + 1]
    ux, uy, uz = u
    mx = gap[1] + gap[7] + gap[9] + gap[11] + gap[13]
    my = gap[3] + gap[7] - gap[9] + gap[15] + gap[17]
    mz = gap[5] + gap[11] - gap[13] + gap[15] - gap[17]
    xy_sum, xz_sum, yz_sum = total[7] + total[9], total[11] + total[13], total[15] + total[17]
    xx = 2.0 * total[1] + xy_sum + xz_sum
    yy = 2.0 * total[3] + xy_sum + yz_sum
    zz = 2.0 * total[5] + xz_sum + yz_sum
    xy, xz, yz = total[7] - total[9], total[11] - total[13], total[15] - total[17]
    mass = 12.0 * f[0] + 2.0 * (total[1] + total[3] + total[5]) + (xy_sum + xz_sum + yz_sum)
    speed_sq = ux * ux + uy * uy + uz * uz
    qx = xx * ux + xy * uy + xz * uz
    qy = xy * ux + yy * uy + yz * uz
    qz = xz * ux + yz * uy + zz * uz
    sens = ux * mx + uy * my + uz * mz
    drag = DRAG_RATE * porosity
    scale = RELAX_RATE / 36.0
    quad = ux * qx + uy * qy + uz * qz
    base = scale * (mass + 1.5 * (speed_sq * mass) - 4.5 * quad) + drag * sens
    gx = (3.0 * scale) * (mx + gap[1] + 3.0 * qx - ux * mass) - drag * mx
    gy = (3.0 * scale) * (my + gap[3] + 3.0 * qy - uy * mass) - drag * my
    gz = (3.0 * scale) * (mz + gap[5] + 3.0 * qz - uz * mass) - drag * mz
    along = {1: gx, 3: gy, 5: gz, 7: gx + gy, 9: gx - gy, 11: gx + gz, 13: gx - gz, 15: gy + gz, 17: gy - gz}
    keep = 1.0 - RELAX_RATE
    post = [base + keep * f[0]]
    for i in range(1, POPS, 2):
        post.append(base + along[i] + keep * f[i])
        post.append(base - along[i] + keep * f[i + 1])
    return post, sens


def collide_block(read, velocity_ref, porosity_ref, post_ref, edge, plane):
    parts = {}
    for low in range(0, edge, 8):
        for left in range(0, plane, 128):
            zs, cells = pl.ds(low, 8), pl.ds(left, 128)
            post, sens = collide_cells(
                [read(p, zs, cells) for p in range(POPS)],
                [velocity_ref[c, zs, cells] for c in range(3)],
                porosity_ref[zs, cells],
            )
            for p in range(POPS):
                post_ref[p, zs, cells] = post[p]
            parts[low, left] = sens
    return parts


def pack_faces(block, blocks, swapped, post_ref, faces_ref, edge, plane):
    def put_ends(target, row, cells, low, high):
        faces_ref[target, FIRST + row : FIRST + row + 1, cells] = jnp.where(swapped, high, low)
        faces_ref[target, SECOND + row : SECOND + row + 1, cells] = jnp.where(swapped, low, high)

    every = slice(0, plane)
    slot = lanes((edge, plane)) % edge
    x_tile = jnp.zeros((edge, plane), jnp.float32)
    for s, p in enumerate(EAST_POPS):
        x_tile = jnp.where(slot == s, shift(post_ref[p], s), x_tile)
    for s, p in enumerate(WEST_POPS):
        x_tile = jnp.where(slot == 5 + s, shift(post_ref[p], 5 + s - (edge - 1)), x_tile)
    faces_ref[block, 0:16, :] = x_tile
    for i in range(5):
        put_ends(block, i, every, post_ref[UPPER_POPS[i], 0:1, :], post_ref[LOWER_POPS[i], edge - 1 : edge, :])
    put_ends(block, 5, every, x_tile[0:1], x_tile[edge - 1 : edge])
    group = lanes((edge, 128)) // edge
    north = jnp.zeros((edge, 128), jnp.float32)
    south = jnp.zeros((edge, 128), jnp.float32)
    for q in range(4):
        north = jnp.where(group == q, shift(post_ref[NORTH_POPS[q], :, 0:128], q * edge), north)
        south = jnp.where(
            group == 4 + q, shift(post_ref[SOUTH_POPS[q], :, plane - 128 : plane], (q + 5) * edge), south
        )

    def put_y(target, tile, start, pop, left, first, row):
        for half in range(2):
            rows = tile[half * 8 : half * 8 + 8]
            at = half * 128
            faces_ref[target, 16:24, at + start : at + start + 64] = rows[:, start : start + 64]
            line = post_ref[pop, half * 8 : half * 8 + 8, left : left + 128]
            line = jnp.where(group[0:8] == first, line, 0.0)
            line = pltpu.roll(line, (128 - first * edge) % 128, 1, stride=edge, stride_axis=0)
            faces_ref[target, row + 7 : row + 8, at : at + 128] = jnp.sum(line, axis=0, keepdims=True)
        put_ends(target, 6, slice(start, start + 64), tile[0:1, start : start + 64], tile[edge - 1 : edge, start : start + 64])

    @pl.when(block > 0)
    def _():
        put_y(block - 1, north, 0, 3, 0, 0, FIRST)

    @pl.when(block < blocks - 1)
    def _():
        put_y(block + 1, south, SOUTH, 4, plane - 128, 7, SECOND)


def first_partner_above():
    return lax.rem(lax.axis_index("gz").astype(jnp.int32), jnp.int32(2)) == 0


def stream_pop(p, source, halo_ref, edge, plane):
    cx, cy, cz = VELOCITIES[p]
    lane = lanes((edge, plane))
    value = shift(source, -(cx + edge * cy))
    if cx != 0:
        face = edge - 1 if cx > 0 else 0
        s = EAST_POPS.index(p) if cx > 0 else 5 + WEST_POPS.index(p)
        arrived = shift(halo_ref[0:16, :], face - s - edge * cy)
        value = jnp.where(lane % edge == face, arrived, value)
    if cy != 0:
        face = 7 if cy > 0 else 0
        if p in (3, 4):
            row = (FIRST if cy > 0 else SECOND) + 7
            lined = lax.broadcasted_iota(jnp.int32, (8, 128), 0) == lane[0:8, 0:128] // edge
            arrived = [jnp.where(lined, halo_ref[row : row + 1, at : at + 128], 0.0) for at in (0, 128)]
            for step in (4, 2, 1):
                arrived = [part + shift(part, step * edge) for part in arrived]
        else:
            start = NORTH_POPS.index(p) * edge if cy > 0 else SOUTH + SOUTH_POPS.index(p) * edge
            arrived = [shift(halo_ref[16:24, at : at + 128], face * edge - start) for at in (0, 128)]
        arrived = jnp.concatenate(arrived, axis=0)
        halves = [value[:, side : side + 128] for side in range(0, plane, 128)]
        at = -1 if cy > 0 else 0
        halves[at] = jnp.where(lane[:, 0:128] // edge == face, arrived, halves[at])
        value = jnp.concatenate(halves, axis=1)
    if cz != 0:
        face = edge - 1 if cz > 0 else 0
        row = FIRST + UPPER_POPS.index(p) if cz > 0 else SECOND + LOWER_POPS.index(p)
        arrived = halo_ref[row : row + 1, :]
        depth = lax.broadcasted_iota(jnp.int32, (edge, plane), 0)
        value = jnp.where(depth == face, arrived, shift(value, -cz, 0))
    return value


def first_kernel(
    blocks,
    state_hbm,
    velocity_hbm,
    porosity_hbm,
    post_hbm,
    faces_ref,
    state_ref,
    velocity_ref,
    porosity_ref,
    post_ref,
    sems,
):
    edge, plane = porosity_ref.shape[1:]
    swapped = first_partner_above()

    def copies(b):
        return (
            pltpu.make_async_copy(state_hbm.at[b], state_ref.at[b], sems.at[0, b]),
            pltpu.make_async_copy(velocity_hbm.at[b], velocity_ref.at[b], sems.at[1, b]),
            pltpu.make_async_copy(porosity_hbm.at[b], porosity_ref.at[b], sems.at[2, b]),
        )

    def result(b):
        return pltpu.make_async_copy(post_ref.at[b], post_hbm.at[b], sems.at[3, b])

    for b in range(blocks):
        for copy in copies(b):
            copy.start()

    def one(b, carry):
        for copy in copies(b):
            copy.wait()
        parts = collide_block(
            lambda p, zs, cells: state_ref[b, p, zs, cells],
            velocity_ref.at[b],
            porosity_ref.at[b],
            post_ref.at[b],
            edge,
            plane,
        )
        for (low, left), sens in parts.items():
            post_ref[b, POPS, pl.ds(low, 8), pl.ds(left, 128)] = sens
        result(b).start()
        pack_faces(b, blocks, swapped, post_ref.at[b], faces_ref, edge, plane)
        return carry

    lax.fori_loop(0, blocks, one, 0)
    for b in range(blocks):
        result(b).wait()


def slab_start(owner_ref, slab, devices):
    start = jnp.int32(0)
    for j in range(devices):
        start = start + jnp.where(j < slab, 2 * owner_ref[j], 0)
    return start


def second_kernel(
    blocks,
    devices,
    chunks,
    owner_ref,
    before_hbm,
    velocity_hbm,
    porosity_hbm,
    halo_ref,
    post_hbm,
    faces_ref,
    before_ref,
    velocity_ref,
    porosity_ref,
    post_ref,
    state_ref,
    field_ref,
    sems,
):
    edge, plane = porosity_ref.shape[1:]
    swapped = first_partner_above()

    def copies(b):
        return (
            pltpu.make_async_copy(before_hbm.at[b], before_ref.at[b], sems.at[0, b]),
            pltpu.make_async_copy(velocity_hbm.at[b], velocity_ref.at[b], sems.at[1, b]),
            pltpu.make_async_copy(porosity_hbm.at[b], porosity_ref.at[b], sems.at[2, b]),
        )

    def result(b):
        return pltpu.make_async_copy(post_ref.at[b], post_hbm.at[b], sems.at[3, b])

    for b in range(blocks):
        for copy in copies(b):
            copy.start()

    def one(b, carry):
        for copy in copies(b):
            copy.wait()
        for p in range(POPS):
            state_ref[p] = stream_pop(p, before_ref[b, p], halo_ref.at[b], edge, plane)
        parts = collide_block(
            lambda p, zs, cells: state_ref[p, zs, cells],
            velocity_ref.at[b],
            porosity_ref.at[b],
            post_ref.at[b],
            edge,
            plane,
        )
        result(b).start()
        for (low, left), sens in parts.items():
            field_ref[b * (plane // 128) + left // 128, pl.ds(low, 8), :] = (
                before_ref[b, POPS, pl.ds(low, 8), pl.ds(left, 128)] + sens
            )
        pack_faces(b, blocks, swapped, post_ref.at[b], faces_ref, edge, plane)
        return carry

    lax.fori_loop(0, blocks, one, 0)
    held = blocks * (plane // 128)
    start = jnp.int32(0)
    lane = lanes((edge, 128))
    for j in range(devices):
        first = lax.div(start + 6, jnp.int32(8)) - 1
        behind = (start - 2 - 8 * first) * edge
        turned = [
            pltpu.roll(field_ref[jnp.clip(first + i, 0, held - 1)], lax.rem(128 - behind, jnp.int32(128)), 1)
            for i in range(chunks + 1)
        ]
        for i in range(chunks):
            value = jnp.where(lane < 128 - behind, turned[i], turned[i + 1])
            at = FACE_ROWS + 8 * i
            faces_ref[j, at : at + 8, 0:128] = value[0:8]
            faces_ref[j, at : at + 8, 128:256] = value[8:16]
        start = start + 2 * owner_ref[j]
    for b in range(blocks):
        result(b).wait()


def last_kernel(blocks, before_hbm, halo_ref, out_hbm, before_ref, out_ref, sems):
    edge, plane = before_ref.shape[2:]

    def copy(b):
        return pltpu.make_async_copy(before_hbm.at[b], before_ref.at[b], sems.at[0, b])

    def result(b):
        return pltpu.make_async_copy(out_ref.at[b], out_hbm.at[b], sems.at[1, b])

    for b in range(blocks):
        copy(b).start()

    def one(b, carry):
        copy(b).wait()
        for p in range(POPS):
            out_ref[b, p] = stream_pop(p, before_ref[b, p], halo_ref.at[b], edge, plane)
        result(b).start()
        return carry

    lax.fori_loop(0, blocks, one, 0)
    for b in range(blocks):
        result(b).wait()


def route_kernel(blocks, devices, table_ref, faces_ref, first_ref, second_ref, halo_ref):
    row = jnp.minimum(lax.axis_index("blk").astype(jnp.int32), blocks - 1)
    swapped = first_partner_above()
    edge, plane = 16, faces_ref.shape[2]
    slot = lanes((edge, plane)) % edge
    line = lanes((1, plane))
    lane = lanes((8, plane)) % 128
    from_north = lane < SOUTH
    in_east = (lane < edge) | ((lane >= SOUTH + edge) & (lane < SOUTH + 2 * edge))
    in_west = ((lane >= edge) & (lane < 2 * edge)) | ((lane >= SOUTH) & (lane < SOUTH + edge))
    dev = functools.partial(dev_of, blocks=blocks)

    def beside(slot_id, face):
        return jnp.where(slot_id < 0, -1, table_ref[jnp.maximum(slot_id, 0), face])

    def one(d, carry):
        here = d * blocks + row
        west, east, south, north, below, above = [table_ref[here, face] for face in range(6)]
        zero = jnp.float32(0.0)
        halo_ref[d, 0:16, :] = jnp.where(
            slot < 5,
            jnp.where(east >= 0, faces_ref[dev(east), 0:16, :], zero),
            jnp.where(west >= 0, faces_ref[dev(west), 0:16, :], zero),
        )

        def y_tile(north_slot, south_slot):
            n = jnp.where(north_slot >= 0, faces_ref[dev(north_slot), 16:24, :], zero)
            s = jnp.where(south_slot >= 0, faces_ref[dev(south_slot), 16:24, :], zero)
            return jnp.where(from_north, n, s)

        own = y_tile(north, south)
        far_east = y_tile(beside(north, 1), beside(south, 1))
        far_west = y_tile(beside(north, 0), beside(south, 0))
        east_part = jnp.where(lane % edge == edge - 1, shift(far_east, edge - 1), shift(own, -1))
        west_part = jnp.where(lane % edge == 0, shift(far_west, 1 - edge), shift(own, 1))
        halo_ref[d, 16:24, :] = jnp.where(in_east, east_part, jnp.where(in_west, west_part, own))
        for slot_id, r in ((north, FIRST + 7), (south, SECOND + 7)):
            halo_ref[d, r : r + 1, :] = jnp.where(slot_id >= 0, faces_ref[dev(slot_id), r : r + 1, :], zero)

        def z_face(from_first, where_from, face, pops, row0):
            def rows(slot_id, r):
                first, second = [ref[dev(slot_id), r : r + 1, :] for ref in (first_ref, second_ref)]
                return jnp.where(slot_id >= 0, jnp.where(from_first, first, second), zero)

            from_x = {1: rows(beside(east, face), 5), -1: rows(beside(west, face), 5)}
            from_y = {1: rows(beside(north, face), 6), -1: rows(beside(south, face), 6)}
            for i, p in enumerate(pops):
                cx, cy, _ = VELOCITIES[p]
                value = shift(rows(where_from, i), -(cx + edge * cy))
                if cx != 0:
                    at = edge - 1 if cx > 0 else 0
                    s = EAST_POPS.index(p) if cx > 0 else 5 + WEST_POPS.index(p)
                    value = jnp.where(line % edge == at, shift(from_x[cx], at - s), value)
                if cy != 0:
                    at = edge - 1 if cy > 0 else 0
                    start = NORTH_POPS.index(p) * edge if cy > 0 else SOUTH + SOUTH_POPS.index(p) * edge
                    value = jnp.where(line // edge == at, shift(from_y[cy], at * edge - start), value)
                halo_ref[d, row0 + i : row0 + i + 1, :] = value

        z_face(swapped, above, 5, UPPER_POPS, FIRST)
        z_face(jnp.logical_not(swapped), below, 4, LOWER_POPS, SECOND)
        return carry

    lax.fori_loop(0, devices, one, 0, unroll=4)


def slab_kernel(
    blocks, devices, chunks, owner_ref, column_ref, rows_ref, out_ref, first_ref, second_ref, field_ref
):
    slab = lax.axis_index("blk").astype(jnp.int32)
    swapped = first_partner_above()
    count, edge, width = out_ref.shape
    start = slab_start(owner_ref, slab, devices)
    group = lanes((edge, width)) // edge
    lane = lanes((edge, width))
    height = blocks * edge

    def chunk(i, carry):
        top = start - 2 + 8 * i
        tiles = [jnp.zeros((edge, width), jnp.float32) for _ in range(8)]
        at = pl.multiple_of(FACE_ROWS + 8 * i, 8)
        values = [
            jnp.concatenate([rows_ref[e, pl.ds(at, 8), 0:128], rows_ref[e, pl.ds(at, 8), 128:256]], axis=0)
            for e in range(devices)
        ]
        for r in range(0, 8, 2):
            inside = (top + r >= 0) & (top + r < height)
            block_row = lax.div(jnp.clip(top + r, 0, height - 1), jnp.int32(edge))
            for e in range(devices):
                column = column_ref[0, e * blocks + block_row]
                hit = group == jnp.where(inside, column, -1)
                for k in range(r, r + 2):
                    part = pltpu.roll(values[e], lax.rem(column + (8 - k), jnp.int32(8)) * edge, 1)
                    if width > 128:
                        part = jnp.concatenate([part] * (width // 128), axis=1)
                    tiles[k] = jnp.where(hit, part, tiles[k])
        for r in range(8):
            field_ref[i * 8 + r] = tiles[r]
        return carry

    lax.fori_loop(0, chunks, chunk, 0)

    def row(r):
        at = r
        mixed = TAP_EDGE * (field_ref[at] + field_ref[at + 4]) + (
            TAP_NEAR * (field_ref[at + 1] + field_ref[at + 3]) + field_ref[at + 2]
        )
        value = mixed
        for step, tap in ((1, TAP_NEAR), (2, TAP_EDGE)):
            left = jnp.where(lane >= step, shift(mixed, step), 0.0)
            right = jnp.where(lane < width - step, shift(mixed, -step), 0.0)
            value = value + tap * (left + right)
        out_ref[r] = value
        low, high = value[0:2], value[edge - 2 : edge]
        first_ref[r] = jnp.where(swapped, high, low)
        second_ref[r] = jnp.where(swapped, low, high)

    by_rows(count, row)


def by_rows(count, body):
    step = 8 if count % 8 == 0 else 4 if count % 4 == 0 else 2

    def several(i, carry):
        for k in range(step):
            body(i * step + k)
        return carry

    lax.fori_loop(0, count // step, several, 0)


def depth_kernel(devices, layers, owner_ref, rows_ref, first_ref, second_ref, out_ref):
    count, edge, width = out_ref.shape
    slab, layer = lax.axis_index("blk").astype(jnp.int32), lax.axis_index("gz").astype(jnp.int32)
    own_rows = jnp.int32(0)
    for j in range(devices):
        own_rows = jnp.where(slab == j, 2 * owner_ref[j], own_rows)
    swapped = first_partner_above()
    depth = lax.broadcasted_iota(jnp.int32, (edge, width), 0)

    def row(r):
        value = rows_ref[r]
        first, second = first_ref[r], second_ref[r]
        below = jnp.where(layer > 0, jnp.where(swapped, second, first), 0.0)
        above = jnp.where(layer < layers - 1, jnp.where(swapped, first, second), 0.0)
        b0, b1, a0, a1 = below[0:1], below[1:2], above[0:1], above[1:2]
        down = jnp.where(depth == 0, b1, shift(value, 1, 0))
        up = jnp.where(depth == edge - 1, a0, shift(value, -1, 0))
        down_2 = jnp.where(depth == 0, b0, jnp.where(depth == 1, b1, shift(value, 2, 0)))
        up_2 = jnp.where(depth == edge - 1, a1, jnp.where(depth == edge - 2, a0, shift(value, -2, 0)))
        total = value + TAP_NEAR * (down + up) + TAP_EDGE * (down_2 + up_2)
        out_ref[r] = jnp.where(r < own_rows, total, 0.0)

    by_rows(count, row)


SMEM = pl.BlockSpec(memory_space=pltpu.SMEM)
VMEM = pl.BlockSpec(memory_space=pltpu.VMEM)


ANY = pl.BlockSpec(memory_space=pl.ANY)


def f32(*shape):
    return jax.ShapeDtypeStruct(shape, jnp.float32)


def hbm(*shape):
    return pltpu.HBM(shape, jnp.float32)


def vmem(*shape):
    return pltpu.VMEM(shape, jnp.float32)


def local(adjoint, velocity, porosity, block_x, neighbours, owner_map):
    blocks, _, edge, plane = adjoint.shape[1:]
    devices, layers = lax.axis_size("blk"), lax.axis_size("gz")
    table = neighbours[0]
    state, flow, design = [pltpu.with_memory_space_constraint(x[0], pltpu.HBM) for x in (adjoint, velocity, porosity)]
    rows_cap = 2 * (3 * (blocks * edge // 2) // devices)
    chunks = -(-(rows_cap + 4) // 8)
    width = devices * edge
    first_pairs = [(g, g ^ 1) for g in range(layers)]
    second_pairs = [(g, (g + 1 if g % 2 else g - 1) % layers) for g in range(layers)]
    faces_shape = (devices, FACE_ROWS, plane)
    post_shape = (blocks, POPS + 1, edge, plane)
    params = pltpu.CompilerParams(vmem_limit_bytes=32 * 1024 * 1024)

    def to_halo(gathered):
        first = lax.ppermute(gathered[:, FIRST : FIRST + 8], "gz", first_pairs)
        second = lax.ppermute(gathered[:, SECOND : SECOND + 8], "gz", second_pairs)
        halo = pl.pallas_call(
            functools.partial(route_kernel, blocks, devices),
            out_shape=f32(*faces_shape),
            in_specs=[SMEM, VMEM, VMEM, VMEM],
            out_specs=VMEM,
            compiler_params=params,
            name="route",
        )(table, gathered, first, second)
        return lax.all_to_all(halo, "blk", 0, 0, tiled=True)

    inputs = [vmem(*state.shape), vmem(*flow.shape), vmem(*design.shape)]
    post, faces = pl.pallas_call(
        functools.partial(first_kernel, blocks),
        out_shape=(hbm(*post_shape), f32(*faces_shape)),
        in_specs=[ANY] * 3,
        out_specs=(ANY, VMEM),
        scratch_shapes=inputs + [vmem(*post_shape), pltpu.SemaphoreType.DMA((4, blocks))],
        compiler_params=params,
        name="collide_first",
    )(state, flow, design)
    halo = to_halo(lax.all_to_all(faces, "blk", 0, 0, tiled=True))
    post, faces = pl.pallas_call(
        functools.partial(second_kernel, blocks, devices, chunks),
        out_shape=(hbm(*state.shape), f32(devices, FACE_ROWS + 8 * chunks, plane)),
        in_specs=[SMEM] + [ANY] * 3 + [VMEM],
        out_specs=(ANY, VMEM),
        scratch_shapes=[vmem(*post_shape)]
        + inputs[1:]
        + [
            vmem(*state.shape),
            vmem(POPS, edge, plane),
            vmem(blocks * plane // 128, edge, 128),
            pltpu.SemaphoreType.DMA((4, blocks)),
        ],
        compiler_params=params,
        name="stream_collide",
    )(owner_map, pltpu.with_memory_space_constraint(post, pltpu.HBM), flow, design, halo)
    gathered = lax.all_to_all(faces, "blk", 0, 0, tiled=True)
    halo = to_halo(gathered)
    slab_shape, ends = (rows_cap, edge, width), (rows_cap, 2, width)
    slab, first, second = pl.pallas_call(
        functools.partial(slab_kernel, blocks, devices, chunks),
        out_shape=(f32(*slab_shape), f32(*ends), f32(*ends)),
        in_specs=[SMEM, SMEM, VMEM],
        out_specs=(VMEM,) * 3,
        scratch_shapes=[vmem(chunks * 8, edge, width)],
        compiler_params=params,
        name="slab_rows",
    )(owner_map, block_x, gathered)
    first = lax.ppermute(first, "gz", first_pairs)
    second = lax.ppermute(second, "gz", second_pairs)
    smoothed = pl.pallas_call(
        functools.partial(depth_kernel, devices, layers),
        out_shape=f32(*slab_shape),
        in_specs=[SMEM, VMEM, VMEM, VMEM],
        out_specs=VMEM,
        compiler_params=params,
        name="slab_depth",
    )(owner_map, slab, first, second)
    moved = pl.pallas_call(
        functools.partial(last_kernel, blocks),
        out_shape=hbm(*state.shape),
        in_specs=[ANY, VMEM],
        out_specs=ANY,
        scratch_shapes=[vmem(*state.shape), vmem(*state.shape), pltpu.SemaphoreType.DMA((2, blocks))],
        compiler_params=params,
        name="stream_last",
    )(pltpu.with_memory_space_constraint(post, pltpu.HBM), halo)
    return (moved[None], smoothed[None, None])


def solution(mesh):
    placed = (
        P("gz", "blk", None, None, None),
        P("gz", "blk", None, None, None),
        P("gz", "blk", None, None),
        P("gz", None),
        P("gz", None, None),
        P(),
    )
    return jax.shard_map(
        local,
        mesh=mesh,
        in_specs=placed,
        out_specs=(P("gz", "blk", None, None, None), P("gz", "blk", None, None, None)),
        check_vma=False,
    )
```

```python
import functools

import jax
import jax.numpy as jnp
import numpy as np
from jax import lax
from jax.experimental import pallas as pl
from jax.experimental.pallas import tpu as pltpu
from jax.sharding import PartitionSpec as P

STEPS = 2
VELOCITIES = [
    (0, 0, 0),
    (1, 0, 0),
    (-1, 0, 0),
    (0, 1, 0),
    (0, -1, 0),
    (0, 0, 1),
    (0, 0, -1),
    (1, 1, 0),
    (-1, -1, 0),
    (1, -1, 0),
    (-1, 1, 0),
    (1, 0, 1),
    (-1, 0, -1),
    (1, 0, -1),
    (-1, 0, 1),
    (0, 1, 1),
    (0, -1, -1),
    (0, 1, -1),
    (0, -1, 1),
]
POPS = 19
EAST_POPS = [1, 7, 9, 11, 13]
WEST_POPS = [2, 8, 10, 12, 14]
NORTH_POPS = [7, 10, 15, 17]
SOUTH_POPS = [8, 9, 16, 18]
UPPER_POPS = [5, 11, 14, 15, 18]
LOWER_POPS = [6, 12, 13, 16, 17]
RELAX_RATE = 1.25
DRAG_RATE = 0.3
TAP_EDGE, TAP_NEAR = 1.0 / 3.0, 2.0 / 3.0

FACE_ROWS = 40
STREAM_GROUP = 5
FIRST, SECOND = 24, 32
SOUTH = 64


SOURCES = 16


def shift(value, amount, axis=1):
    amount = amount % value.shape[axis]
    return value if amount == 0 else pltpu.roll(value, amount, axis)


def lanes(shape):
    return lax.broadcasted_iota(jnp.int32, shape, len(shape) - 1)


def collide_cells(f, u, porosity):
    total, gap = {}, {}
    for i in range(1, POPS, 2):
        total[i], gap[i] = f[i] + f[i + 1], f[i] - f[i + 1]
    ux, uy, uz = u
    mx = gap[1] + gap[7] + gap[9] + gap[11] + gap[13]
    my = gap[3] + gap[7] - gap[9] + gap[15] + gap[17]
    mz = gap[5] + gap[11] - gap[13] + gap[15] - gap[17]
    xy_sum, xz_sum, yz_sum = total[7] + total[9], total[11] + total[13], total[15] + total[17]
    xx = 2.0 * total[1] + xy_sum + xz_sum
    yy = 2.0 * total[3] + xy_sum + yz_sum
    zz = 2.0 * total[5] + xz_sum + yz_sum
    xy, xz, yz = total[7] - total[9], total[11] - total[13], total[15] - total[17]
    mass = 12.0 * f[0] + 2.0 * (total[1] + total[3] + total[5]) + (xy_sum + xz_sum + yz_sum)
    speed_sq = ux * ux + uy * uy + uz * uz
    qx = xx * ux + xy * uy + xz * uz
    qy = xy * ux + yy * uy + yz * uz
    qz = xz * ux + yz * uy + zz * uz
    sens = ux * mx + uy * my + uz * mz
    drag = DRAG_RATE * porosity
    scale = RELAX_RATE / 36.0
    quad = ux * qx + uy * qy + uz * qz
    base = scale * (mass + 1.5 * (speed_sq * mass) - 4.5 * quad) + drag * sens
    gx = (3.0 * scale) * (mx + gap[1] + 3.0 * qx - ux * mass) - drag * mx
    gy = (3.0 * scale) * (my + gap[3] + 3.0 * qy - uy * mass) - drag * my
    gz = (3.0 * scale) * (mz + gap[5] + 3.0 * qz - uz * mass) - drag * mz
    along = {1: gx, 3: gy, 5: gz, 7: gx + gy, 9: gx - gy, 11: gx + gz, 13: gx - gz, 15: gy + gz, 17: gy - gz}
    keep = 1.0 - RELAX_RATE
    post = [base + keep * f[0]]
    for i in range(1, POPS, 2):
        post.append(base + along[i] + keep * f[i])
        post.append(base - along[i] + keep * f[i + 1])
    return post, sens


def collide_block(read, velocity_ref, porosity_ref, post_ref, edge, plane):
    parts = {}
    for low in range(0, edge, 8):
        for left in range(0, plane, 128):
            zs, cells = pl.ds(low, 8), pl.ds(left, 128)
            post, sens = collide_cells(
                [read(p, zs, cells) for p in range(POPS)],
                [velocity_ref[c, zs, cells] for c in range(3)],
                porosity_ref[zs, cells],
            )
            for p in range(POPS):
                post_ref[p, zs, cells] = post[p]
            parts[low, left] = sens
    return parts


def part(ref, p, low, left):
    return ref[p, low : low + 8, left : left + 128]


def pack_faces(block, blocks, swapped, post_ref, faces_ref, edge, plane):
    def put_ends(target, row, cells, low, high):
        faces_ref[target, FIRST + row : FIRST + row + 1, cells] = jnp.where(swapped, high, low)
        faces_ref[target, SECOND + row : SECOND + row + 1, cells] = jnp.where(swapped, low, high)

    lane = lanes((8, 128))
    slot, group = lane % edge, lane // edge
    for left in range(0, plane, 128):
        cells = slice(left, left + 128)
        tiles = []
        for low in range(0, edge, 8):
            tile = part(post_ref, EAST_POPS[0], low, left)
            for s, p in enumerate(EAST_POPS[1:], 1):
                tile = jnp.where(slot == s, shift(part(post_ref, p, low, left), s), tile)
            for s, p in enumerate(WEST_POPS, 5):
                tile = jnp.where(slot == s, shift(part(post_ref, p, low, left), s - (edge - 1)), tile)
            faces_ref[block, low : low + 8, cells] = tile
            tiles.append(tile)
        put_ends(block, 5, cells, tiles[0][0:1], tiles[-1][7:8])
        for i in range(5):
            put_ends(
                block,
                i,
                cells,
                post_ref[UPPER_POPS[i], 0:1, cells],
                post_ref[LOWER_POPS[i], edge - 1 : edge, cells],
            )

    def y_tiles(pops, left, first):
        tiles = []
        for low in range(0, edge, 8):
            tile = None
            for q, p in enumerate(pops):
                moved = shift(part(post_ref, p, low, left), q * edge if first == 0 else (q + 5) * edge)
                tile = moved if tile is None else jnp.where(group == first + q, moved, tile)
            tiles.append(tile)
        return tiles

    north = y_tiles(NORTH_POPS, 0, 0)
    south = y_tiles(SOUTH_POPS, plane - 128, 4)

    def put_y(target, tiles, start, pop, left, first, row):
        cells = slice(start, start + 64)
        for half in range(2):
            at = half * 128
            faces_ref[target, 16:24, at + start : at + start + 64] = tiles[half][:, cells]
            line = jnp.where(group == first, part(post_ref, pop, half * 8, left), 0.0)
            line = pltpu.roll(line, (128 - first * edge) % 128, 1, stride=edge, stride_axis=0)
            faces_ref[target, row + 7 : row + 8, at : at + 128] = jnp.sum(line, axis=0, keepdims=True)
        put_ends(target, 6, cells, tiles[0][0:1, cells], tiles[1][7:8, cells])

    if block > 0:
        put_y(block - 1, north, 0, 3, 0, 0, FIRST)
    if block < blocks - 1:
        put_y(block + 1, south, SOUTH, 4, plane - 128, 7, SECOND)


def first_partner_above():
    return lax.rem(lax.axis_index("gz").astype(jnp.int32), jnp.int32(2)) == 0


def stream_pop(p, source_ref, halo_ref, edge):
    cx, cy, cz = VELOCITIES[p]
    lane = lanes((8, 128))
    sides, depths = (0, 1), (0, 1)
    value = {(z, c): shift(part(source_ref, p, z * 8, c * 128), -(cx + edge * cy)) for z in depths for c in sides}
    at_face = lane % edge == (edge - 1 if cx > 0 else 0)
    if cx != 0:
        s = EAST_POPS.index(p) if cx > 0 else 5 + WEST_POPS.index(p)
        turn = (edge - 1 if cx > 0 else 0) - s - edge * cy
        arrived = {(z, c): shift(halo_ref[z * 8 : z * 8 + 8, c * 128 : c * 128 + 128], turn) for z in depths for c in sides}
    if cy == 0:
        if cx != 0:
            value = {at: jnp.where(at_face, arrived[at], value[at]) for at in value}
    else:
        far = 7 if cy > 0 else 0
        border = lane // edge == far
        outer = 1 if cy > 0 else 0
        if p in (3, 4):
            row = (FIRST if cy > 0 else SECOND) + 7
            lined = lax.broadcasted_iota(jnp.int32, (8, 128), 0) == lane // edge
            faces = [jnp.where(lined, halo_ref[row : row + 1, at : at + 128], 0.0) for at in (0, 128)]
            for step in (4, 2, 1):
                faces = [face + shift(face, step * edge) for face in faces]
        else:
            start = NORTH_POPS.index(p) * edge if cy > 0 else SOUTH + SOUTH_POPS.index(p) * edge
            faces = [shift(halo_ref[16:24, at : at + 128], far * edge - start) for at in (0, 128)]
        moved = {}
        for z in depths:
            inner = jnp.where(border, value[z, outer], value[z, 1 - outer])
            rim = value[z, outer]
            if cx != 0:
                inner = jnp.where(at_face, jnp.where(border, arrived[z, outer], arrived[z, 1 - outer]), inner)
                rim = jnp.where(at_face, arrived[z, outer], rim)
            moved[z, 1 - outer] = inner
            moved[z, outer] = jnp.where(border, faces[z], rim)
        value = moved
    if cz != 0:
        row = FIRST + UPPER_POPS.index(p) if cz > 0 else SECOND + LOWER_POPS.index(p)
        outer = 1 if cz > 0 else 0
        border = lax.broadcasted_iota(jnp.int32, (8, 128), 0) == (7 if cz > 0 else 0)
        moved = {}
        for c in sides:
            turned = [shift(value[z, c], -cz, 0) for z in depths]
            moved[1 - outer, c] = jnp.where(border, turned[outer], turned[1 - outer])
            moved[outer, c] = jnp.where(border, halo_ref[row : row + 1, c * 128 : c * 128 + 128], turned[outer])
        value = moved
    return value


def stream_block(source_ref, halo_ref, out_ref, edge):
    for start in range(0, POPS, STREAM_GROUP):
        pops = range(start, min(start + STREAM_GROUP, POPS))
        values = [stream_pop(p, source_ref, halo_ref, edge) for p in pops]
        for p, value in zip(pops, values):
            for (z, c), tile in value.items():
                out_ref[p, z * 8 : z * 8 + 8, c * 128 : c * 128 + 128] = tile


def source_rows(d, row, blocks, table_ref, sources_ref, edge):
    here = d * blocks + row
    west, east, south, north, below, above = [table_ref[face, 0, here] for face in range(6)]

    def beside(slot_id, face):
        return jnp.where(slot_id < 0, -1, table_ref[face, 0, jnp.maximum(slot_id, 0)])

    lane = lanes((1, 128))
    in_north = lane < SOUTH
    near = jnp.where(in_north, north, south)
    far_east = jnp.where(in_north, beside(north, 1), beside(south, 1))
    far_west = jnp.where(in_north, beside(north, 0), beside(south, 0))
    in_east, in_west = east_west_groups(lane, edge)
    rows = [
        jnp.where(lane % edge < 5, east, west),
        jnp.where(
            in_east & (lane % edge == edge - 1),
            far_east,
            jnp.where(in_west & (lane % edge == 0), far_west, near),
        ),
        north,
        south,
    ]
    for face, own in ((5, above), (4, below)):
        rows += [own, beside(east, face), beside(west, face), beside(north, face), beside(south, face)]
    for r, slot_id in enumerate(rows):
        device = lax.shift_right_arithmetic(slot_id, jnp.int32(blocks.bit_length() - 1))
        sources_ref[d, r : r + 1, :] = jnp.broadcast_to(device, (1, 128))


def east_west_groups(lane, edge):
    group = lane // edge
    return (group == 0) | (group == 5), (group == 1) | (group == 4)


def first_kernel(
    blocks,
    devices,
    table_hbm,
    state_hbm,
    velocity_hbm,
    porosity_hbm,
    post_ref,
    faces_ref,
    sources_ref,
    state_ref,
    velocity_ref,
    porosity_ref,
    table_ref,
    sems,
    sem,
):
    edge, plane = porosity_ref.shape[1:]
    swapped = first_partner_above()
    row = jnp.minimum(lax.axis_index("blk").astype(jnp.int32), blocks - 1)

    def copy(b):
        return pltpu.make_async_copy(state_hbm.at[b], state_ref.at[b], sems.at[b])

    others = [
        pltpu.make_async_copy(table_hbm, table_ref, sem.at[0]),
        pltpu.make_async_copy(velocity_hbm, velocity_ref, sem.at[1]),
        pltpu.make_async_copy(porosity_hbm, porosity_ref, sem.at[2]),
    ]
    copy(0).start()
    for other in others:
        other.start()
    for b in range(1, blocks):
        copy(b).start()
    for other in others:
        other.wait()
    per = -(-devices // blocks)

    def one(b, carry):
        copy(b).wait()
        parts = collide_block(
            lambda p, zs, cells: state_ref[b, p, zs, cells],
            velocity_ref.at[b],
            porosity_ref.at[b],
            post_ref.at[b],
            edge,
            plane,
        )
        for (low, left), sens in parts.items():
            post_ref[b, POPS, pl.ds(low, 8), pl.ds(left, 128)] = sens
        for k in range(per):
            source_rows(jnp.minimum(b * per + k, devices - 1), row, blocks, table_ref, sources_ref, edge)
        return carry

    lax.fori_loop(0, blocks, one, 0)
    for b in range(blocks):
        pack_faces(b, blocks, swapped, post_ref.at[b], faces_ref, edge, plane)


def slab_start(owner_ref, slab, devices):
    start = jnp.int32(0)
    for j in range(devices):
        start = start + jnp.where(j < slab, 2 * owner_ref[j], 0)
    return start


def second_kernel(
    blocks,
    devices,
    chunks,
    owner_hbm,
    before_ref,
    velocity_hbm,
    porosity_hbm,
    halo_ref,
    near_hbm,
    late_hbm,
    faces_ref,
    velocity_ref,
    porosity_ref,
    post_ref,
    state_ref,
    field_ref,
    turned_ref,
    owner_ref,
    sems,
    sem,
):
    edge, plane = porosity_ref.shape[1:]
    swapped = first_partner_above()
    others = [
        pltpu.make_async_copy(velocity_hbm, velocity_ref, sem.at[1]),
        pltpu.make_async_copy(porosity_hbm, porosity_ref, sem.at[2]),
        pltpu.make_async_copy(owner_hbm, owner_ref, sem.at[0]),
    ]
    for other in others:
        other.start()

    half = blocks // 2

    def result(b, out_hbm, first):
        return pltpu.make_async_copy(post_ref.at[b], out_hbm.at[b - first], sems.at[b])

    def stream(b, carry):
        stream_block(before_ref.at[b], halo_ref.at[b], state_ref.at[b], edge)
        return carry

    lax.fori_loop(0, blocks, stream, 0)
    for other in others:
        other.wait()

    def collide(b, carry):
        parts = collide_block(
            lambda p, zs, cells: state_ref[b, p, zs, cells],
            velocity_ref.at[b],
            porosity_ref.at[b],
            post_ref.at[b],
            edge,
            plane,
        )

        @pl.when(b < half)
        def _():
            result(b, near_hbm, 0).start()

        @pl.when(b >= half)
        def _():
            result(b, late_hbm, half).start()

        for (low, left), sens in parts.items():
            field_ref[b * (plane // 128) + left // 128, pl.ds(low, 8), :] = (
                before_ref[b, POPS, pl.ds(low, 8), pl.ds(left, 128)] + sens
            )
        return carry

    lax.fori_loop(0, blocks, collide, 0)

    for b in range(blocks):
        pack_faces(b, blocks, swapped, post_ref.at[b], faces_ref, edge, plane)
    held = blocks * (plane // 128)
    lane = lanes((8, 128))
    for m in range(4):
        for low in (0, 8):
            turned = [shift(field_ref[c, low : low + 8, :], -2 * m * edge) for c in range(held)]
            for c in range(held + 1):
                ahead = turned[min(c, held - 1)]
                if 0 < c < held and m > 0:
                    ahead = jnp.where(lane < 128 - 2 * m * edge, turned[c - 1], ahead)
                elif m == 0 or c == held:
                    ahead = turned[max(c - 1, 0)]
                turned_ref[m, c, low : low + 8, :] = ahead
    start = jnp.int32(0)
    for j in range(devices):
        first = lax.div(start + 6, jnp.int32(8))
        phase = lax.div(start + 6 - 8 * first, jnp.int32(2))
        for i in range(chunks):
            at = FACE_ROWS + 8 * i
            value = turned_ref[phase, jnp.minimum(first + i, held)]
            faces_ref[j, at : at + 8, 0:128] = value[0:8]
            faces_ref[j, at : at + 8, 128:256] = value[8:16]
        start = start + 2 * owner_ref[j]
    for b in range(blocks):
        (result(b, near_hbm, 0) if b < half else result(b, late_hbm, half)).wait()


def last_kernel(blocks, near_ref, late_hbm, halo_ref, out_hbm, late_ref, out_ref, sems):
    edge = late_ref.shape[2]
    half = blocks // 2

    def late(b):
        return pltpu.make_async_copy(late_hbm.at[b - half], late_ref.at[b - half], sems.at[blocks + b - half])

    def result(b):
        return pltpu.make_async_copy(out_ref.at[b], out_hbm.at[b], sems.at[b])

    for b in range(half, blocks):
        late(b).start()

    def one(b, before_ref):
        stream_block(before_ref, halo_ref.at[b], out_ref.at[b], edge)
        result(b).start()

    def near_one(b, carry):
        one(b, near_ref.at[b])
        return carry

    def late_one(b, carry):
        late(b).wait()
        one(b, late_ref.at[b - half])
        return carry

    lax.fori_loop(0, half, near_one, 0)
    lax.fori_loop(half, blocks, late_one, 0)
    for b in range(blocks):
        result(b).wait()


def route_kernel(devices, sources_ref, faces_ref, first_ref, second_ref, halo_ref, y_ref, above_ref, below_ref):
    edge = 16
    swapped = first_partner_above()
    lane = lanes((8, 128))
    level = lax.broadcasted_iota(jnp.int32, (8, 128), 0)
    x, group = lane % edge, lane // edge
    in_east, in_west = east_west_groups(lane, edge)
    sides = (0, 128)

    def z_tiles(own, pops, last):
        out = list(own)
        for i, p in enumerate(pops):
            cx, cy, _ = VELOCITIES[p]
            if cx != 0:
                face = edge - 1 if cx > 0 else 0
                s = EAST_POPS.index(p) if cx > 0 else 5 + WEST_POPS.index(p)
                for c in range(2):
                    arrived = jnp.broadcast_to(shift(own[c][5:6], face - s), (8, 128))
                    value = jnp.where(x == face, arrived, shift(own[c], -cx))
                    out[c] = jnp.where(level == i, value, out[c])
            if cy != 0:
                outer = 1 if cy > 0 else 0
                face = 7 if cy > 0 else 0
                start = NORTH_POPS.index(p) * edge if cy > 0 else SOUTH + SOUTH_POPS.index(p) * edge
                turned = [shift(side, -cy * edge) for side in own]
                arrived = jnp.broadcast_to(shift(own[0][6:7], face * edge - start), (8, 128))
                inner = jnp.where(group == face, turned[outer], turned[1 - outer])
                rim = jnp.where(group == face, arrived, turned[outer])
                out[1 - outer] = jnp.where(level == i, inner, out[1 - outer])
                out[outer] = jnp.where(level == i, rim, out[outer])
        return [jnp.where(level == 7, last[c], out[c]) for c in range(2)]

    def prepare(e, carry):
        first, second = [[ref[e, :, at : at + 128] for at in sides] for ref in (first_ref, second_ref)]
        above = [jnp.where(swapped, a, b) for a, b in zip(first, second)]
        below = [jnp.where(swapped, b, a) for a, b in zip(first, second)]
        for own, pops, row, ref in ((above, UPPER_POPS, FIRST, above_ref), (below, LOWER_POPS, SECOND, below_ref)):
            last = [faces_ref[e, row + 7 : row + 8, at : at + 128] for at in sides]
            for at, tile in zip(sides, z_tiles(own, pops, last)):
                ref[e, :, at : at + 128] = tile
        for at in sides:
            own = faces_ref[e, 16:24, at : at + 128]
            east = jnp.where(x == edge - 1, shift(own, edge - 1), shift(own, -1))
            west = jnp.where(x == 0, shift(own, 1 - edge), shift(own, 1))
            y_ref[e, :, at : at + 128] = jnp.where(in_east, east, jnp.where(in_west, west, own))
        return carry

    lax.fori_loop(0, devices, prepare, 0, unroll=2)

    def pick(index, tiles_of):
        total = None
        for e in range(devices):
            hit = index == e
            tiles = tiles_of(e)
            total = [jnp.where(hit, t, 0.0 if total is None else total[k]) for k, t in enumerate(tiles)]
        return total

    def one(d, carry):
        row = [jnp.broadcast_to(sources_ref[d, r : r + 1, :], (8, 128)) for r in range(14)]
        spots = [(low, at) for low in (0, 8) for at in sides]
        x_tiles = pick(row[0], lambda e: [faces_ref[e, low : low + 8, at : at + 128] for low, at in spots])
        for (low, at), tile in zip(spots, x_tiles):
            halo_ref[d, low : low + 8, at : at + 128] = tile
        y_tiles = pick(row[1], lambda e: [y_ref[e, :, at : at + 128] for at in sides])
        for at, tile in zip(sides, y_tiles):
            halo_ref[d, 16:24, at : at + 128] = tile
        for pops, last, base, ref, top in ((UPPER_POPS, 2, 4, above_ref, FIRST), (LOWER_POPS, 3, 9, below_ref, SECOND)):
            index = [jnp.where(level == 7, row[last], row[base])] * 2
            for i, p in enumerate(pops):
                cx, cy, _ = VELOCITIES[p]
                if cx != 0:
                    here = (level == i) & (x == (edge - 1 if cx > 0 else 0))
                    index = [jnp.where(here, row[base + (1 if cx > 0 else 2)], side) for side in index]
                if cy != 0:
                    outer, face = (1, 7) if cy > 0 else (0, 0)
                    here = (level == i) & (group == face)
                    index[outer] = jnp.where(here, row[base + (3 if cy > 0 else 4)], index[outer])
            for at, side in zip(sides, index):
                (tile,) = pick(side, lambda e: [ref[e, :, at : at + 128]])
                halo_ref[d, top : top + 8, at : at + 128] = tile
        return carry

    lax.fori_loop(0, devices, one, 0, unroll=2)


def slab_kernel(
    blocks, devices, chunks, owner_ref, column_ref, rows_ref, out_ref, first_ref, second_ref, field_ref
):
    slab = lax.axis_index("blk").astype(jnp.int32)
    swapped = first_partner_above()
    count, edge, width = out_ref.shape
    start = slab_start(owner_ref, slab, devices)
    group = lanes((edge, width)) // edge
    lane = lanes((edge, width))
    height = blocks * edge

    def chunk(i, carry):
        top = start - 2 + 8 * i
        tiles = [jnp.zeros((edge, width), jnp.float32) for _ in range(8)]
        at = pl.multiple_of(FACE_ROWS + 8 * i, 8)
        values = [
            jnp.concatenate([rows_ref[e, pl.ds(at, 8), 0:128], rows_ref[e, pl.ds(at, 8), 128:256]], axis=0)
            for e in range(devices)
        ]
        for r in range(0, 8, 2):
            inside = (top + r >= 0) & (top + r < height)
            block_row = lax.div(jnp.clip(top + r, 0, height - 1), jnp.int32(edge))
            for e in range(devices):
                column = column_ref[0, e * blocks + block_row]
                hit = group == jnp.where(inside, column, -1)
                for k in range(r, r + 2):
                    part = pltpu.roll(values[e], lax.rem(column + (8 - k), jnp.int32(8)) * edge, 1)
                    if width > 128:
                        part = jnp.concatenate([part] * (width // 128), axis=1)
                    tiles[k] = jnp.where(hit, part, tiles[k])
        for r in range(8):
            field_ref[i * 8 + r] = tiles[r]
        return carry

    lax.fori_loop(0, chunks, chunk, 0)

    def row(r):
        at = r
        mixed = TAP_EDGE * (field_ref[at] + field_ref[at + 4]) + (
            TAP_NEAR * (field_ref[at + 1] + field_ref[at + 3]) + field_ref[at + 2]
        )
        value = mixed
        for step, tap in ((1, TAP_NEAR), (2, TAP_EDGE)):
            left = jnp.where(lane >= step, shift(mixed, step), 0.0)
            right = jnp.where(lane < width - step, shift(mixed, -step), 0.0)
            value = value + tap * (left + right)
        out_ref[r] = value
        low, high = value[0:2], value[edge - 2 : edge]
        first_ref[r] = jnp.where(swapped, high, low)
        second_ref[r] = jnp.where(swapped, low, high)

    by_rows(count, row)


def by_rows(count, body):
    step = 8 if count % 8 == 0 else 4 if count % 4 == 0 else 2

    def several(i, carry):
        for k in range(step):
            body(i * step + k)
        return carry

    lax.fori_loop(0, count // step, several, 0)


def depth_kernel(devices, layers, owner_ref, rows_ref, first_ref, second_ref, out_ref):
    count, edge, width = out_ref.shape
    slab, layer = lax.axis_index("blk").astype(jnp.int32), lax.axis_index("gz").astype(jnp.int32)
    own_rows = jnp.int32(0)
    for j in range(devices):
        own_rows = jnp.where(slab == j, 2 * owner_ref[j], own_rows)
    swapped = first_partner_above()
    depth = lax.broadcasted_iota(jnp.int32, (edge, width), 0)

    def row(r):
        value = rows_ref[r]
        first, second = first_ref[r], second_ref[r]
        below = jnp.where(layer > 0, jnp.where(swapped, second, first), 0.0)
        above = jnp.where(layer < layers - 1, jnp.where(swapped, first, second), 0.0)
        b0, b1, a0, a1 = below[0:1], below[1:2], above[0:1], above[1:2]
        down = jnp.where(depth == 0, b1, shift(value, 1, 0))
        up = jnp.where(depth == edge - 1, a0, shift(value, -1, 0))
        down_2 = jnp.where(depth == 0, b0, jnp.where(depth == 1, b1, shift(value, 2, 0)))
        up_2 = jnp.where(depth == edge - 1, a1, jnp.where(depth == edge - 2, a0, shift(value, -2, 0)))
        total = value + TAP_NEAR * (down + up) + TAP_EDGE * (down_2 + up_2)
        out_ref[r] = jnp.where(r < own_rows, total, 0.0)

    by_rows(count, row)


SMEM = pl.BlockSpec(memory_space=pltpu.SMEM)
VMEM = pl.BlockSpec(memory_space=pltpu.VMEM)


ANY = pl.BlockSpec(memory_space=pl.ANY)


def f32(*shape):
    return jax.ShapeDtypeStruct(shape, jnp.float32)


def hbm(*shape):
    return pltpu.HBM(shape, jnp.float32)


def vmem(*shape):
    return pltpu.VMEM(shape, jnp.float32)


def local(adjoint, velocity, porosity, block_x, neighbours, owner_map):
    blocks, _, edge, plane = adjoint.shape[1:]
    devices, layers = lax.axis_size("blk"), lax.axis_size("gz")
    table = pltpu.with_memory_space_constraint(jnp.transpose(neighbours, (2, 0, 1)), pltpu.HBM)
    state, flow, design = [pltpu.with_memory_space_constraint(x[0], pltpu.HBM) for x in (adjoint, velocity, porosity)]
    rows_cap = 2 * (3 * (blocks * edge // 2) // devices)
    chunks = -(-(rows_cap + 4) // 8)
    width = devices * edge
    first_pairs = [(g, g ^ 1) for g in range(layers)]
    second_pairs = [(g, (g + 1 if g % 2 else g - 1) % layers) for g in range(layers)]
    near_shape, late_shape = [(count,) + state.shape[1:] for count in (blocks // 2, blocks - blocks // 2)]
    faces_shape = (devices, FACE_ROWS, plane)
    post_shape = (blocks, POPS + 1, edge, plane)
    params = pltpu.CompilerParams(vmem_limit_bytes=32 * 1024 * 1024)

    def to_halo(gathered):
        first = lax.ppermute(gathered[:, FIRST : FIRST + 8], "gz", first_pairs)
        second = lax.ppermute(gathered[:, SECOND : SECOND + 8], "gz", second_pairs)
        halo = pl.pallas_call(
            functools.partial(route_kernel, devices),
            out_shape=f32(*faces_shape),
            in_specs=[VMEM] * 4,
            out_specs=VMEM,
            scratch_shapes=[vmem(devices, 8, plane)] * 3,
            compiler_params=params,
            name="route",
        )(sources, gathered, first, second)
        return lax.all_to_all(halo, "blk", 0, 0, tiled=True)

    inputs = [vmem(*state.shape), vmem(*flow.shape), vmem(*design.shape)]
    post, faces, sources = pl.pallas_call(
        functools.partial(first_kernel, blocks, devices),
        out_shape=(
            vmem(*post_shape),
            f32(*faces_shape),
            jax.ShapeDtypeStruct((devices, SOURCES, 128), jnp.int32),
        ),
        in_specs=[ANY] * 4,
        out_specs=(VMEM,) * 3,
        scratch_shapes=inputs
        + [
            pltpu.SMEM(table.shape, jnp.int32),
            pltpu.SemaphoreType.DMA((blocks,)),
            pltpu.SemaphoreType.DMA((3,)),
        ],
        compiler_params=params,
        name="collide_first",
    )(table, state, flow, design)
    halo = to_halo(lax.all_to_all(faces, "blk", 0, 0, tiled=True))
    near, late, faces = pl.pallas_call(
        functools.partial(second_kernel, blocks, devices, chunks),
        out_shape=(hbm(*near_shape), hbm(*late_shape), f32(devices, FACE_ROWS + 8 * chunks, plane)),
        in_specs=[ANY, VMEM, ANY, ANY, VMEM],
        out_specs=(ANY, ANY, VMEM),
        scratch_shapes=inputs[1:]
        + [
            vmem(*state.shape),
            vmem(*state.shape),
            vmem(blocks * plane // 128, edge, 128),
            vmem(4, blocks * plane // 128 + 1, edge, 128),
            pltpu.SMEM(owner_map.shape, jnp.int32),
            pltpu.SemaphoreType.DMA((blocks,)),
            pltpu.SemaphoreType.DMA((3,)),
        ],
        compiler_params=params,
        name="stream_collide",
    )(owner_map, post, flow, design, halo)
    gathered = lax.all_to_all(faces, "blk", 0, 0, tiled=True)
    halo = to_halo(gathered)
    slab_shape, ends = (rows_cap, edge, width), (rows_cap, 2, width)
    slab, first, second = pl.pallas_call(
        functools.partial(slab_kernel, blocks, devices, chunks),
        out_shape=(f32(*slab_shape), f32(*ends), f32(*ends)),
        in_specs=[SMEM, SMEM, VMEM],
        out_specs=(VMEM,) * 3,
        scratch_shapes=[vmem(chunks * 8, edge, width)],
        compiler_params=params,
        name="slab_rows",
    )(owner_map, block_x, gathered)
    first = lax.ppermute(first, "gz", first_pairs)
    second = lax.ppermute(second, "gz", second_pairs)
    smoothed = pl.pallas_call(
        functools.partial(depth_kernel, devices, layers),
        out_shape=f32(*slab_shape),
        in_specs=[SMEM, VMEM, VMEM, VMEM],
        out_specs=VMEM,
        compiler_params=params,
        name="slab_depth",
    )(owner_map, slab, first, second)
    moved = pl.pallas_call(
        functools.partial(last_kernel, blocks),
        out_shape=hbm(*state.shape),
        in_specs=[VMEM, ANY, VMEM],
        out_specs=ANY,
        scratch_shapes=[
            vmem(*late_shape),
            vmem(*state.shape),
            pltpu.SemaphoreType.DMA((2 * blocks - blocks // 2,)),
        ],
        compiler_params=params,
        name="stream_last",
    )(near, pltpu.with_memory_space_constraint(late, pltpu.HBM), halo)
    return (moved[None], smoothed[None, None])


def solution(mesh):
    placed = (
        P("gz", "blk", None, None, None),
        P("gz", "blk", None, None, None),
        P("gz", "blk", None, None),
        P("gz", None),
        P("gz", None, None),
        P(),
    )
    return jax.shard_map(
        local,
        mesh=mesh,
        in_specs=placed,
        out_specs=(P("gz", "blk", None, None, None), P("gz", "blk", None, None, None)),
        check_vma=False,
    )
```

```python
import functools

import jax
import jax.numpy as jnp
import numpy as np
from jax import lax
from jax.experimental import pallas as pl
from jax.experimental.pallas import tpu as pltpu
from jax.sharding import PartitionSpec as P

STEPS = 2
VELOCITIES = [
    (0, 0, 0),
    (1, 0, 0),
    (-1, 0, 0),
    (0, 1, 0),
    (0, -1, 0),
    (0, 0, 1),
    (0, 0, -1),
    (1, 1, 0),
    (-1, -1, 0),
    (1, -1, 0),
    (-1, 1, 0),
    (1, 0, 1),
    (-1, 0, -1),
    (1, 0, -1),
    (-1, 0, 1),
    (0, 1, 1),
    (0, -1, -1),
    (0, 1, -1),
    (0, -1, 1),
]
POPS = 19
EAST_POPS = [1, 7, 9, 11, 13]
WEST_POPS = [2, 8, 10, 12, 14]
NORTH_POPS = [7, 10, 15, 17]
SOUTH_POPS = [8, 9, 16, 18]
UPPER_POPS = [5, 11, 14, 15, 18]
LOWER_POPS = [6, 12, 13, 16, 17]
RELAX_RATE = 1.25
DRAG_RATE = 0.3
TAP_EDGE, TAP_NEAR = 1.0 / 3.0, 2.0 / 3.0

FACE_ROWS, HALO_ROWS = 80, 72
Y_ROWS, FIRST, SECOND = 32, 48, 64
SOUTH = 64
STREAM_GROUP = 5


SOURCES = 16


def shift(value, amount, axis=1):
    amount = amount % value.shape[axis]
    return value if amount == 0 else pltpu.roll(value, amount, axis)


def lanes(shape):
    return lax.broadcasted_iota(jnp.int32, shape, len(shape) - 1)


def collide_cells(f, u, porosity):
    total, gap = {}, {}
    for i in range(1, POPS, 2):
        total[i], gap[i] = f[i] + f[i + 1], f[i] - f[i + 1]
    ux, uy, uz = u
    mx = gap[1] + gap[7] + gap[9] + gap[11] + gap[13]
    my = gap[3] + gap[7] - gap[9] + gap[15] + gap[17]
    mz = gap[5] + gap[11] - gap[13] + gap[15] - gap[17]
    xy_sum, xz_sum, yz_sum = total[7] + total[9], total[11] + total[13], total[15] + total[17]
    xx = 2.0 * total[1] + xy_sum + xz_sum
    yy = 2.0 * total[3] + xy_sum + yz_sum
    zz = 2.0 * total[5] + xz_sum + yz_sum
    xy, xz, yz = total[7] - total[9], total[11] - total[13], total[15] - total[17]
    mass = 12.0 * f[0] + 2.0 * (total[1] + total[3] + total[5]) + (xy_sum + xz_sum + yz_sum)
    speed_sq = ux * ux + uy * uy + uz * uz
    qx = xx * ux + xy * uy + xz * uz
    qy = xy * ux + yy * uy + yz * uz
    qz = xz * ux + yz * uy + zz * uz
    sens = ux * mx + uy * my + uz * mz
    drag = DRAG_RATE * porosity
    scale = RELAX_RATE / 36.0
    quad = ux * qx + uy * qy + uz * qz
    base = scale * (mass + 1.5 * (speed_sq * mass) - 4.5 * quad) + drag * sens
    gx = (3.0 * scale) * (mx + gap[1] + 3.0 * qx - ux * mass) - drag * mx
    gy = (3.0 * scale) * (my + gap[3] + 3.0 * qy - uy * mass) - drag * my
    gz = (3.0 * scale) * (mz + gap[5] + 3.0 * qz - uz * mass) - drag * mz
    along = {1: gx, 3: gy, 5: gz, 7: gx + gy, 9: gx - gy, 11: gx + gz, 13: gx - gz, 15: gy + gz, 17: gy - gz}
    keep = 1.0 - RELAX_RATE
    post = [base + keep * f[0]]
    for i in range(1, POPS, 2):
        post.append(base + along[i] + keep * f[i])
        post.append(base - along[i] + keep * f[i + 1])
    return post, sens


def collide_block(read, velocity_ref, porosity_ref, post_ref, edge, plane):
    parts = {}
    for low in range(0, edge, 8):
        for left in range(0, plane, 128):
            zs, cells = pl.ds(low, 8), pl.ds(left, 128)
            post, sens = collide_cells(
                [read(p, zs, cells) for p in range(POPS)],
                [velocity_ref[c, zs, cells] for c in range(3)],
                porosity_ref[zs, cells],
            )
            for p in range(POPS):
                post_ref[p, zs, cells] = post[p]
            parts[low, left] = sens
    return parts


def part(ref, p, low, left):
    return ref[p, low : low + 8, left : left + 128]


def x_rows(low, left):
    at = low * 2 + left // 16
    return slice(at, at + 8)


def end_row(tile, left, row):
    at = tile + left // 16 + row
    return slice(at, at + 1)


def halo_row(upper, left, row):
    at = FIRST + (0 if upper else 12) + (6 if left else 0) + row
    return slice(at, at + 1)


def pack_faces(block, blocks, swapped, post_ref, faces_ref, edge, plane):
    def put_ends(target, row, left, cells, low, high):
        faces_ref[target, end_row(FIRST, left, row), cells] = jnp.where(swapped, high, low)
        faces_ref[target, end_row(SECOND, left, row), cells] = jnp.where(swapped, low, high)

    lane = lanes((8, 128))
    slot, group = lane % edge, lane // edge
    every = slice(0, 128)
    for left in range(0, plane, 128):
        cells = slice(left, left + 128)
        tiles = []
        for low in range(0, edge, 8):
            tile = part(post_ref, EAST_POPS[0], low, left)
            for s, p in enumerate(EAST_POPS[1:], 1):
                tile = jnp.where(slot == s, shift(part(post_ref, p, low, left), s), tile)
            for s, p in enumerate(WEST_POPS, 5):
                tile = jnp.where(slot == s, shift(part(post_ref, p, low, left), s - (edge - 1)), tile)
            faces_ref[block, x_rows(low, left), :] = tile
            tiles.append(tile)
        put_ends(block, 5, left, every, tiles[0][0:1], tiles[-1][7:8])
        for i in range(5):
            put_ends(
                block,
                i,
                left,
                every,
                post_ref[UPPER_POPS[i], 0:1, cells],
                post_ref[LOWER_POPS[i], edge - 1 : edge, cells],
            )

    def y_tiles(pops, left, first):
        tiles = []
        for low in range(0, edge, 8):
            tile = None
            for q, p in enumerate(pops):
                moved = shift(part(post_ref, p, low, left), q * edge if first == 0 else (q + 5) * edge)
                tile = moved if tile is None else jnp.where(group == first + q, moved, tile)
            tiles.append(tile)
        return tiles

    north = y_tiles(NORTH_POPS, 0, 0)
    south = y_tiles(SOUTH_POPS, plane - 128, 4)

    def put_y(target, tiles, start, pop, left, first, row):
        cells = slice(start, start + 64)
        for half in range(2):
            at = Y_ROWS + half * 8
            faces_ref[target, at : at + 8, cells] = tiles[half][:, cells]
            line = jnp.where(group == first, part(post_ref, pop, half * 8, left), 0.0)
            line = pltpu.roll(line, (128 - first * edge) % 128, 1, stride=edge, stride_axis=0)
            faces_ref[target, end_row(row, half * 128, 7), :] = jnp.sum(line, axis=0, keepdims=True)
        put_ends(target, 6, 0, cells, tiles[0][0:1, cells], tiles[1][7:8, cells])

    if block > 0:
        put_y(block - 1, north, 0, 3, 0, 0, FIRST)
    if block < blocks - 1:
        put_y(block + 1, south, SOUTH, 4, plane - 128, 7, SECOND)


def first_partner_above():
    return lax.rem(lax.axis_index("gz").astype(jnp.int32), jnp.int32(2)) == 0


def stream_pop(p, source_ref, halo_ref, edge):
    cx, cy, cz = VELOCITIES[p]
    lane = lanes((8, 128))
    sides, depths = (0, 1), (0, 1)
    value = {(z, c): shift(part(source_ref, p, z * 8, c * 128), -(cx + edge * cy)) for z in depths for c in sides}
    at_face = lane % edge == (edge - 1 if cx > 0 else 0)
    if cx != 0:
        s = EAST_POPS.index(p) if cx > 0 else 5 + WEST_POPS.index(p)
        turn = (edge - 1 if cx > 0 else 0) - s - edge * cy
        arrived = {(z, c): shift(halo_ref[x_rows(z * 8, c * 128), :], turn) for z in depths for c in sides}
    if cy == 0:
        if cx != 0:
            value = {at: jnp.where(at_face, arrived[at], value[at]) for at in value}
    else:
        far = 7 if cy > 0 else 0
        border = lane // edge == far
        outer = 1 if cy > 0 else 0
        if p in (3, 4):
            lined = lax.broadcasted_iota(jnp.int32, (8, 128), 0) == lane // edge
            faces = [jnp.where(lined, halo_ref[halo_row(cy > 0, at, 5), :], 0.0) for at in (0, 128)]
            for step in (4, 2, 1):
                faces = [face + shift(face, step * edge) for face in faces]
        else:
            start = NORTH_POPS.index(p) * edge if cy > 0 else SOUTH + SOUTH_POPS.index(p) * edge
            faces = [shift(halo_ref[at : at + 8, :], far * edge - start) for at in (Y_ROWS, Y_ROWS + 8)]
        moved = {}
        for z in depths:
            inner = jnp.where(border, value[z, outer], value[z, 1 - outer])
            rim = value[z, outer]
            if cx != 0:
                inner = jnp.where(at_face, jnp.where(border, arrived[z, outer], arrived[z, 1 - outer]), inner)
                rim = jnp.where(at_face, arrived[z, outer], rim)
            moved[z, 1 - outer] = inner
            moved[z, outer] = jnp.where(border, faces[z], rim)
        value = moved
    if cz != 0:
        row = UPPER_POPS.index(p) if cz > 0 else LOWER_POPS.index(p)
        outer = 1 if cz > 0 else 0
        border = lax.broadcasted_iota(jnp.int32, (8, 128), 0) == (7 if cz > 0 else 0)
        moved = {}
        for c in sides:
            turned = [shift(value[z, c], -cz, 0) for z in depths]
            moved[1 - outer, c] = jnp.where(border, turned[outer], turned[1 - outer])
            moved[outer, c] = jnp.where(border, halo_ref[halo_row(cz > 0, c * 128, row), :], turned[outer])
        value = moved
    return value


def stream_block(source_ref, halo_ref, out_ref, edge):
    for start in range(0, POPS, STREAM_GROUP):
        pops = range(start, min(start + STREAM_GROUP, POPS))
        values = [stream_pop(p, source_ref, halo_ref, edge) for p in pops]
        for p, value in zip(pops, values):
            for (z, c), tile in value.items():
                out_ref[p, z * 8 : z * 8 + 8, c * 128 : c * 128 + 128] = tile


def source_rows(d, row, blocks, table_ref, sources_ref, edge):
    here = d * blocks + row
    west, east, south, north, below, above = [table_ref[face, 0, here] for face in range(6)]

    def beside(slot_id, face):
        return jnp.where(slot_id < 0, -1, table_ref[face, 0, jnp.maximum(slot_id, 0)])

    lane = lanes((1, 128))
    in_north = lane < SOUTH
    near = jnp.where(in_north, north, south)
    far_east = jnp.where(in_north, beside(north, 1), beside(south, 1))
    far_west = jnp.where(in_north, beside(north, 0), beside(south, 0))
    in_east, in_west = east_west_groups(lane, edge)
    rows = [
        jnp.where(lane % edge < 5, east, west),
        jnp.where(
            in_east & (lane % edge == edge - 1),
            far_east,
            jnp.where(in_west & (lane % edge == 0), far_west, near),
        ),
        north,
        south,
    ]
    for face, own in ((5, above), (4, below)):
        rows += [own, beside(east, face), beside(west, face), beside(north, face), beside(south, face)]
    for r, slot_id in enumerate(rows):
        device = lax.shift_right_arithmetic(slot_id, jnp.int32(blocks.bit_length() - 1))
        sources_ref[d, r : r + 1, :] = jnp.broadcast_to(device, (1, 128))


def east_west_groups(lane, edge):
    group = lane // edge
    return (group == 0) | (group == 5), (group == 1) | (group == 4)


def first_kernel(
    blocks,
    devices,
    table_hbm,
    state_hbm,
    velocity_hbm,
    porosity_hbm,
    post_ref,
    faces_ref,
    sources_ref,
    state_ref,
    velocity_ref,
    porosity_ref,
    table_ref,
    sems,
    sem,
):
    edge, plane = porosity_ref.shape[1:]
    swapped = first_partner_above()
    row = jnp.minimum(lax.axis_index("blk").astype(jnp.int32), blocks - 1)

    def copy(b):
        return pltpu.make_async_copy(state_hbm.at[b], state_ref.at[b], sems.at[b])

    others = [
        pltpu.make_async_copy(table_hbm, table_ref, sem.at[0]),
        pltpu.make_async_copy(velocity_hbm, velocity_ref, sem.at[1]),
        pltpu.make_async_copy(porosity_hbm, porosity_ref, sem.at[2]),
    ]
    copy(0).start()
    for other in others:
        other.start()
    for b in range(1, blocks):
        copy(b).start()
    for other in others:
        other.wait()
    per = -(-devices // blocks)

    def one(b, carry):
        copy(b).wait()
        parts = collide_block(
            lambda p, zs, cells: state_ref[b, p, zs, cells],
            velocity_ref.at[b],
            porosity_ref.at[b],
            post_ref.at[b],
            edge,
            plane,
        )
        for (low, left), sens in parts.items():
            post_ref[b, POPS, pl.ds(low, 8), pl.ds(left, 128)] = sens
        for k in range(per):
            source_rows(jnp.minimum(b * per + k, devices - 1), row, blocks, table_ref, sources_ref, edge)
        return carry

    lax.fori_loop(0, blocks, one, 0)
    for b in range(blocks):
        pack_faces(b, blocks, swapped, post_ref.at[b], faces_ref, edge, plane)


def slab_start(owner_ref, slab, devices):
    start = jnp.int32(0)
    for j in range(devices):
        start = start + jnp.where(j < slab, 2 * owner_ref[j], 0)
    return start


def second_kernel(
    blocks,
    devices,
    chunks,
    owner_hbm,
    before_ref,
    velocity_hbm,
    porosity_hbm,
    halo_ref,
    near_hbm,
    late_hbm,
    faces_ref,
    velocity_ref,
    porosity_ref,
    post_ref,
    state_ref,
    turned_ref,
    owner_ref,
    sems,
    sem,
):
    edge, plane = porosity_ref.shape[1:]
    swapped = first_partner_above()
    others = [
        pltpu.make_async_copy(velocity_hbm, velocity_ref, sem.at[1]),
        pltpu.make_async_copy(porosity_hbm, porosity_ref, sem.at[2]),
        pltpu.make_async_copy(owner_hbm, owner_ref, sem.at[0]),
    ]
    for other in others:
        other.start()

    half = blocks // 2

    def result(b, out_hbm, first):
        return pltpu.make_async_copy(post_ref.at[b], out_hbm.at[b - first], sems.at[b])

    def stream(b, carry):
        stream_block(before_ref.at[b], halo_ref.at[b], state_ref.at[b], edge)
        return carry

    lax.fori_loop(0, blocks, stream, 0)
    for other in others:
        other.wait()

    def collide(b, carry):
        parts = collide_block(
            lambda p, zs, cells: state_ref[b, p, zs, cells],
            velocity_ref.at[b],
            porosity_ref.at[b],
            post_ref.at[b],
            edge,
            plane,
        )

        @pl.when(b < half)
        def _():
            result(b, near_hbm, 0).start()

        @pl.when(b >= half)
        def _():
            result(b, late_hbm, half).start()

        for (low, left), sens in parts.items():
            sens = before_ref[b, POPS, pl.ds(low, 8), pl.ds(left, 128)] + sens
            turned_ref[0, b * (plane // 128) + left // 128, pl.ds(low, 8), :] = sens
        return carry

    lax.fori_loop(0, blocks, collide, 0)

    for b in range(blocks):
        pack_faces(b, blocks, swapped, post_ref.at[b], faces_ref, edge, plane)
    held = blocks * (plane // 128)
    for c in range(held):
        for m in range(1, 4):
            for low in (0, 8):
                turned_ref[m, c, low : low + 8, :] = shift(turned_ref[0, c, low : low + 8, :], -2 * m * edge)
    lane = lanes((edge, 128))
    start = jnp.int32(0)
    for j in range(devices):
        first = lax.div(start + 6, jnp.int32(8)) - 1
        behind = start - 2 - 8 * first
        phase = lax.div(behind, jnp.int32(2))
        turned = [turned_ref[phase, jnp.clip(first + i, 0, held - 1)] for i in range(chunks + 1)]
        kept = lane < 128 - behind * edge
        for i in range(chunks):
            value = jnp.where(kept, turned[i], turned[i + 1])
            at = FACE_ROWS + 16 * i
            if at + 16 <= faces_ref.shape[1]:
                faces_ref[j, at : at + 16, :] = value
            else:
                faces_ref[j, at : at + 8, :] = jnp.where(lane[0:8] < 64, value[0:8], shift(value[8:16], 64))
        start = start + 2 * owner_ref[j]
    for b in range(blocks):
        (result(b, near_hbm, 0) if b < half else result(b, late_hbm, half)).wait()


def last_kernel(blocks, near_ref, late_hbm, halo_ref, out_hbm, late_ref, out_ref, sems):
    edge = late_ref.shape[2]
    half = blocks // 2

    def late(b):
        return pltpu.make_async_copy(late_hbm.at[b - half], late_ref.at[b - half], sems.at[blocks + b - half])

    def result(b):
        return pltpu.make_async_copy(out_ref.at[b], out_hbm.at[b], sems.at[b])

    for b in range(half, blocks):
        late(b).start()

    def one(b, before_ref):
        stream_block(before_ref, halo_ref.at[b], out_ref.at[b], edge)
        result(b).start()

    def near_one(b, carry):
        one(b, near_ref.at[b])
        return carry

    def late_one(b, carry):
        late(b).wait()
        one(b, late_ref.at[b - half])
        return carry

    lax.fori_loop(0, half, near_one, 0)
    lax.fori_loop(half, blocks, late_one, 0)
    for b in range(blocks):
        result(b).wait()


def route_kernel(devices, sources_ref, faces_ref, first_ref, second_ref, halo_ref, y_ref, above_ref, below_ref):
    edge = 16
    swapped = first_partner_above()
    lane = lanes((8, 128))
    level = lax.broadcasted_iota(jnp.int32, (8, 128), 0)
    x, group = lane % edge, lane // edge
    in_east, in_west = east_west_groups(lane, edge)
    sides = (0, 128)

    def z_tiles(own, pops, last):
        out = list(own)
        for i, p in enumerate(pops):
            cx, cy, _ = VELOCITIES[p]
            if cx != 0:
                face = edge - 1 if cx > 0 else 0
                s = EAST_POPS.index(p) if cx > 0 else 5 + WEST_POPS.index(p)
                for c in range(2):
                    arrived = jnp.broadcast_to(shift(own[c][5:6], face - s), (8, 128))
                    value = jnp.where(x == face, arrived, shift(own[c], -cx))
                    out[c] = jnp.where(level == i, value, out[c])
            if cy != 0:
                outer = 1 if cy > 0 else 0
                face = 7 if cy > 0 else 0
                start = NORTH_POPS.index(p) * edge if cy > 0 else SOUTH + SOUTH_POPS.index(p) * edge
                turned = [shift(side, -cy * edge) for side in own]
                arrived = jnp.broadcast_to(shift(own[0][6:7], face * edge - start), (8, 128))
                inner = jnp.where(group == face, turned[outer], turned[1 - outer])
                rim = jnp.where(group == face, arrived, turned[outer])
                out[1 - outer] = jnp.where(level == i, inner, out[1 - outer])
                out[outer] = jnp.where(level == i, rim, out[outer])
        return [jnp.where(level == 5, last[c], out[c]) for c in range(2)]

    def prepare(e, carry):
        first, second = [[ref[e, at : at + 8, :] for at in (0, 8)] for ref in (first_ref, second_ref)]
        above = [jnp.where(swapped, a, b) for a, b in zip(first, second)]
        below = [jnp.where(swapped, b, a) for a, b in zip(first, second)]
        for own, pops, row, ref in ((above, UPPER_POPS, FIRST, above_ref), (below, LOWER_POPS, SECOND, below_ref)):
            last = [faces_ref[e, end_row(row, left, 7), :] for left in sides]
            for at, tile in zip((0, 8), z_tiles(own, pops, last)):
                ref[e, at : at + 8, :] = tile
        for at in (0, 8):
            own = faces_ref[e, Y_ROWS + at : Y_ROWS + at + 8, :]
            east = jnp.where(x == edge - 1, shift(own, edge - 1), shift(own, -1))
            west = jnp.where(x == 0, shift(own, 1 - edge), shift(own, 1))
            y_ref[e, at : at + 8, :] = jnp.where(in_east, east, jnp.where(in_west, west, own))
        return carry

    lax.fori_loop(0, devices, prepare, 0, unroll=2)

    def pick(index, tiles_of):
        total = None
        for e in range(devices):
            hit = index == e
            tiles = tiles_of(e)
            total = [jnp.where(hit, t, 0.0 if total is None else total[k]) for k, t in enumerate(tiles)]
        return total

    def one(d, carry):
        row = [jnp.broadcast_to(sources_ref[d, r : r + 1, :], (8, 128)) for r in range(14)]
        spots = range(0, Y_ROWS, 8)
        for at, tile in zip(spots, pick(row[0], lambda e: [faces_ref[e, at : at + 8, :] for at in spots])):
            halo_ref[d, at : at + 8, :] = tile
        for at, tile in zip((0, 8), pick(row[1], lambda e: [y_ref[e, at : at + 8, :] for at in (0, 8)])):
            halo_ref[d, Y_ROWS + at : Y_ROWS + at + 8, :] = tile
        for pops, last, base, ref, upper in ((UPPER_POPS, 2, 4, above_ref, True), (LOWER_POPS, 3, 9, below_ref, False)):
            index = [jnp.where(level == 5, row[last], row[base])] * 2
            for i, p in enumerate(pops):
                cx, cy, _ = VELOCITIES[p]
                if cx != 0:
                    here = (level == i) & (x == (edge - 1 if cx > 0 else 0))
                    index = [jnp.where(here, row[base + (1 if cx > 0 else 2)], side) for side in index]
                if cy != 0:
                    outer, face = (1, 7) if cy > 0 else (0, 0)
                    here = (level == i) & (group == face)
                    index[outer] = jnp.where(here, row[base + (3 if cy > 0 else 4)], index[outer])
            for left, at, side in zip(sides, (0, 8), index):
                (tile,) = pick(side, lambda e: [ref[e, at : at + 8, :]])
                top = halo_row(upper, left, 0).start
                halo_ref[d, top : top + 6, :] = tile[0:6]
        return carry

    lax.fori_loop(0, devices, one, 0, unroll=2)


def slab_kernel(
    blocks, devices, chunks, owner_ref, column_ref, rows_ref, out_ref, first_ref, second_ref, field_ref
):
    slab = lax.axis_index("blk").astype(jnp.int32)
    swapped = first_partner_above()
    count, edge, width = out_ref.shape
    start = slab_start(owner_ref, slab, devices)
    group = lanes((edge, width)) // edge
    lane = lanes((edge, width))
    height = blocks * edge

    def chunk(i):
        top = start - 2 + 8 * i
        tiles = [jnp.zeros((edge, width), jnp.float32) for _ in range(8)]
        at = FACE_ROWS + 16 * i
        if at + 16 <= rows_ref.shape[1]:
            values = [rows_ref[e, at : at + 16, :] for e in range(devices)]
        else:
            halves = [rows_ref[e, at : at + 8, :] for e in range(devices)]
            values = [jnp.concatenate([half, shift(half, 64)], axis=0) for half in halves]
        for r in range(0, 8, 2):
            inside = (top + r >= 0) & (top + r < height)
            block_row = lax.div(jnp.clip(top + r, 0, height - 1), jnp.int32(edge))
            for e in range(devices):
                column = column_ref[0, e * blocks + block_row]
                hit = group == jnp.where(inside, column, -1)
                for k in range(r, r + 2):
                    part = pltpu.roll(values[e], lax.rem(column + (8 - k), jnp.int32(8)) * edge, 1)
                    if width > 128:
                        part = jnp.concatenate([part] * (width // 128), axis=1)
                    tiles[k] = jnp.where(hit, part, tiles[k])
        for r in range(8):
            field_ref[i * 8 + r] = tiles[r]

    for i in range(chunks):
        chunk(i)

    def row(r):
        at = r
        mixed = TAP_EDGE * (field_ref[at] + field_ref[at + 4]) + (
            TAP_NEAR * (field_ref[at + 1] + field_ref[at + 3]) + field_ref[at + 2]
        )
        value = mixed
        for step, tap in ((1, TAP_NEAR), (2, TAP_EDGE)):
            left = jnp.where(lane >= step, shift(mixed, step), 0.0)
            right = jnp.where(lane < width - step, shift(mixed, -step), 0.0)
            value = value + tap * (left + right)
        out_ref[r] = value
        low, high = value[0:2], value[edge - 2 : edge]
        first_ref[r] = jnp.where(swapped, high, low)
        second_ref[r] = jnp.where(swapped, low, high)

    by_rows(count, row)


def by_rows(count, body):
    step = 8 if count % 8 == 0 else 4 if count % 4 == 0 else 2

    def several(i, carry):
        for k in range(step):
            body(i * step + k)
        return carry

    lax.fori_loop(0, count // step, several, 0)


def depth_kernel(devices, layers, owner_ref, rows_ref, first_ref, second_ref, out_ref):
    count, edge, width = out_ref.shape
    slab, layer = lax.axis_index("blk").astype(jnp.int32), lax.axis_index("gz").astype(jnp.int32)
    own_rows = jnp.int32(0)
    for j in range(devices):
        own_rows = jnp.where(slab == j, 2 * owner_ref[j], own_rows)
    swapped = first_partner_above()
    depth = lax.broadcasted_iota(jnp.int32, (edge, width), 0)

    def row(r):
        value = rows_ref[r]
        first, second = first_ref[r], second_ref[r]
        below = jnp.where(layer > 0, jnp.where(swapped, second, first), 0.0)
        above = jnp.where(layer < layers - 1, jnp.where(swapped, first, second), 0.0)
        b0, b1, a0, a1 = below[0:1], below[1:2], above[0:1], above[1:2]
        down = jnp.where(depth == 0, b1, shift(value, 1, 0))
        up = jnp.where(depth == edge - 1, a0, shift(value, -1, 0))
        down_2 = jnp.where(depth == 0, b0, jnp.where(depth == 1, b1, shift(value, 2, 0)))
        up_2 = jnp.where(depth == edge - 1, a1, jnp.where(depth == edge - 2, a0, shift(value, -2, 0)))
        total = value + TAP_NEAR * (down + up) + TAP_EDGE * (down_2 + up_2)
        out_ref[r] = jnp.where(r < own_rows, total, 0.0)

    by_rows(count, row)


SMEM = pl.BlockSpec(memory_space=pltpu.SMEM)
VMEM = pl.BlockSpec(memory_space=pltpu.VMEM)


ANY = pl.BlockSpec(memory_space=pl.ANY)


def f32(*shape):
    return jax.ShapeDtypeStruct(shape, jnp.float32)


def hbm(*shape):
    return pltpu.HBM(shape, jnp.float32)


def vmem(*shape):
    return pltpu.VMEM(shape, jnp.float32)


def local(adjoint, velocity, porosity, block_x, neighbours, owner_map):
    blocks, _, edge, plane = adjoint.shape[1:]
    devices, layers = lax.axis_size("blk"), lax.axis_size("gz")
    table = pltpu.with_memory_space_constraint(jnp.transpose(neighbours, (2, 0, 1)), pltpu.HBM)
    state, flow, design = [pltpu.with_memory_space_constraint(x[0], pltpu.HBM) for x in (adjoint, velocity, porosity)]
    rows_cap = 2 * (3 * (blocks * edge // 2) // devices)
    chunks = -(-(rows_cap + 4) // 8)
    width = devices * edge
    first_pairs = [(g, g ^ 1) for g in range(layers)]
    second_pairs = [(g, (g + 1 if g % 2 else g - 1) % layers) for g in range(layers)]
    near_shape, late_shape = [(count,) + state.shape[1:] for count in (blocks // 2, blocks - blocks // 2)]
    faces_shape, halo_shape = (devices, FACE_ROWS, 128), (devices, HALO_ROWS, 128)
    row_count = 16 * chunks - (8 if 0 < (rows_cap + 4) % 8 <= 4 else 0)
    post_shape = (blocks, POPS + 1, edge, plane)
    params = pltpu.CompilerParams(vmem_limit_bytes=32 * 1024 * 1024)

    def to_halo(gathered):
        first = lax.ppermute(gathered[:, FIRST : FIRST + 16], "gz", first_pairs)
        second = lax.ppermute(gathered[:, SECOND : SECOND + 16], "gz", second_pairs)
        halo = pl.pallas_call(
            functools.partial(route_kernel, devices),
            out_shape=f32(*halo_shape),
            in_specs=[VMEM] * 4,
            out_specs=VMEM,
            scratch_shapes=[vmem(devices, 16, 128)] * 3,
            compiler_params=params,
            name="route",
        )(sources, gathered, first, second)
        return lax.all_to_all(halo, "blk", 0, 0, tiled=True)

    inputs = [vmem(*state.shape), vmem(*flow.shape), vmem(*design.shape)]
    post, faces, sources = pl.pallas_call(
        functools.partial(first_kernel, blocks, devices),
        out_shape=(
            vmem(*post_shape),
            f32(*faces_shape),
            jax.ShapeDtypeStruct((devices, SOURCES, 128), jnp.int32),
        ),
        in_specs=[ANY] * 4,
        out_specs=(VMEM,) * 3,
        scratch_shapes=inputs
        + [
            pltpu.SMEM(table.shape, jnp.int32),
            pltpu.SemaphoreType.DMA((blocks,)),
            pltpu.SemaphoreType.DMA((3,)),
        ],
        compiler_params=params,
        name="collide_first",
    )(table, state, flow, design)
    halo = to_halo(lax.all_to_all(faces, "blk", 0, 0, tiled=True))
    near, late, faces = pl.pallas_call(
        functools.partial(second_kernel, blocks, devices, chunks),
        out_shape=(hbm(*near_shape), hbm(*late_shape), f32(devices, FACE_ROWS + row_count, 128)),
        in_specs=[ANY, VMEM, ANY, ANY, VMEM],
        out_specs=(ANY, ANY, VMEM),
        scratch_shapes=inputs[1:]
        + [
            vmem(*state.shape),
            vmem(*state.shape),
            vmem(4, blocks * plane // 128, edge, 128),
            pltpu.SMEM(owner_map.shape, jnp.int32),
            pltpu.SemaphoreType.DMA((blocks,)),
            pltpu.SemaphoreType.DMA((3,)),
        ],
        compiler_params=params,
        name="stream_collide",
    )(owner_map, post, flow, design, halo)
    gathered = lax.all_to_all(faces, "blk", 0, 0, tiled=True)
    halo = to_halo(gathered)
    slab_shape, ends = (rows_cap, edge, width), (rows_cap, 2, width)
    slab, first, second = pl.pallas_call(
        functools.partial(slab_kernel, blocks, devices, chunks),
        out_shape=(f32(*slab_shape), f32(*ends), f32(*ends)),
        in_specs=[SMEM, SMEM, VMEM],
        out_specs=(VMEM,) * 3,
        scratch_shapes=[vmem(chunks * 8, edge, width)],
        compiler_params=params,
        name="slab_rows",
    )(owner_map, block_x, gathered)
    first = lax.ppermute(first, "gz", first_pairs)
    second = lax.ppermute(second, "gz", second_pairs)
    smoothed = pl.pallas_call(
        functools.partial(depth_kernel, devices, layers),
        out_shape=f32(*slab_shape),
        in_specs=[SMEM, VMEM, VMEM, VMEM],
        out_specs=VMEM,
        compiler_params=params,
        name="slab_depth",
    )(owner_map, slab, first, second)
    moved = pl.pallas_call(
        functools.partial(last_kernel, blocks),
        out_shape=hbm(*state.shape),
        in_specs=[VMEM, ANY, VMEM],
        out_specs=ANY,
        scratch_shapes=[
            vmem(*late_shape),
            vmem(*state.shape),
            pltpu.SemaphoreType.DMA((2 * blocks - blocks // 2,)),
        ],
        compiler_params=params,
        name="stream_last",
    )(near, pltpu.with_memory_space_constraint(late, pltpu.HBM), halo)
    return (moved[None], smoothed[None, None])


def solution(mesh):
    placed = (
        P("gz", "blk", None, None, None),
        P("gz", "blk", None, None, None),
        P("gz", "blk", None, None),
        P("gz", None),
        P("gz", None, None),
        P(),
    )
    return jax.shard_map(
        local,
        mesh=mesh,
        in_specs=placed,
        out_specs=(P("gz", "blk", None, None, None), P("gz", "blk", None, None, None)),
        check_vma=False,
    )
```

```python
import functools

import jax
import jax.numpy as jnp
import numpy as np
from jax import lax
from jax.experimental import pallas as pl
from jax.experimental.pallas import tpu as pltpu
from jax.sharding import PartitionSpec as P

STEPS = 2
VELOCITIES = [
    (0, 0, 0),
    (1, 0, 0),
    (-1, 0, 0),
    (0, 1, 0),
    (0, -1, 0),
    (0, 0, 1),
    (0, 0, -1),
    (1, 1, 0),
    (-1, -1, 0),
    (1, -1, 0),
    (-1, 1, 0),
    (1, 0, 1),
    (-1, 0, -1),
    (1, 0, -1),
    (-1, 0, 1),
    (0, 1, 1),
    (0, -1, -1),
    (0, 1, -1),
    (0, -1, 1),
]
POPS = 19
EAST_POPS = [1, 7, 9, 11, 13]
WEST_POPS = [2, 8, 10, 12, 14]
NORTH_POPS = [7, 10, 15, 17]
SOUTH_POPS = [8, 9, 16, 18]
UPPER_POPS = [5, 11, 14, 15, 18]
LOWER_POPS = [6, 12, 13, 16, 17]
RELAX_RATE = 1.25
DRAG_RATE = 0.3
TAP_EDGE, TAP_NEAR = 1.0 / 3.0, 2.0 / 3.0

FACE_ROWS, HALO_ROWS = 72, 64
Y_ROWS, FIRST, SECOND = 24, 40, 56
SOUTH = 64
STREAM_GROUP = 5


SOURCES = 16


def shift(value, amount, axis=1):
    amount = amount % value.shape[axis]
    return value if amount == 0 else pltpu.roll(value, amount, axis)


def lanes(shape):
    return lax.broadcasted_iota(jnp.int32, shape, len(shape) - 1)


def collide_cells(f, u, porosity):
    total, gap = {}, {}
    for i in range(1, POPS, 2):
        total[i], gap[i] = f[i] + f[i + 1], f[i] - f[i + 1]
    ux, uy, uz = u
    mx = gap[1] + gap[7] + gap[9] + gap[11] + gap[13]
    my = gap[3] + gap[7] - gap[9] + gap[15] + gap[17]
    mz = gap[5] + gap[11] - gap[13] + gap[15] - gap[17]
    xy_sum, xz_sum, yz_sum = total[7] + total[9], total[11] + total[13], total[15] + total[17]
    xx = 2.0 * total[1] + xy_sum + xz_sum
    yy = 2.0 * total[3] + xy_sum + yz_sum
    zz = 2.0 * total[5] + xz_sum + yz_sum
    xy, xz, yz = total[7] - total[9], total[11] - total[13], total[15] - total[17]
    mass = 12.0 * f[0] + 2.0 * (total[1] + total[3] + total[5]) + (xy_sum + xz_sum + yz_sum)
    speed_sq = ux * ux + uy * uy + uz * uz
    qx = xx * ux + xy * uy + xz * uz
    qy = xy * ux + yy * uy + yz * uz
    qz = xz * ux + yz * uy + zz * uz
    sens = ux * mx + uy * my + uz * mz
    drag = DRAG_RATE * porosity
    scale = RELAX_RATE / 36.0
    quad = ux * qx + uy * qy + uz * qz
    base = scale * (mass + 1.5 * (speed_sq * mass) - 4.5 * quad) + drag * sens
    gx = (3.0 * scale) * (mx + gap[1] + 3.0 * qx - ux * mass) - drag * mx
    gy = (3.0 * scale) * (my + gap[3] + 3.0 * qy - uy * mass) - drag * my
    gz = (3.0 * scale) * (mz + gap[5] + 3.0 * qz - uz * mass) - drag * mz
    along = {1: gx, 3: gy, 5: gz, 7: gx + gy, 9: gx - gy, 11: gx + gz, 13: gx - gz, 15: gy + gz, 17: gy - gz}
    keep = 1.0 - RELAX_RATE
    post = [base + keep * f[0]]
    for i in range(1, POPS, 2):
        post.append(base + along[i] + keep * f[i])
        post.append(base - along[i] + keep * f[i + 1])
    return post, sens


def collide_block(read, velocity_ref, porosity_ref, post_ref, edge, plane):
    parts = {}
    for low in range(0, edge, 8):
        for left in range(0, plane, 128):
            zs, cells = pl.ds(low, 8), pl.ds(left, 128)
            post, sens = collide_cells(
                [read(p, zs, cells) for p in range(POPS)],
                [velocity_ref[c, zs, cells] for c in range(3)],
                porosity_ref[zs, cells],
            )
            for p in range(POPS):
                post_ref[p, zs, cells] = post[p]
            parts[low, left] = sens
    return parts


def part(ref, p, low, left):
    return ref[p, low : low + 8, left : left + 128]


def x_spot(p, depth, side):
    east = p in EAST_POPS
    i = EAST_POPS.index(p) if east else WEST_POPS.index(p)
    if (depth, side) == (1, 1):
        return i // 3, (10 if east else 13) + i % 3
    return depth * 2 + side, (0 if east else 5) + i


def from_east(slot):
    return (slot < 5) | ((slot >= 10) & (slot < 13))


def end_row(tile, left, row):
    at = tile + left // 16 + row
    return slice(at, at + 1)


def halo_row(upper, left, row):
    at = FIRST + (0 if upper else 12) + (6 if left else 0) + row
    return slice(at, at + 1)


def pack_faces(block, blocks, swapped, post_ref, faces_ref, edge, plane):
    def put_ends(target, row, left, cells, low, high):
        faces_ref[target, end_row(FIRST, left, row), cells] = jnp.where(swapped, high, low)
        faces_ref[target, end_row(SECOND, left, row), cells] = jnp.where(swapped, low, high)

    lane = lanes((8, 128))
    slot, group = lane % edge, lane // edge
    every = slice(0, 128)
    tiles = [None] * 3
    for depth, side in ((0, 0), (0, 1), (1, 0), (1, 1)):
        for p in EAST_POPS + WEST_POPS:
            t, s = x_spot(p, depth, side)
            moved = shift(part(post_ref, p, depth * 8, side * 128), s - (0 if p in EAST_POPS else edge - 1))
            tiles[t] = moved if tiles[t] is None else jnp.where(slot == s, moved, tiles[t])
    for t, tile in enumerate(tiles):
        faces_ref[block, t * 8 : t * 8 + 8, :] = tile
    for left in range(0, plane, 128):
        cells = slice(left, left + 128)
        for i in range(5):
            put_ends(
                block,
                i,
                left,
                every,
                post_ref[UPPER_POPS[i], 0:1, cells],
                post_ref[LOWER_POPS[i], edge - 1 : edge, cells],
            )

    def y_tiles(pops, left, first):
        tiles = []
        for low in range(0, edge, 8):
            tile = None
            for q, p in enumerate(pops):
                moved = shift(part(post_ref, p, low, left), q * edge if first == 0 else (q + 5) * edge)
                tile = moved if tile is None else jnp.where(group == first + q, moved, tile)
            tiles.append(tile)
        return tiles

    north = y_tiles(NORTH_POPS, 0, 0)
    south = y_tiles(SOUTH_POPS, plane - 128, 4)

    def put_y(target, tiles, start, pop, left, first, row):
        cells = slice(start, start + 64)
        for half in range(2):
            at = Y_ROWS + half * 8
            faces_ref[target, at : at + 8, cells] = tiles[half][:, cells]
            line = jnp.where(group == first, part(post_ref, pop, half * 8, left), 0.0)
            line = pltpu.roll(line, (128 - first * edge) % 128, 1, stride=edge, stride_axis=0)
            faces_ref[target, end_row(row, half * 128, 7), :] = jnp.sum(line, axis=0, keepdims=True)
        put_ends(target, 6, 0, cells, tiles[0][0:1, cells], tiles[1][7:8, cells])

    if block > 0:
        put_y(block - 1, north, 0, 3, 0, 0, FIRST)
    if block < blocks - 1:
        put_y(block + 1, south, SOUTH, 4, plane - 128, 7, SECOND)


def first_partner_above():
    return lax.rem(lax.axis_index("gz").astype(jnp.int32), jnp.int32(2)) == 0


def stream_pop(p, source_ref, halo_ref, edge):
    cx, cy, cz = VELOCITIES[p]
    lane = lanes((8, 128))
    sides, depths = (0, 1), (0, 1)
    value = {(z, c): shift(part(source_ref, p, z * 8, c * 128), -(cx + edge * cy)) for z in depths for c in sides}
    at_face = lane % edge == (edge - 1 if cx > 0 else 0)
    if cx != 0:
        arrived = {}
        for z in depths:
            for c in sides:
                t, s = x_spot(p, z, c)
                turn = (edge - 1 if cx > 0 else 0) - s - edge * cy
                arrived[z, c] = shift(halo_ref[t * 8 : t * 8 + 8, :], turn)
    if cy == 0:
        if cx != 0:
            value = {at: jnp.where(at_face, arrived[at], value[at]) for at in value}
    else:
        far = 7 if cy > 0 else 0
        border = lane // edge == far
        outer = 1 if cy > 0 else 0
        if p in (3, 4):
            lined = lax.broadcasted_iota(jnp.int32, (8, 128), 0) == lane // edge
            faces = [jnp.where(lined, halo_ref[halo_row(cy > 0, at, 5), :], 0.0) for at in (0, 128)]
            for step in (4, 2, 1):
                faces = [face + shift(face, step * edge) for face in faces]
        else:
            start = NORTH_POPS.index(p) * edge if cy > 0 else SOUTH + SOUTH_POPS.index(p) * edge
            faces = [shift(halo_ref[at : at + 8, :], far * edge - start) for at in (Y_ROWS, Y_ROWS + 8)]
        moved = {}
        for z in depths:
            inner = jnp.where(border, value[z, outer], value[z, 1 - outer])
            rim = value[z, outer]
            if cx != 0:
                inner = jnp.where(at_face, jnp.where(border, arrived[z, outer], arrived[z, 1 - outer]), inner)
                rim = jnp.where(at_face, arrived[z, outer], rim)
            moved[z, 1 - outer] = inner
            moved[z, outer] = jnp.where(border, faces[z], rim)
        value = moved
    if cz != 0:
        row = UPPER_POPS.index(p) if cz > 0 else LOWER_POPS.index(p)
        outer = 1 if cz > 0 else 0
        border = lax.broadcasted_iota(jnp.int32, (8, 128), 0) == (7 if cz > 0 else 0)
        moved = {}
        for c in sides:
            turned = [shift(value[z, c], -cz, 0) for z in depths]
            moved[1 - outer, c] = jnp.where(border, turned[outer], turned[1 - outer])
            moved[outer, c] = jnp.where(border, halo_ref[halo_row(cz > 0, c * 128, row), :], turned[outer])
        value = moved
    return value


def stream_block(source_ref, halo_ref, out_ref, edge):
    for start in range(0, POPS, STREAM_GROUP):
        pops = range(start, min(start + STREAM_GROUP, POPS))
        values = [stream_pop(p, source_ref, halo_ref, edge) for p in pops]
        for p, value in zip(pops, values):
            for (z, c), tile in value.items():
                out_ref[p, z * 8 : z * 8 + 8, c * 128 : c * 128 + 128] = tile


def source_rows(d, row, blocks, table_ref, sources_ref, edge):
    here = d * blocks + row
    west, east, south, north, below, above = [table_ref[face, 0, here] for face in range(6)]

    def beside(slot_id, face):
        return jnp.where(slot_id < 0, -1, table_ref[face, 0, jnp.maximum(slot_id, 0)])

    lane = lanes((1, 128))
    in_north = lane < SOUTH
    near = jnp.where(in_north, north, south)
    far_east = jnp.where(in_north, beside(north, 1), beside(south, 1))
    far_west = jnp.where(in_north, beside(north, 0), beside(south, 0))
    in_east, in_west = east_west_groups(lane, edge)
    rows = [
        jnp.where(from_east(lane % edge), east, west),
        jnp.where(
            in_east & (lane % edge == edge - 1),
            far_east,
            jnp.where(in_west & (lane % edge == 0), far_west, near),
        ),
        north,
        south,
    ]
    for face, own in ((5, above), (4, below)):
        rows += [own, beside(east, face), beside(west, face), beside(north, face), beside(south, face)]
    for r, slot_id in enumerate(rows):
        device = lax.shift_right_arithmetic(slot_id, jnp.int32(blocks.bit_length() - 1))
        sources_ref[d, r : r + 1, :] = jnp.broadcast_to(device, (1, 128))


def east_west_groups(lane, edge):
    group = lane // edge
    return (group == 0) | (group == 5), (group == 1) | (group == 4)


def first_kernel(
    blocks,
    devices,
    table_hbm,
    state_hbm,
    velocity_hbm,
    porosity_hbm,
    post_ref,
    faces_ref,
    sources_ref,
    state_ref,
    velocity_ref,
    porosity_ref,
    table_ref,
    sems,
    sem,
):
    edge, plane = porosity_ref.shape[1:]
    swapped = first_partner_above()
    row = jnp.minimum(lax.axis_index("blk").astype(jnp.int32), blocks - 1)

    def copy(b):
        return pltpu.make_async_copy(state_hbm.at[b], state_ref.at[b], sems.at[b])

    others = [
        pltpu.make_async_copy(table_hbm, table_ref, sem.at[0]),
        pltpu.make_async_copy(velocity_hbm, velocity_ref, sem.at[1]),
        pltpu.make_async_copy(porosity_hbm, porosity_ref, sem.at[2]),
    ]
    copy(0).start()
    for other in others:
        other.start()
    for b in range(1, blocks):
        copy(b).start()
    for other in others:
        other.wait()
    per = -(-devices // blocks)

    def one(b, carry):
        copy(b).wait()
        parts = collide_block(
            lambda p, zs, cells: state_ref[b, p, zs, cells],
            velocity_ref.at[b],
            porosity_ref.at[b],
            post_ref.at[b],
            edge,
            plane,
        )
        for (low, left), sens in parts.items():
            post_ref[b, POPS, pl.ds(low, 8), pl.ds(left, 128)] = sens
        for k in range(per):
            source_rows(jnp.minimum(b * per + k, devices - 1), row, blocks, table_ref, sources_ref, edge)
        return carry

    lax.fori_loop(0, blocks, one, 0)
    for b in range(blocks):
        pack_faces(b, blocks, swapped, post_ref.at[b], faces_ref, edge, plane)


def slab_start(owner_ref, slab, devices):
    start = jnp.int32(0)
    for j in range(devices):
        start = start + jnp.where(j < slab, 2 * owner_ref[j], 0)
    return start


def second_kernel(
    blocks,
    devices,
    chunks,
    owner_hbm,
    before_ref,
    velocity_hbm,
    porosity_hbm,
    halo_ref,
    near_hbm,
    late_hbm,
    faces_ref,
    velocity_ref,
    porosity_ref,
    post_ref,
    state_ref,
    turned_ref,
    owner_ref,
    sems,
    sem,
):
    edge, plane = porosity_ref.shape[1:]
    swapped = first_partner_above()
    others = [
        pltpu.make_async_copy(velocity_hbm, velocity_ref, sem.at[1]),
        pltpu.make_async_copy(porosity_hbm, porosity_ref, sem.at[2]),
        pltpu.make_async_copy(owner_hbm, owner_ref, sem.at[0]),
    ]
    for other in others:
        other.start()

    half = blocks // 2

    def result(b, out_hbm, first):
        return pltpu.make_async_copy(post_ref.at[b], out_hbm.at[b - first], sems.at[b])

    def stream(b, carry):
        stream_block(before_ref.at[b], halo_ref.at[b], state_ref.at[b], edge)
        return carry

    lax.fori_loop(0, blocks, stream, 0)
    for other in others:
        other.wait()

    def collide(b, carry):
        parts = collide_block(
            lambda p, zs, cells: state_ref[b, p, zs, cells],
            velocity_ref.at[b],
            porosity_ref.at[b],
            post_ref.at[b],
            edge,
            plane,
        )

        @pl.when(b < half)
        def _():
            result(b, near_hbm, 0).start()

        @pl.when(b >= half)
        def _():
            result(b, late_hbm, half).start()

        for (low, left), sens in parts.items():
            sens = before_ref[b, POPS, pl.ds(low, 8), pl.ds(left, 128)] + sens
            turned_ref[0, b * (plane // 128) + left // 128, pl.ds(low, 8), :] = sens
        return carry

    lax.fori_loop(0, blocks, collide, 0)

    for b in range(blocks):
        pack_faces(b, blocks, swapped, post_ref.at[b], faces_ref, edge, plane)
    held = blocks * (plane // 128)
    for c in range(held):
        for m in range(1, 4):
            for low in (0, 8):
                turned_ref[m, c, low : low + 8, :] = shift(turned_ref[0, c, low : low + 8, :], -2 * m * edge)
    lane = lanes((edge, 128))
    start = jnp.int32(0)
    for j in range(devices):
        first = lax.div(start + 6, jnp.int32(8)) - 1
        behind = start - 2 - 8 * first
        phase = lax.div(behind, jnp.int32(2))
        turned = [turned_ref[phase, jnp.clip(first + i, 0, held - 1)] for i in range(chunks + 1)]
        kept = lane < 128 - behind * edge
        for i in range(chunks):
            value = jnp.where(kept, turned[i], turned[i + 1])
            at = FACE_ROWS + 16 * i
            if at + 16 <= faces_ref.shape[1]:
                faces_ref[j, at : at + 16, :] = value
            else:
                faces_ref[j, at : at + 8, :] = jnp.where(lane[0:8] < 64, value[0:8], shift(value[8:16], 64))
        start = start + 2 * owner_ref[j]
    for b in range(blocks):
        (result(b, near_hbm, 0) if b < half else result(b, late_hbm, half)).wait()


def last_kernel(blocks, near_ref, late_hbm, halo_ref, out_hbm, late_ref, out_ref, sems):
    edge = late_ref.shape[2]
    half = blocks // 2

    def late(b):
        return pltpu.make_async_copy(late_hbm.at[b - half], late_ref.at[b - half], sems.at[blocks + b - half])

    def result(b):
        return pltpu.make_async_copy(out_ref.at[b], out_hbm.at[b], sems.at[b])

    for b in range(half, blocks):
        late(b).start()

    def one(b, before_ref):
        stream_block(before_ref, halo_ref.at[b], out_ref.at[b], edge)
        result(b).start()

    def near_one(b, carry):
        one(b, near_ref.at[b])
        return carry

    def late_one(b, carry):
        late(b).wait()
        one(b, late_ref.at[b - half])
        return carry

    lax.fori_loop(0, half, near_one, 0)
    lax.fori_loop(half, blocks, late_one, 0)
    for b in range(blocks):
        result(b).wait()


def route_kernel(devices, sources_ref, faces_ref, first_ref, second_ref, halo_ref, y_ref, above_ref, below_ref):
    edge = 16
    swapped = first_partner_above()
    lane = lanes((8, 128))
    level = lax.broadcasted_iota(jnp.int32, (8, 128), 0)
    x, group = lane % edge, lane // edge
    in_east, in_west = east_west_groups(lane, edge)
    sides = (0, 128)

    def z_tiles(own, pops, last):
        out = list(own)
        for i, p in enumerate(pops):
            cx, cy, _ = VELOCITIES[p]
            if cx != 0:
                face = edge - 1 if cx > 0 else 0
                for c in range(2):
                    value = jnp.where(x == face, shift(own[c], cx * (edge - 1)), shift(own[c], -cx))
                    out[c] = jnp.where(level == i, value, out[c])
            if cy != 0:
                outer = 1 if cy > 0 else 0
                face = 7 if cy > 0 else 0
                start = NORTH_POPS.index(p) * edge if cy > 0 else SOUTH + SOUTH_POPS.index(p) * edge
                turned = [shift(side, -cy * edge) for side in own]
                arrived = jnp.broadcast_to(shift(own[0][6:7], face * edge - start), (8, 128))
                inner = jnp.where(group == face, turned[outer], turned[1 - outer])
                rim = jnp.where(group == face, arrived, turned[outer])
                out[1 - outer] = jnp.where(level == i, inner, out[1 - outer])
                out[outer] = jnp.where(level == i, rim, out[outer])
        return [jnp.where(level == 5, last[c], out[c]) for c in range(2)]

    def prepare(e, carry):
        first, second = [[ref[e, at : at + 8, :] for at in (0, 8)] for ref in (first_ref, second_ref)]
        above = [jnp.where(swapped, a, b) for a, b in zip(first, second)]
        below = [jnp.where(swapped, b, a) for a, b in zip(first, second)]
        for own, pops, row, ref in ((above, UPPER_POPS, FIRST, above_ref), (below, LOWER_POPS, SECOND, below_ref)):
            last = [faces_ref[e, end_row(row, left, 7), :] for left in sides]
            for at, tile in zip((0, 8), z_tiles(own, pops, last)):
                ref[e, at : at + 8, :] = tile
        for at in (0, 8):
            own = faces_ref[e, Y_ROWS + at : Y_ROWS + at + 8, :]
            east = jnp.where(x == edge - 1, shift(own, edge - 1), shift(own, -1))
            west = jnp.where(x == 0, shift(own, 1 - edge), shift(own, 1))
            y_ref[e, at : at + 8, :] = jnp.where(in_east, east, jnp.where(in_west, west, own))
        return carry

    lax.fori_loop(0, devices, prepare, 0, unroll=2)

    def pick(index, tiles_of):
        total = None
        for e in range(devices):
            hit = index == e
            tiles = tiles_of(e)
            total = [jnp.where(hit, t, 0.0 if total is None else total[k]) for k, t in enumerate(tiles)]
        return total

    def one(d, carry):
        row = [jnp.broadcast_to(sources_ref[d, r : r + 1, :], (8, 128)) for r in range(14)]
        spots = range(0, Y_ROWS, 8)
        for at, tile in zip(spots, pick(row[0], lambda e: [faces_ref[e, at : at + 8, :] for at in spots])):
            halo_ref[d, at : at + 8, :] = tile
        for at, tile in zip((0, 8), pick(row[1], lambda e: [y_ref[e, at : at + 8, :] for at in (0, 8)])):
            halo_ref[d, Y_ROWS + at : Y_ROWS + at + 8, :] = tile
        for pops, last, base, ref, upper in ((UPPER_POPS, 2, 4, above_ref, True), (LOWER_POPS, 3, 9, below_ref, False)):
            index = [jnp.where(level == 5, row[last], row[base])] * 2
            for i, p in enumerate(pops):
                cx, cy, _ = VELOCITIES[p]
                if cx != 0:
                    here = (level == i) & (x == (edge - 1 if cx > 0 else 0))
                    index = [jnp.where(here, row[base + (1 if cx > 0 else 2)], side) for side in index]
                if cy != 0:
                    outer, face = (1, 7) if cy > 0 else (0, 0)
                    here = (level == i) & (group == face)
                    index[outer] = jnp.where(here, row[base + (3 if cy > 0 else 4)], index[outer])
            for left, at, side in zip(sides, (0, 8), index):
                (tile,) = pick(side, lambda e: [ref[e, at : at + 8, :]])
                top = halo_row(upper, left, 0).start
                halo_ref[d, top : top + 6, :] = tile[0:6]
        return carry

    lax.fori_loop(0, devices, one, 0, unroll=2)


def slab_kernel(
    blocks, devices, chunks, owner_ref, column_ref, rows_ref, out_ref, first_ref, second_ref, field_ref
):
    slab = lax.axis_index("blk").astype(jnp.int32)
    swapped = first_partner_above()
    count, edge, width = out_ref.shape
    start = slab_start(owner_ref, slab, devices)
    group = lanes((edge, width)) // edge
    lane = lanes((edge, width))
    height = blocks * edge

    def chunk(i):
        top = start - 2 + 8 * i
        tiles = [jnp.zeros((edge, width), jnp.float32) for _ in range(8)]
        at = FACE_ROWS + 16 * i
        if at + 16 <= rows_ref.shape[1]:
            values = [rows_ref[e, at : at + 16, :] for e in range(devices)]
        else:
            halves = [rows_ref[e, at : at + 8, :] for e in range(devices)]
            values = [jnp.concatenate([half, shift(half, 64)], axis=0) for half in halves]
        for r in range(0, 8, 2):
            inside = (top + r >= 0) & (top + r < height)
            block_row = lax.div(jnp.clip(top + r, 0, height - 1), jnp.int32(edge))
            for e in range(devices):
                column = column_ref[0, e * blocks + block_row]
                hit = group == jnp.where(inside, column, -1)
                for k in range(r, r + 2):
                    part = pltpu.roll(values[e], lax.rem(column + (8 - k), jnp.int32(8)) * edge, 1)
                    if width > 128:
                        part = jnp.concatenate([part] * (width // 128), axis=1)
                    tiles[k] = jnp.where(hit, part, tiles[k])
        for r in range(8):
            field_ref[i * 8 + r] = tiles[r]

    for i in range(chunks):
        chunk(i)

    def row(r):
        at = r
        mixed = TAP_EDGE * (field_ref[at] + field_ref[at + 4]) + (
            TAP_NEAR * (field_ref[at + 1] + field_ref[at + 3]) + field_ref[at + 2]
        )
        value = mixed
        for step, tap in ((1, TAP_NEAR), (2, TAP_EDGE)):
            left = jnp.where(lane >= step, shift(mixed, step), 0.0)
            right = jnp.where(lane < width - step, shift(mixed, -step), 0.0)
            value = value + tap * (left + right)
        out_ref[r] = value
        low, high = value[0:2], value[edge - 2 : edge]
        first_ref[r] = jnp.where(swapped, high, low)
        second_ref[r] = jnp.where(swapped, low, high)

    by_rows(count, row)


def by_rows(count, body):
    step = 8 if count % 8 == 0 else 4 if count % 4 == 0 else 2

    def several(i, carry):
        for k in range(step):
            body(i * step + k)
        return carry

    lax.fori_loop(0, count // step, several, 0)


def depth_kernel(devices, layers, owner_ref, rows_ref, first_ref, second_ref, out_ref):
    count, edge, width = out_ref.shape
    slab, layer = lax.axis_index("blk").astype(jnp.int32), lax.axis_index("gz").astype(jnp.int32)
    own_rows = jnp.int32(0)
    for j in range(devices):
        own_rows = jnp.where(slab == j, 2 * owner_ref[j], own_rows)
    swapped = first_partner_above()
    depth = lax.broadcasted_iota(jnp.int32, (edge, width), 0)

    def row(r):
        value = rows_ref[r]
        first, second = first_ref[r], second_ref[r]
        below = jnp.where(layer > 0, jnp.where(swapped, second, first), 0.0)
        above = jnp.where(layer < layers - 1, jnp.where(swapped, first, second), 0.0)
        b0, b1, a0, a1 = below[0:1], below[1:2], above[0:1], above[1:2]
        down = jnp.where(depth == 0, b1, shift(value, 1, 0))
        up = jnp.where(depth == edge - 1, a0, shift(value, -1, 0))
        down_2 = jnp.where(depth == 0, b0, jnp.where(depth == 1, b1, shift(value, 2, 0)))
        up_2 = jnp.where(depth == edge - 1, a1, jnp.where(depth == edge - 2, a0, shift(value, -2, 0)))
        total = value + TAP_NEAR * (down + up) + TAP_EDGE * (down_2 + up_2)
        out_ref[r] = jnp.where(r < own_rows, total, 0.0)

    by_rows(count, row)


SMEM = pl.BlockSpec(memory_space=pltpu.SMEM)
VMEM = pl.BlockSpec(memory_space=pltpu.VMEM)


ANY = pl.BlockSpec(memory_space=pl.ANY)


def f32(*shape):
    return jax.ShapeDtypeStruct(shape, jnp.float32)


def hbm(*shape):
    return pltpu.HBM(shape, jnp.float32)


def vmem(*shape):
    return pltpu.VMEM(shape, jnp.float32)


def local(adjoint, velocity, porosity, block_x, neighbours, owner_map):
    blocks, _, edge, plane = adjoint.shape[1:]
    devices, layers = lax.axis_size("blk"), lax.axis_size("gz")
    table = pltpu.with_memory_space_constraint(jnp.transpose(neighbours, (2, 0, 1)), pltpu.HBM)
    state, flow, design = [pltpu.with_memory_space_constraint(x[0], pltpu.HBM) for x in (adjoint, velocity, porosity)]
    rows_cap = 2 * (3 * (blocks * edge // 2) // devices)
    chunks = -(-(rows_cap + 4) // 8)
    width = devices * edge
    first_pairs = [(g, g ^ 1) for g in range(layers)]
    second_pairs = [(g, (g + 1 if g % 2 else g - 1) % layers) for g in range(layers)]
    near_shape, late_shape = [(count,) + state.shape[1:] for count in (blocks // 2, blocks - blocks // 2)]
    faces_shape, halo_shape = (devices, FACE_ROWS, 128), (devices, HALO_ROWS, 128)
    row_count = 16 * chunks - (8 if 0 < (rows_cap + 4) % 8 <= 4 else 0)
    post_shape = (blocks, POPS + 1, edge, plane)
    params = pltpu.CompilerParams(vmem_limit_bytes=32 * 1024 * 1024)

    def to_halo(gathered):
        first = lax.ppermute(gathered[:, FIRST : FIRST + 16], "gz", first_pairs)
        second = lax.ppermute(gathered[:, SECOND : SECOND + 16], "gz", second_pairs)
        halo = pl.pallas_call(
            functools.partial(route_kernel, devices),
            out_shape=f32(*halo_shape),
            in_specs=[VMEM] * 4,
            out_specs=VMEM,
            scratch_shapes=[vmem(devices, 16, 128)] * 3,
            compiler_params=params,
            name="route",
        )(sources, gathered, first, second)
        return lax.all_to_all(halo, "blk", 0, 0, tiled=True)

    inputs = [vmem(*state.shape), vmem(*flow.shape), vmem(*design.shape)]
    post, faces, sources = pl.pallas_call(
        functools.partial(first_kernel, blocks, devices),
        out_shape=(
            vmem(*post_shape),
            f32(*faces_shape),
            jax.ShapeDtypeStruct((devices, SOURCES, 128), jnp.int32),
        ),
        in_specs=[ANY] * 4,
        out_specs=(VMEM,) * 3,
        scratch_shapes=inputs
        + [
            pltpu.SMEM(table.shape, jnp.int32),
            pltpu.SemaphoreType.DMA((blocks,)),
            pltpu.SemaphoreType.DMA((3,)),
        ],
        compiler_params=params,
        name="collide_first",
    )(table, state, flow, design)
    halo = to_halo(lax.all_to_all(faces, "blk", 0, 0, tiled=True))
    near, late, faces = pl.pallas_call(
        functools.partial(second_kernel, blocks, devices, chunks),
        out_shape=(hbm(*near_shape), hbm(*late_shape), f32(devices, FACE_ROWS + row_count, 128)),
        in_specs=[ANY, VMEM, ANY, ANY, VMEM],
        out_specs=(ANY, ANY, VMEM),
        scratch_shapes=inputs[1:]
        + [
            vmem(*state.shape),
            vmem(*state.shape),
            vmem(4, blocks * plane // 128, edge, 128),
            pltpu.SMEM(owner_map.shape, jnp.int32),
            pltpu.SemaphoreType.DMA((blocks,)),
            pltpu.SemaphoreType.DMA((3,)),
        ],
        compiler_params=params,
        name="stream_collide",
    )(owner_map, post, flow, design, halo)
    gathered = lax.all_to_all(faces, "blk", 0, 0, tiled=True)
    halo = to_halo(gathered)
    slab_shape, ends = (rows_cap, edge, width), (rows_cap, 2, width)
    slab, first, second = pl.pallas_call(
        functools.partial(slab_kernel, blocks, devices, chunks),
        out_shape=(f32(*slab_shape), f32(*ends), f32(*ends)),
        in_specs=[SMEM, SMEM, VMEM],
        out_specs=(VMEM,) * 3,
        scratch_shapes=[vmem(chunks * 8, edge, width)],
        compiler_params=params,
        name="slab_rows",
    )(owner_map, block_x, gathered)
    first = lax.ppermute(first, "gz", first_pairs)
    second = lax.ppermute(second, "gz", second_pairs)
    smoothed = pl.pallas_call(
        functools.partial(depth_kernel, devices, layers),
        out_shape=f32(*slab_shape),
        in_specs=[SMEM, VMEM, VMEM, VMEM],
        out_specs=VMEM,
        compiler_params=params,
        name="slab_depth",
    )(owner_map, slab, first, second)
    moved = pl.pallas_call(
        functools.partial(last_kernel, blocks),
        out_shape=hbm(*state.shape),
        in_specs=[VMEM, ANY, VMEM],
        out_specs=ANY,
        scratch_shapes=[
            vmem(*late_shape),
            vmem(*state.shape),
            pltpu.SemaphoreType.DMA((2 * blocks - blocks // 2,)),
        ],
        compiler_params=params,
        name="stream_last",
    )(near, pltpu.with_memory_space_constraint(late, pltpu.HBM), halo)
    return (moved[None], smoothed[None, None])


def solution(mesh):
    placed = (
        P("gz", "blk", None, None, None),
        P("gz", "blk", None, None, None),
        P("gz", "blk", None, None),
        P("gz", None),
        P("gz", None, None),
        P(),
    )
    return jax.shard_map(
        local,
        mesh=mesh,
        in_specs=placed,
        out_specs=(P("gz", "blk", None, None, None), P("gz", "blk", None, None, None)),
        check_vma=False,
    )
```

```python
import functools

import jax
import jax.numpy as jnp
import numpy as np
from jax import lax
from jax.experimental import pallas as pl
from jax.experimental.pallas import tpu as pltpu
from jax.sharding import PartitionSpec as P

STEPS = 2
VELOCITIES = [
    (0, 0, 0),
    (1, 0, 0),
    (-1, 0, 0),
    (0, 1, 0),
    (0, -1, 0),
    (0, 0, 1),
    (0, 0, -1),
    (1, 1, 0),
    (-1, -1, 0),
    (1, -1, 0),
    (-1, 1, 0),
    (1, 0, 1),
    (-1, 0, -1),
    (1, 0, -1),
    (-1, 0, 1),
    (0, 1, 1),
    (0, -1, -1),
    (0, 1, -1),
    (0, -1, 1),
]
POPS = 19
EAST_POPS = [1, 7, 9, 11, 13]
WEST_POPS = [2, 8, 10, 12, 14]
NORTH_POPS = [7, 10, 15, 17]
SOUTH_POPS = [8, 9, 16, 18]
UPPER_POPS = [5, 11, 14, 15, 18]
LOWER_POPS = [6, 12, 13, 16, 17]
RELAX_RATE = 1.25
DRAG_RATE = 0.3
TAP_EDGE, TAP_NEAR = 1.0 / 3.0, 2.0 / 3.0

FACE_ROWS = 64
Y_ROWS, FIRST, SECOND = 24, 40, 52
SOUTH = 64
EAST_SLOTS = [0, 1, 2, 3, 4]
WEST_SLOTS = [5, 8, 9, 10, 11]
EAST_FREE = [(0, 12), (0, 6), (1, 12), (1, 6), (2, 12)]
WEST_FREE = [(0, 13), (0, 14), (1, 13), (1, 14), (2, 13)]
Y_SPOTS = {3: [(0, 7), (1, 7)], 4: [(2, 6), (2, 7)]}
STREAM_GROUP = 5


SOURCES = 16


def shift(value, amount, axis=1):
    amount = amount % value.shape[axis]
    return value if amount == 0 else pltpu.roll(value, amount, axis)


def lanes(shape):
    return lax.broadcasted_iota(jnp.int32, shape, len(shape) - 1)


def collide_cells(f, u, porosity):
    total, gap = {}, {}
    for i in range(1, POPS, 2):
        total[i], gap[i] = f[i] + f[i + 1], f[i] - f[i + 1]
    ux, uy, uz = u
    mx = gap[1] + gap[7] + gap[9] + gap[11] + gap[13]
    my = gap[3] + gap[7] - gap[9] + gap[15] + gap[17]
    mz = gap[5] + gap[11] - gap[13] + gap[15] - gap[17]
    xy_sum, xz_sum, yz_sum = total[7] + total[9], total[11] + total[13], total[15] + total[17]
    xx = 2.0 * total[1] + xy_sum + xz_sum
    yy = 2.0 * total[3] + xy_sum + yz_sum
    zz = 2.0 * total[5] + xz_sum + yz_sum
    xy, xz, yz = total[7] - total[9], total[11] - total[13], total[15] - total[17]
    mass = 12.0 * f[0] + 2.0 * (total[1] + total[3] + total[5]) + (xy_sum + xz_sum + yz_sum)
    speed_sq = ux * ux + uy * uy + uz * uz
    qx = xx * ux + xy * uy + xz * uz
    qy = xy * ux + yy * uy + yz * uz
    qz = xz * ux + yz * uy + zz * uz
    sens = ux * mx + uy * my + uz * mz
    drag = DRAG_RATE * porosity
    scale = RELAX_RATE / 36.0
    quad = ux * qx + uy * qy + uz * qz
    base = scale * (mass + 1.5 * (speed_sq * mass) - 4.5 * quad) + drag * sens
    gx = (3.0 * scale) * (mx + gap[1] + 3.0 * qx - ux * mass) - drag * mx
    gy = (3.0 * scale) * (my + gap[3] + 3.0 * qy - uy * mass) - drag * my
    gz = (3.0 * scale) * (mz + gap[5] + 3.0 * qz - uz * mass) - drag * mz
    along = {1: gx, 3: gy, 5: gz, 7: gx + gy, 9: gx - gy, 11: gx + gz, 13: gx - gz, 15: gy + gz, 17: gy - gz}
    keep = 1.0 - RELAX_RATE
    post = [base + keep * f[0]]
    for i in range(1, POPS, 2):
        post.append(base + along[i] + keep * f[i])
        post.append(base - along[i] + keep * f[i + 1])
    return post, sens


def collide_block(read, velocity_ref, porosity_ref, post_ref, edge, plane):
    parts = {}
    for low in range(0, edge, 8):
        for left in range(0, plane, 128):
            zs, cells = pl.ds(low, 8), pl.ds(left, 128)
            post, sens = collide_cells(
                [read(p, zs, cells) for p in range(POPS)],
                [velocity_ref[c, zs, cells] for c in range(3)],
                porosity_ref[zs, cells],
            )
            for p in range(POPS):
                post_ref[p, zs, cells] = post[p]
            parts[low, left] = sens
    return parts


def part(ref, p, low, left):
    return ref[p, low : low + 8, left : left + 128]


def x_spot(p, depth, side):
    east = p in EAST_POPS
    i = EAST_POPS.index(p) if east else WEST_POPS.index(p)
    if (depth, side) == (1, 1):
        return EAST_FREE[i] if east else WEST_FREE[i]
    return depth * 2 + side, EAST_SLOTS[i] if east else WEST_SLOTS[i]


def slot_source(slot, tile, east, west, y_face):
    spots = [(2, s) for s in EAST_SLOTS] + EAST_FREE
    y_slots = [s + half for pair in Y_SPOTS.values() for t, s in pair if t == tile for half in (0, 8)]
    source = west
    for t, s in spots:
        if t in (tile, 2) and (t == tile or s in EAST_SLOTS):
            source = jnp.where(slot == s, east, source)
    for s in y_slots:
        source = jnp.where(slot == s, y_face, source)
    return source


def spread(values, bases, lane):
    places = [(lane - base) % 128 for base in bases]
    for bit in (2, 1, 0):
        moved = [shift(value, 15 << bit) for value in values]
        values = [jnp.where(p & (16 << bit) != 0, m, v) for p, m, v in zip(places, moved, values)]
    return values


def gathered_lanes(values, bases, lane):
    places = [(lane - base) % 128 for base in bases]
    for bit in (0, 1, 2):
        moved = [shift(value, -(15 << bit)) for value in values]
        values = [jnp.where(p & (1 << bit) != 0, m, v) for p, m, v in zip(places, moved, values)]
    return values


def end_row(tile, left, row):
    at = tile + (6 if left else 0) + row
    return slice(at, at + 1)


def halo_row(upper, left, row):
    at = FIRST + (0 if upper else 12) + (6 if left else 0) + row
    return slice(at, at + 1)


def pack_faces(block, blocks, swapped, post_ref, lines_ref, faces_ref, edge, plane):
    def put_ends(target, row, left, cells, low, high):
        faces_ref[target, end_row(FIRST, left, row), cells] = jnp.where(swapped, high, low)
        faces_ref[target, end_row(SECOND, left, row), cells] = jnp.where(swapped, low, high)

    lane = lanes((8, 128))
    slot, group = lane % edge, lane // edge
    every = slice(0, 128)
    tiles = [None] * 3
    for depth, side in ((0, 0), (0, 1), (1, 0), (1, 1)):
        for p in EAST_POPS + WEST_POPS:
            t, s = x_spot(p, depth, side)
            moved = shift(part(post_ref, p, depth * 8, side * 128), s - (0 if p in EAST_POPS else edge - 1))
            tiles[t] = moved if tiles[t] is None else jnp.where(slot == s, moved, tiles[t])
    for p, beyond in ((3, block + 1), (4, block - 1)):
        if 0 <= beyond < blocks:
            for depth, (t, s) in enumerate(Y_SPOTS[p]):
                at = (p - 3) * 16 + depth * 8
                tiles[t] = jnp.where((slot == s) | (slot == s + 8), lines_ref[beyond, at : at + 8, :], tiles[t])
    for t, tile in enumerate(tiles):
        faces_ref[block, t * 8 : t * 8 + 8, :] = tile
    for left in range(0, plane, 128):
        cells = slice(left, left + 128)
        for i in range(5):
            put_ends(
                block,
                i,
                left,
                every,
                post_ref[UPPER_POPS[i], 0:1, cells],
                post_ref[LOWER_POPS[i], edge - 1 : edge, cells],
            )

    def y_tiles(pops, left, first):
        tiles = []
        for low in range(0, edge, 8):
            tile = None
            for q, p in enumerate(pops):
                moved = shift(part(post_ref, p, low, left), q * edge if first == 0 else (q + 5) * edge)
                tile = moved if tile is None else jnp.where(group == first + q, moved, tile)
            tiles.append(tile)
        return tiles

    north = y_tiles(NORTH_POPS, 0, 0)
    south = y_tiles(SOUTH_POPS, plane - 128, 4)

    def put_y(target, tiles, start):
        cells = slice(start, start + 64)
        for half in range(2):
            at = Y_ROWS + half * 8
            faces_ref[target, at : at + 8, cells] = tiles[half][:, cells]
        put_ends(target, 5, 0, cells, tiles[0][0:1, cells], tiles[1][7:8, cells])

    if block > 0:
        put_y(block - 1, north, 0)
    if block < blocks - 1:
        put_y(block + 1, south, SOUTH)


def y_lines(blocks, posts_ref, lines_ref, plane):
    lane = lanes((8, 128))
    spots = [(b, p, depth) for b in range(blocks) for p in (3, 4) for depth in (0, 1)]
    bases = [0 if p == 3 else 112 for _, p, _ in spots]
    lines = [part(posts_ref.at[b], p, depth * 8, 0 if p == 3 else plane - 128) for b, p, depth in spots]
    for (b, p, depth), line, base in zip(spots, spread(lines, bases, lane), bases):
        at = (p - 3) * 16 + depth * 8
        lines_ref[b, at : at + 8, :] = shift(line, Y_SPOTS[p][depth][1] - base)


def y_halos(blocks, halo_ref, lines_ref):
    lane = lanes((8, 128))
    spots = [(b, p, depth) for b in range(blocks) for p in (3, 4) for depth in (0, 1)]
    bases = [Y_SPOTS[p][depth][1] for _, p, depth in spots]
    lines = []
    for b, p, depth in spots:
        t = Y_SPOTS[p][depth][0]
        lines.append(halo_ref[b, t * 8 : t * 8 + 8, :])
    for (b, p, depth), line, base in zip(spots, gathered_lanes(lines, bases, lane), bases):
        at = (p - 3) * 16 + depth * 8
        lines_ref[b, at : at + 8, :] = shift(line, (112 if p == 3 else 0) - base)


def first_partner_above():
    return lax.rem(lax.axis_index("gz").astype(jnp.int32), jnp.int32(2)) == 0


def stream_pop(p, source_ref, halo_ref, y_faces, edge):
    cx, cy, cz = VELOCITIES[p]
    lane = lanes((8, 128))
    sides, depths = (0, 1), (0, 1)
    value = {(z, c): shift(part(source_ref, p, z * 8, c * 128), -(cx + edge * cy)) for z in depths for c in sides}
    at_face = lane % edge == (edge - 1 if cx > 0 else 0)
    if cx != 0:
        arrived = {}
        for z in depths:
            for c in sides:
                t, s = x_spot(p, z, c)
                turn = (edge - 1 if cx > 0 else 0) - s - edge * cy
                arrived[z, c] = shift(halo_ref[t * 8 : t * 8 + 8, :], turn)
    if cy == 0:
        if cx != 0:
            value = {at: jnp.where(at_face, arrived[at], value[at]) for at in value}
    else:
        far = 7 if cy > 0 else 0
        border = lane // edge == far
        outer = 1 if cy > 0 else 0
        if p in (3, 4):
            faces = y_faces[p]
        else:
            start = NORTH_POPS.index(p) * edge if cy > 0 else SOUTH + SOUTH_POPS.index(p) * edge
            faces = [shift(halo_ref[at : at + 8, :], far * edge - start) for at in (Y_ROWS, Y_ROWS + 8)]
        moved = {}
        for z in depths:
            inner = jnp.where(border, value[z, outer], value[z, 1 - outer])
            rim = value[z, outer]
            if cx != 0:
                inner = jnp.where(at_face, jnp.where(border, arrived[z, outer], arrived[z, 1 - outer]), inner)
                rim = jnp.where(at_face, arrived[z, outer], rim)
            moved[z, 1 - outer] = inner
            moved[z, outer] = jnp.where(border, faces[z], rim)
        value = moved
    if cz != 0:
        row = UPPER_POPS.index(p) if cz > 0 else LOWER_POPS.index(p)
        outer = 1 if cz > 0 else 0
        border = lax.broadcasted_iota(jnp.int32, (8, 128), 0) == (7 if cz > 0 else 0)
        moved = {}
        for c in sides:
            turned = [shift(value[z, c], -cz, 0) for z in depths]
            moved[1 - outer, c] = jnp.where(border, turned[outer], turned[1 - outer])
            moved[outer, c] = jnp.where(border, halo_ref[halo_row(cz > 0, c * 128, row), :], turned[outer])
        value = moved
    return value


def stream_block(source_ref, halo_ref, lines_ref, out_ref, edge):
    y_faces = {3: [lines_ref[0:8, :], lines_ref[8:16, :]], 4: [lines_ref[16:24, :], lines_ref[24:32, :]]}
    order = [p for p in range(POPS) if p not in y_faces] + list(y_faces)
    for start in range(0, POPS, STREAM_GROUP):
        pops = order[start : start + STREAM_GROUP]
        values = [stream_pop(p, source_ref, halo_ref, y_faces, edge) for p in pops]
        for p, value in zip(pops, values):
            for (z, c), tile in value.items():
                out_ref[p, z * 8 : z * 8 + 8, c * 128 : c * 128 + 128] = tile


def source_rows(d, row, blocks, table_ref, sources_ref, edge):
    here = d * blocks + row
    west, east, south, north, below, above = [table_ref[face, 0, here] for face in range(6)]

    def beside(slot_id, face):
        return jnp.where(slot_id < 0, -1, table_ref[face, 0, jnp.maximum(slot_id, 0)])

    lane = lanes((1, 128))
    in_north = lane < SOUTH
    near = jnp.where(in_north, north, south)
    far_east = jnp.where(in_north, beside(north, 1), beside(south, 1))
    far_west = jnp.where(in_north, beside(north, 0), beside(south, 0))
    in_east, in_west = east_west_groups(lane, edge)
    rows = [
        slot_source(lane % edge, 0, east, west, north),
        slot_source(lane % edge, 2, east, west, south),
        jnp.where(
            in_east & (lane % edge == edge - 1),
            far_east,
            jnp.where(in_west & (lane % edge == 0), far_west, near),
        ),
    ]
    for face, own in ((5, above), (4, below)):
        rows += [own, beside(east, face), beside(west, face), beside(north, face), beside(south, face)]
    for r, slot_id in enumerate(rows):
        device = lax.shift_right_arithmetic(slot_id, jnp.int32(blocks.bit_length() - 1))
        sources_ref[d, r : r + 1, :] = jnp.broadcast_to(device, (1, 128))


def east_west_groups(lane, edge):
    group = lane // edge
    return (group == 0) | (group == 5), (group == 1) | (group == 4)


def first_kernel(
    blocks,
    devices,
    table_hbm,
    state_hbm,
    velocity_hbm,
    porosity_hbm,
    post_ref,
    faces_ref,
    sources_ref,
    state_ref,
    velocity_ref,
    porosity_ref,
    lines_ref,
    table_ref,
    sems,
    sem,
):
    edge, plane = porosity_ref.shape[1:]
    swapped = first_partner_above()
    row = jnp.minimum(lax.axis_index("blk").astype(jnp.int32), blocks - 1)

    def copy(b):
        return pltpu.make_async_copy(state_hbm.at[b], state_ref.at[b], sems.at[b])

    others = [
        pltpu.make_async_copy(table_hbm, table_ref, sem.at[0]),
        pltpu.make_async_copy(velocity_hbm, velocity_ref, sem.at[1]),
        pltpu.make_async_copy(porosity_hbm, porosity_ref, sem.at[2]),
    ]
    copy(0).start()
    for other in others:
        other.start()
    for b in range(1, blocks):
        copy(b).start()
    for other in others:
        other.wait()
    per = -(-devices // blocks)

    def one(b, carry):
        copy(b).wait()
        parts = collide_block(
            lambda p, zs, cells: state_ref[b, p, zs, cells],
            velocity_ref.at[b],
            porosity_ref.at[b],
            post_ref.at[b],
            edge,
            plane,
        )
        for (low, left), sens in parts.items():
            post_ref[b, POPS, pl.ds(low, 8), pl.ds(left, 128)] = sens
        for k in range(per):
            source_rows(jnp.minimum(b * per + k, devices - 1), row, blocks, table_ref, sources_ref, edge)
        return carry

    lax.fori_loop(0, blocks, one, 0)
    y_lines(blocks, post_ref, lines_ref, plane)
    for b in range(blocks):
        pack_faces(b, blocks, swapped, post_ref.at[b], lines_ref, faces_ref, edge, plane)


def slab_start(owner_ref, slab, devices):
    start = jnp.int32(0)
    for j in range(devices):
        start = start + jnp.where(j < slab, 2 * owner_ref[j], 0)
    return start


def second_kernel(
    blocks,
    devices,
    chunks,
    owner_hbm,
    before_ref,
    velocity_hbm,
    porosity_hbm,
    halo_ref,
    near_hbm,
    late_hbm,
    faces_ref,
    velocity_ref,
    porosity_ref,
    post_ref,
    state_ref,
    lines_ref,
    turned_ref,
    owner_ref,
    sems,
    sem,
):
    edge, plane = porosity_ref.shape[1:]
    swapped = first_partner_above()
    others = [
        pltpu.make_async_copy(velocity_hbm, velocity_ref, sem.at[1]),
        pltpu.make_async_copy(porosity_hbm, porosity_ref, sem.at[2]),
        pltpu.make_async_copy(owner_hbm, owner_ref, sem.at[0]),
    ]
    for other in others:
        other.start()

    half = blocks // 2

    def result(b, out_hbm, first):
        return pltpu.make_async_copy(post_ref.at[b], out_hbm.at[b - first], sems.at[b])

    def stream(b, carry):
        stream_block(before_ref.at[b], halo_ref.at[b], lines_ref.at[b], state_ref.at[b], edge)
        return carry

    y_halos(blocks, halo_ref, lines_ref)
    lax.fori_loop(0, blocks, stream, 0)
    for other in others:
        other.wait()

    def collide(b, carry):
        parts = collide_block(
            lambda p, zs, cells: state_ref[b, p, zs, cells],
            velocity_ref.at[b],
            porosity_ref.at[b],
            post_ref.at[b],
            edge,
            plane,
        )

        @pl.when(b < half)
        def _():
            result(b, near_hbm, 0).start()

        @pl.when(b >= half)
        def _():
            result(b, late_hbm, half).start()

        for (low, left), sens in parts.items():
            sens = before_ref[b, POPS, pl.ds(low, 8), pl.ds(left, 128)] + sens
            turned_ref[0, b * (plane // 128) + left // 128, pl.ds(low, 8), :] = sens
        return carry

    lax.fori_loop(0, blocks, collide, 0)
    y_lines(blocks, post_ref, lines_ref, plane)

    for b in range(blocks):
        pack_faces(b, blocks, swapped, post_ref.at[b], lines_ref, faces_ref, edge, plane)
    held = blocks * (plane // 128)
    for c in range(held):
        for m in range(1, 4):
            for low in (0, 8):
                turned_ref[m, c, low : low + 8, :] = shift(turned_ref[0, c, low : low + 8, :], -2 * m * edge)
    lane = lanes((edge, 128))
    start = jnp.int32(0)
    for j in range(devices):
        first = lax.div(start + 6, jnp.int32(8)) - 1
        behind = start - 2 - 8 * first
        phase = lax.div(behind, jnp.int32(2))
        turned = [turned_ref[phase, jnp.clip(first + i, 0, held - 1)] for i in range(chunks + 1)]
        kept = lane < 128 - behind * edge
        for i in range(chunks):
            value = jnp.where(kept, turned[i], turned[i + 1])
            at = FACE_ROWS + 16 * i
            if at + 16 <= faces_ref.shape[1]:
                faces_ref[j, at : at + 16, :] = value
            else:
                faces_ref[j, at : at + 8, :] = jnp.where(lane[0:8] < 64, value[0:8], shift(value[8:16], 64))
        start = start + 2 * owner_ref[j]
    for b in range(blocks):
        (result(b, near_hbm, 0) if b < half else result(b, late_hbm, half)).wait()


def last_kernel(blocks, near_ref, late_hbm, halo_ref, out_hbm, late_ref, out_ref, lines_ref, sems):
    edge = late_ref.shape[2]
    half = blocks // 2

    def late(b):
        return pltpu.make_async_copy(late_hbm.at[b - half], late_ref.at[b - half], sems.at[blocks + b - half])

    def result(b):
        return pltpu.make_async_copy(out_ref.at[b], out_hbm.at[b], sems.at[b])

    for b in range(half, blocks):
        late(b).start()

    def one(b, before_ref):
        stream_block(before_ref, halo_ref.at[b], lines_ref.at[b], out_ref.at[b], edge)
        result(b).start()

    def near_one(b, carry):
        one(b, near_ref.at[b])
        return carry

    def late_one(b, carry):
        late(b).wait()
        one(b, late_ref.at[b - half])
        return carry

    y_halos(blocks, halo_ref, lines_ref)
    lax.fori_loop(0, half, near_one, 0)
    lax.fori_loop(half, blocks, late_one, 0)
    for b in range(blocks):
        result(b).wait()


def route_kernel(devices, sources_ref, faces_ref, first_ref, second_ref, halo_ref, y_ref, above_ref, below_ref):
    edge = 16
    swapped = first_partner_above()
    lane = lanes((8, 128))
    level = lax.broadcasted_iota(jnp.int32, (8, 128), 0)
    x, group = lane % edge, lane // edge
    in_east, in_west = east_west_groups(lane, edge)
    sides = (0, 128)

    def z_tiles(own, pops):
        out = list(own)
        for i, p in enumerate(pops):
            cx, cy, _ = VELOCITIES[p]
            if cx != 0:
                face = edge - 1 if cx > 0 else 0
                for c in range(2):
                    value = jnp.where(x == face, shift(own[c], cx * (edge - 1)), shift(own[c], -cx))
                    out[c] = jnp.where(level == i, value, out[c])
            if cy != 0:
                outer = 1 if cy > 0 else 0
                face = 7 if cy > 0 else 0
                start = NORTH_POPS.index(p) * edge if cy > 0 else SOUTH + SOUTH_POPS.index(p) * edge
                turned = [shift(side, -cy * edge) for side in own]
                arrived = jnp.broadcast_to(shift(own[0][5:6], face * edge - start), (8, 128))
                inner = jnp.where(group == face, turned[outer], turned[1 - outer])
                rim = jnp.where(group == face, arrived, turned[outer])
                out[1 - outer] = jnp.where(level == i, inner, out[1 - outer])
                out[outer] = jnp.where(level == i, rim, out[outer])
        return out

    def prepare(e, carry):
        first = [first_ref[e, at : at + 8, :] for at in (0, 6)]
        second = [second_ref[e, 4:12, :], shift(second_ref[e, 8:16, :], -2, 0)]
        above = [jnp.where(swapped, a, b) for a, b in zip(first, second)]
        below = [jnp.where(swapped, b, a) for a, b in zip(first, second)]
        for own, pops, ref in ((above, UPPER_POPS, above_ref), (below, LOWER_POPS, below_ref)):
            for at, tile in zip((0, 8), z_tiles(own, pops)):
                ref[e, at : at + 8, :] = tile
        for at in (0, 8):
            own = faces_ref[e, Y_ROWS + at : Y_ROWS + at + 8, :]
            east = jnp.where(x == edge - 1, shift(own, edge - 1), shift(own, -1))
            west = jnp.where(x == 0, shift(own, 1 - edge), shift(own, 1))
            y_ref[e, at : at + 8, :] = jnp.where(in_east, east, jnp.where(in_west, west, own))
        return carry

    lax.fori_loop(0, devices, prepare, 0, unroll=2)

    def pick(index, tiles_of):
        total = None
        for e in range(devices):
            hit = index == e
            tiles = tiles_of(e)
            total = [jnp.where(hit, t, 0.0 if total is None else total[k]) for k, t in enumerate(tiles)]
        return total

    def one(d, carry):
        row = [jnp.broadcast_to(sources_ref[d, r : r + 1, :], (8, 128)) for r in range(13)]
        for index, spots in ((row[0], (0, 8)), (row[1], (16,))):
            for at, tile in zip(spots, pick(index, lambda e: [faces_ref[e, at : at + 8, :] for at in spots])):
                halo_ref[d, at : at + 8, :] = tile
        for at, tile in zip((0, 8), pick(row[2], lambda e: [y_ref[e, at : at + 8, :] for at in (0, 8)])):
            halo_ref[d, Y_ROWS + at : Y_ROWS + at + 8, :] = tile
        for pops, base, ref, upper in ((UPPER_POPS, 3, above_ref, True), (LOWER_POPS, 8, below_ref, False)):
            index = [row[base]] * 2
            for i, p in enumerate(pops):
                cx, cy, _ = VELOCITIES[p]
                if cx != 0:
                    here = (level == i) & (x == (edge - 1 if cx > 0 else 0))
                    index = [jnp.where(here, row[base + (1 if cx > 0 else 2)], side) for side in index]
                if cy != 0:
                    outer, face = (1, 7) if cy > 0 else (0, 0)
                    here = (level == i) & (group == face)
                    index[outer] = jnp.where(here, row[base + (3 if cy > 0 else 4)], index[outer])
            for left, at, side in zip(sides, (0, 8), index):
                (tile,) = pick(side, lambda e: [ref[e, at : at + 8, :]])
                top = halo_row(upper, left, 0).start
                halo_ref[d, top : top + 6, :] = tile[0:6]
        return carry

    lax.fori_loop(0, devices, one, 0, unroll=2)


def slab_kernel(
    blocks, devices, chunks, owner_ref, column_ref, rows_ref, out_ref, first_ref, second_ref, field_ref
):
    slab = lax.axis_index("blk").astype(jnp.int32)
    swapped = first_partner_above()
    count, edge, width = out_ref.shape
    start = slab_start(owner_ref, slab, devices)
    group = lanes((edge, width)) // edge
    lane = lanes((edge, width))
    height = blocks * edge

    def chunk(i):
        top = start - 2 + 8 * i
        tiles = [jnp.zeros((edge, width), jnp.float32) for _ in range(8)]
        at = FACE_ROWS + 16 * i
        if at + 16 <= rows_ref.shape[1]:
            values = [rows_ref[e, at : at + 16, :] for e in range(devices)]
        else:
            halves = [rows_ref[e, at : at + 8, :] for e in range(devices)]
            values = [jnp.concatenate([half, shift(half, 64)], axis=0) for half in halves]
        for r in range(0, 8, 2):
            inside = (top + r >= 0) & (top + r < height)
            block_row = lax.div(jnp.clip(top + r, 0, height - 1), jnp.int32(edge))
            for e in range(devices):
                column = column_ref[0, e * blocks + block_row]
                hit = group == jnp.where(inside, column, -1)
                for k in range(r, r + 2):
                    part = pltpu.roll(values[e], lax.rem(column + (8 - k), jnp.int32(8)) * edge, 1)
                    if width > 128:
                        part = jnp.concatenate([part] * (width // 128), axis=1)
                    tiles[k] = jnp.where(hit, part, tiles[k])
        for r in range(8):
            field_ref[i * 8 + r] = tiles[r]

    for i in range(chunks):
        chunk(i)

    def row(r):
        at = r
        mixed = TAP_EDGE * (field_ref[at] + field_ref[at + 4]) + (
            TAP_NEAR * (field_ref[at + 1] + field_ref[at + 3]) + field_ref[at + 2]
        )
        value = mixed
        for step, tap in ((1, TAP_NEAR), (2, TAP_EDGE)):
            left = jnp.where(lane >= step, shift(mixed, step), 0.0)
            right = jnp.where(lane < width - step, shift(mixed, -step), 0.0)
            value = value + tap * (left + right)
        out_ref[r] = value
        low, high = value[0:2], value[edge - 2 : edge]
        first_ref[r] = jnp.where(swapped, high, low)
        second_ref[r] = jnp.where(swapped, low, high)

    by_rows(count, row)


def by_rows(count, body):
    step = 8 if count % 8 == 0 else 4 if count % 4 == 0 else 2

    def several(i, carry):
        for k in range(step):
            body(i * step + k)
        return carry

    lax.fori_loop(0, count // step, several, 0)


def depth_kernel(devices, layers, owner_ref, rows_ref, first_ref, second_ref, out_ref):
    count, edge, width = out_ref.shape
    slab, layer = lax.axis_index("blk").astype(jnp.int32), lax.axis_index("gz").astype(jnp.int32)
    own_rows = jnp.int32(0)
    for j in range(devices):
        own_rows = jnp.where(slab == j, 2 * owner_ref[j], own_rows)
    swapped = first_partner_above()
    depth = lax.broadcasted_iota(jnp.int32, (edge, width), 0)

    def row(r):
        value = rows_ref[r]
        first, second = first_ref[r], second_ref[r]
        below = jnp.where(layer > 0, jnp.where(swapped, second, first), 0.0)
        above = jnp.where(layer < layers - 1, jnp.where(swapped, first, second), 0.0)
        b0, b1, a0, a1 = below[0:1], below[1:2], above[0:1], above[1:2]
        down = jnp.where(depth == 0, b1, shift(value, 1, 0))
        up = jnp.where(depth == edge - 1, a0, shift(value, -1, 0))
        down_2 = jnp.where(depth == 0, b0, jnp.where(depth == 1, b1, shift(value, 2, 0)))
        up_2 = jnp.where(depth == edge - 1, a1, jnp.where(depth == edge - 2, a0, shift(value, -2, 0)))
        total = value + TAP_NEAR * (down + up) + TAP_EDGE * (down_2 + up_2)
        out_ref[r] = jnp.where(r < own_rows, total, 0.0)

    by_rows(count, row)


SMEM = pl.BlockSpec(memory_space=pltpu.SMEM)
VMEM = pl.BlockSpec(memory_space=pltpu.VMEM)


ANY = pl.BlockSpec(memory_space=pl.ANY)


def f32(*shape):
    return jax.ShapeDtypeStruct(shape, jnp.float32)


def hbm(*shape):
    return pltpu.HBM(shape, jnp.float32)


def vmem(*shape):
    return pltpu.VMEM(shape, jnp.float32)


def local(adjoint, velocity, porosity, block_x, neighbours, owner_map):
    blocks, _, edge, plane = adjoint.shape[1:]
    devices, layers = lax.axis_size("blk"), lax.axis_size("gz")
    table = pltpu.with_memory_space_constraint(jnp.transpose(neighbours, (2, 0, 1)), pltpu.HBM)
    state, flow, design = [pltpu.with_memory_space_constraint(x[0], pltpu.HBM) for x in (adjoint, velocity, porosity)]
    rows_cap = 2 * (3 * (blocks * edge // 2) // devices)
    chunks = -(-(rows_cap + 4) // 8)
    width = devices * edge
    first_pairs = [(g, g ^ 1) for g in range(layers)]
    second_pairs = [(g, (g + 1 if g % 2 else g - 1) % layers) for g in range(layers)]
    near_shape, late_shape = [(count,) + state.shape[1:] for count in (blocks // 2, blocks - blocks // 2)]
    faces_shape = (devices, FACE_ROWS, 128)
    row_count = 16 * chunks - (8 if 0 < (rows_cap + 4) % 8 <= 4 else 0)
    post_shape = (blocks, POPS + 1, edge, plane)
    params = pltpu.CompilerParams(vmem_limit_bytes=32 * 1024 * 1024)

    def to_halo(gathered):
        first = lax.ppermute(gathered[:, FIRST : FIRST + 16], "gz", first_pairs)
        second = lax.ppermute(gathered[:, SECOND - 4 : SECOND + 12], "gz", second_pairs)
        halo = pl.pallas_call(
            functools.partial(route_kernel, devices),
            out_shape=f32(*faces_shape),
            in_specs=[VMEM] * 4,
            out_specs=VMEM,
            scratch_shapes=[vmem(devices, 16, 128)] * 3,
            compiler_params=params,
            name="route",
        )(sources, gathered, first, second)
        return lax.all_to_all(halo, "blk", 0, 0, tiled=True)

    inputs = [vmem(*state.shape), vmem(*flow.shape), vmem(*design.shape)]
    post, faces, sources = pl.pallas_call(
        functools.partial(first_kernel, blocks, devices),
        out_shape=(
            vmem(*post_shape),
            f32(*faces_shape),
            jax.ShapeDtypeStruct((devices, SOURCES, 128), jnp.int32),
        ),
        in_specs=[ANY] * 4,
        out_specs=(VMEM,) * 3,
        scratch_shapes=inputs
        + [
            vmem(blocks, 32, 128),
            pltpu.SMEM(table.shape, jnp.int32),
            pltpu.SemaphoreType.DMA((blocks,)),
            pltpu.SemaphoreType.DMA((3,)),
        ],
        compiler_params=params,
        name="collide_first",
    )(table, state, flow, design)
    halo = to_halo(lax.all_to_all(faces, "blk", 0, 0, tiled=True))
    near, late, faces = pl.pallas_call(
        functools.partial(second_kernel, blocks, devices, chunks),
        out_shape=(hbm(*near_shape), hbm(*late_shape), f32(devices, FACE_ROWS + row_count, 128)),
        in_specs=[ANY, VMEM, ANY, ANY, VMEM],
        out_specs=(ANY, ANY, VMEM),
        scratch_shapes=inputs[1:]
        + [
            vmem(*state.shape),
            vmem(*state.shape),
            vmem(blocks, 32, 128),
            vmem(4, blocks * plane // 128, edge, 128),
            pltpu.SMEM(owner_map.shape, jnp.int32),
            pltpu.SemaphoreType.DMA((blocks,)),
            pltpu.SemaphoreType.DMA((3,)),
        ],
        compiler_params=params,
        name="stream_collide",
    )(owner_map, post, flow, design, halo)
    gathered = lax.all_to_all(faces, "blk", 0, 0, tiled=True)
    halo = to_halo(gathered)
    slab_shape, ends = (rows_cap, edge, width), (rows_cap, 2, width)
    slab, first, second = pl.pallas_call(
        functools.partial(slab_kernel, blocks, devices, chunks),
        out_shape=(f32(*slab_shape), f32(*ends), f32(*ends)),
        in_specs=[SMEM, SMEM, VMEM],
        out_specs=(VMEM,) * 3,
        scratch_shapes=[vmem(chunks * 8, edge, width)],
        compiler_params=params,
        name="slab_rows",
    )(owner_map, block_x, gathered)
    first = lax.ppermute(first, "gz", first_pairs)
    second = lax.ppermute(second, "gz", second_pairs)
    smoothed = pl.pallas_call(
        functools.partial(depth_kernel, devices, layers),
        out_shape=f32(*slab_shape),
        in_specs=[SMEM, VMEM, VMEM, VMEM],
        out_specs=VMEM,
        compiler_params=params,
        name="slab_depth",
    )(owner_map, slab, first, second)
    moved = pl.pallas_call(
        functools.partial(last_kernel, blocks),
        out_shape=hbm(*state.shape),
        in_specs=[VMEM, ANY, VMEM],
        out_specs=ANY,
        scratch_shapes=[
            vmem(*late_shape),
            vmem(*state.shape),
            vmem(blocks, 32, 128),
            pltpu.SemaphoreType.DMA((2 * blocks - blocks // 2,)),
        ],
        compiler_params=params,
        name="stream_last",
    )(near, pltpu.with_memory_space_constraint(late, pltpu.HBM), halo)
    return (moved[None], smoothed[None, None])


def solution(mesh):
    placed = (
        P("gz", "blk", None, None, None),
        P("gz", "blk", None, None, None),
        P("gz", "blk", None, None),
        P("gz", None),
        P("gz", None, None),
        P(),
    )
    return jax.shard_map(
        local,
        mesh=mesh,
        in_specs=placed,
        out_specs=(P("gz", "blk", None, None, None), P("gz", "blk", None, None, None)),
        check_vma=False,
    )
```

```python
import functools

import jax
import jax.numpy as jnp
import numpy as np
from jax import lax
from jax.experimental import pallas as pl
from jax.experimental.pallas import tpu as pltpu
from jax.sharding import PartitionSpec as P

STEPS = 2
VELOCITIES = [
    (0, 0, 0),
    (1, 0, 0),
    (-1, 0, 0),
    (0, 1, 0),
    (0, -1, 0),
    (0, 0, 1),
    (0, 0, -1),
    (1, 1, 0),
    (-1, -1, 0),
    (1, -1, 0),
    (-1, 1, 0),
    (1, 0, 1),
    (-1, 0, -1),
    (1, 0, -1),
    (-1, 0, 1),
    (0, 1, 1),
    (0, -1, -1),
    (0, 1, -1),
    (0, -1, 1),
]
POPS = 19
EAST_POPS = [1, 7, 9, 11, 13]
WEST_POPS = [2, 10, 8, 12, 14]
NORTH_POPS = [7, 10, 15, 17]
SOUTH_POPS = [8, 9, 16, 18]
UPPER_POPS = [5, 11, 14, 15, 18]
LOWER_POPS = [6, 12, 13, 16, 17]
RELAX_RATE = 1.25
DRAG_RATE = 0.3
TAP_EDGE, TAP_NEAR = 1.0 / 3.0, 2.0 / 3.0

FACE_ROWS = 64
Y_ROWS, FIRST, SECOND = 24, 40, 52
SOUTH = 64
OWN_PAIRS = [0, 1, 2, 4, 5]
FREE_PAIRS = [(0, 6), (1, 3), (1, 6), (1, 7), (2, 6)]
Y_SPOTS = {3: [(0, 6), (0, 7)], 4: [(2, 6), (2, 7)]}
STREAM_ORDER = [1, 2, 7, 10, 9, 8, 11, 12, 13, 14, 0, 5, 6, 15, 16, 17, 18, 3, 4]
STREAM_GROUP = 4


SOURCES = 16


def shift(value, amount, axis=1):
    amount = amount % value.shape[axis]
    return value if amount == 0 else pltpu.roll(value, amount, axis)


def lanes(shape):
    return lax.broadcasted_iota(jnp.int32, shape, len(shape) - 1)


def collide_cells(f, u, porosity):
    total, gap = {}, {}
    for i in range(1, POPS, 2):
        total[i], gap[i] = f[i] + f[i + 1], f[i] - f[i + 1]
    ux, uy, uz = u
    mx = gap[1] + gap[7] + gap[9] + gap[11] + gap[13]
    my = gap[3] + gap[7] - gap[9] + gap[15] + gap[17]
    mz = gap[5] + gap[11] - gap[13] + gap[15] - gap[17]
    xy_sum, xz_sum, yz_sum = total[7] + total[9], total[11] + total[13], total[15] + total[17]
    xx = 2.0 * total[1] + xy_sum + xz_sum
    yy = 2.0 * total[3] + xy_sum + yz_sum
    zz = 2.0 * total[5] + xz_sum + yz_sum
    xy, xz, yz = total[7] - total[9], total[11] - total[13], total[15] - total[17]
    mass = 12.0 * f[0] + 2.0 * (total[1] + total[3] + total[5]) + (xy_sum + xz_sum + yz_sum)
    speed_sq = ux * ux + uy * uy + uz * uz
    qx = xx * ux + xy * uy + xz * uz
    qy = xy * ux + yy * uy + yz * uz
    qz = xz * ux + yz * uy + zz * uz
    sens = ux * mx + uy * my + uz * mz
    drag = DRAG_RATE * porosity
    scale = RELAX_RATE / 36.0
    quad = ux * qx + uy * qy + uz * qz
    base = scale * (mass + 1.5 * (speed_sq * mass) - 4.5 * quad) + drag * sens
    gx = (3.0 * scale) * (mx + gap[1] + 3.0 * qx - ux * mass) - drag * mx
    gy = (3.0 * scale) * (my + gap[3] + 3.0 * qy - uy * mass) - drag * my
    gz = (3.0 * scale) * (mz + gap[5] + 3.0 * qz - uz * mass) - drag * mz
    along = {1: gx, 3: gy, 5: gz, 7: gx + gy, 9: gx - gy, 11: gx + gz, 13: gx - gz, 15: gy + gz, 17: gy - gz}
    keep = 1.0 - RELAX_RATE
    post = [base + keep * f[0]]
    for i in range(1, POPS, 2):
        post.append(base + along[i] + keep * f[i])
        post.append(base - along[i] + keep * f[i + 1])
    return post, sens


def collide_block(read, velocity_ref, porosity_ref, post_ref, edge, plane):
    parts = {}
    for low in range(0, edge, 8):
        for left in range(0, plane, 128):
            zs, cells = pl.ds(low, 8), pl.ds(left, 128)
            post, sens = collide_cells(
                [read(p, zs, cells) for p in range(POPS)],
                [velocity_ref[c, zs, cells] for c in range(3)],
                porosity_ref[zs, cells],
            )
            for p in range(POPS):
                post_ref[p, zs, cells] = post[p]
            parts[low, left] = sens
    return parts


def part(ref, p, low, left):
    return ref[p, low : low + 8, left : left + 128]


def x_pair(p, depth, side):
    i = EAST_POPS.index(p) if p in EAST_POPS else WEST_POPS.index(p)
    return FREE_PAIRS[i] if (depth, side) == (1, 1) else (depth * 2 + side, OWN_PAIRS[i])


def slot_source(slot, east, west, y_face):
    source = jnp.where(slot % 2 == 0, east, west)
    return source if y_face is None else jnp.where(slot % 8 >= 6, y_face, source)


def spread(values, bases, lane):
    places = [(lane - base) % 128 for base in bases]
    for bit in (2, 1, 0):
        moved = [shift(value, 15 << bit) for value in values]
        values = [jnp.where(p & (16 << bit) != 0, m, v) for p, m, v in zip(places, moved, values)]
    return values


def gathered_lanes(values, bases, lane):
    places = [(lane - base) % 128 for base in bases]
    for bit in (0, 1, 2):
        moved = [shift(value, -(15 << bit)) for value in values]
        values = [jnp.where(p & (1 << bit) != 0, m, v) for p, m, v in zip(places, moved, values)]
    return values


def end_row(tile, left, row):
    at = tile + (6 if left else 0) + row
    return slice(at, at + 1)


def halo_row(upper, left, row):
    at = FIRST + (0 if upper else 12) + (6 if left else 0) + row
    return slice(at, at + 1)


def pack_faces(block, blocks, swapped, post_ref, lines_ref, faces_ref, edge, plane):
    def put_ends(target, row, left, cells, low, high):
        faces_ref[target, end_row(FIRST, left, row), cells] = jnp.where(swapped, high, low)
        faces_ref[target, end_row(SECOND, left, row), cells] = jnp.where(swapped, low, high)

    lane = lanes((8, 128))
    slot, group = lane % edge, lane // edge
    every = slice(0, 128)
    tiles = [None] * 3
    for depth, side in ((0, 0), (0, 1), (1, 0), (1, 1)):
        for p in EAST_POPS + WEST_POPS:
            t, pair = x_pair(p, depth, side)
            east = p in EAST_POPS
            s = 2 * pair + (0 if east else 1)
            moved = shift(part(post_ref, p, depth * 8, side * 128), s - (0 if east else 2 * edge - 1))
            tiles[t] = moved if tiles[t] is None else jnp.where(slot == s, moved, tiles[t])
    for p, beyond in ((3, block + 1), (4, block - 1)):
        if 0 <= beyond < blocks:
            for depth, (t, s) in enumerate(Y_SPOTS[p]):
                at = (p - 3) * 16 + depth * 8
                tiles[t] = jnp.where((slot == s) | (slot == s + 8), lines_ref[beyond, at : at + 8, :], tiles[t])
    for t, tile in enumerate(tiles):
        faces_ref[block, t * 8 : t * 8 + 8, :] = tile
    for left in range(0, plane, 128):
        cells = slice(left, left + 128)
        for i in range(5):
            put_ends(
                block,
                i,
                left,
                every,
                post_ref[UPPER_POPS[i], 0:1, cells],
                post_ref[LOWER_POPS[i], edge - 1 : edge, cells],
            )

    def y_tiles(pops, left, first):
        tiles = []
        for low in range(0, edge, 8):
            tile = None
            for q, p in enumerate(pops):
                moved = shift(part(post_ref, p, low, left), q * edge if first == 0 else (q + 5) * edge)
                tile = moved if tile is None else jnp.where(group == first + q, moved, tile)
            tiles.append(tile)
        return tiles

    north = y_tiles(NORTH_POPS, 0, 0)
    south = y_tiles(SOUTH_POPS, plane - 128, 4)

    def put_y(target, tiles, start):
        cells = slice(start, start + 64)
        for half in range(2):
            at = Y_ROWS + half * 8
            faces_ref[target, at : at + 8, cells] = tiles[half][:, cells]
        put_ends(target, 5, 0, cells, tiles[0][0:1, cells], tiles[1][7:8, cells])

    if block > 0:
        put_y(block - 1, north, 0)
    if block < blocks - 1:
        put_y(block + 1, south, SOUTH)


def y_lines(blocks, posts_ref, lines_ref, plane):
    lane = lanes((8, 128))
    spots = [(b, p, depth) for b in range(blocks) for p in (3, 4) for depth in (0, 1)]
    bases = [0 if p == 3 else 112 for _, p, _ in spots]
    lines = [part(posts_ref.at[b], p, depth * 8, 0 if p == 3 else plane - 128) for b, p, depth in spots]
    for (b, p, depth), line, base in zip(spots, spread(lines, bases, lane), bases):
        at = (p - 3) * 16 + depth * 8
        lines_ref[b, at : at + 8, :] = shift(line, Y_SPOTS[p][depth][1] - base)


def y_halos(blocks, halo_ref, lines_ref):
    lane = lanes((8, 128))
    spots = [(b, p, depth) for b in range(blocks) for p in (3, 4) for depth in (0, 1)]
    bases = [Y_SPOTS[p][depth][1] for _, p, depth in spots]
    lines = []
    for b, p, depth in spots:
        t = Y_SPOTS[p][depth][0]
        lines.append(halo_ref[b, t * 8 : t * 8 + 8, :])
    for (b, p, depth), line, base in zip(spots, gathered_lanes(lines, bases, lane), bases):
        at = (p - 3) * 16 + depth * 8
        lines_ref[b, at : at + 8, :] = shift(line, (112 if p == 3 else 0) - base)


def first_partner_above():
    return lax.rem(lax.axis_index("gz").astype(jnp.int32), jnp.int32(2)) == 0


def stream_pop(p, source_ref, halo_ref, y_faces, x_faces, edge):
    cx, cy, cz = VELOCITIES[p]
    lane = lanes((8, 128))
    sides, depths = (0, 1), (0, 1)
    value = {(z, c): shift(part(source_ref, p, z * 8, c * 128), -(cx + edge * cy)) for z in depths for c in sides}
    at_face = lane % edge == (edge - 1 if cx > 0 else 0)
    if cx != 0:
        arrived = {}
        for z in depths:
            for c in sides:
                spot = x_pair(p, z, c)
                if spot not in x_faces:
                    t, pair = spot
                    x_faces[spot] = shift(halo_ref[t * 8 : t * 8 + 8, :], edge - 1 - 2 * pair - edge * cy)
                arrived[z, c] = x_faces[spot]
    if cy == 0:
        if cx != 0:
            value = {at: jnp.where(at_face, arrived[at], value[at]) for at in value}
    else:
        far = 7 if cy > 0 else 0
        border = lane // edge == far
        outer = 1 if cy > 0 else 0
        if p in (3, 4):
            faces = y_faces[p]
        else:
            start = NORTH_POPS.index(p) * edge if cy > 0 else SOUTH + SOUTH_POPS.index(p) * edge
            faces = [shift(halo_ref[at : at + 8, :], far * edge - start) for at in (Y_ROWS, Y_ROWS + 8)]
        moved = {}
        for z in depths:
            inner = jnp.where(border, value[z, outer], value[z, 1 - outer])
            rim = value[z, outer]
            if cx != 0:
                inner = jnp.where(at_face, jnp.where(border, arrived[z, outer], arrived[z, 1 - outer]), inner)
                rim = jnp.where(at_face, arrived[z, outer], rim)
            moved[z, 1 - outer] = inner
            moved[z, outer] = jnp.where(border, faces[z], rim)
        value = moved
    if cz != 0:
        row = UPPER_POPS.index(p) if cz > 0 else LOWER_POPS.index(p)
        outer = 1 if cz > 0 else 0
        border = lax.broadcasted_iota(jnp.int32, (8, 128), 0) == (7 if cz > 0 else 0)
        moved = {}
        for c in sides:
            turned = [shift(value[z, c], -cz, 0) for z in depths]
            moved[1 - outer, c] = jnp.where(border, turned[outer], turned[1 - outer])
            moved[outer, c] = jnp.where(border, halo_ref[halo_row(cz > 0, c * 128, row), :], turned[outer])
        value = moved
    return value


def stream_block(source_ref, halo_ref, lines_ref, out_ref, edge):
    y_faces = {3: [lines_ref[0:8, :], lines_ref[8:16, :]], 4: [lines_ref[16:24, :], lines_ref[24:32, :]]}
    x_faces = {}
    for start in range(0, POPS, STREAM_GROUP):
        pops = STREAM_ORDER[start : start + STREAM_GROUP]
        values = [stream_pop(p, source_ref, halo_ref, y_faces, x_faces, edge) for p in pops]
        for p, value in zip(pops, values):
            for (z, c), tile in value.items():
                out_ref[p, z * 8 : z * 8 + 8, c * 128 : c * 128 + 128] = tile


def source_rows(d, row, blocks, table_ref, sources_ref, edge):
    here = d * blocks + row
    west, east, south, north, below, above = [table_ref[face, 0, here] for face in range(6)]

    def beside(slot_id, face):
        return jnp.where(slot_id < 0, -1, table_ref[face, 0, jnp.maximum(slot_id, 0)])

    lane = lanes((1, 128))
    in_north = lane < SOUTH
    near = jnp.where(in_north, north, south)
    far_east = jnp.where(in_north, beside(north, 1), beside(south, 1))
    far_west = jnp.where(in_north, beside(north, 0), beside(south, 0))
    in_east, in_west = east_west_groups(lane, edge)
    rows = [
        slot_source(lane % edge, east, west, north),
        slot_source(lane % edge, east, west, None),
        slot_source(lane % edge, east, west, south),
        jnp.where(
            in_east & (lane % edge == edge - 1),
            far_east,
            jnp.where(in_west & (lane % edge == 0), far_west, near),
        ),
    ]
    for face, own in ((5, above), (4, below)):
        rows += [own, beside(east, face), beside(west, face), beside(north, face), beside(south, face)]
    for r, slot_id in enumerate(rows):
        device = lax.shift_right_arithmetic(slot_id, jnp.int32(blocks.bit_length() - 1))
        sources_ref[d, r : r + 1, :] = jnp.broadcast_to(device, (1, 128))


def east_west_groups(lane, edge):
    group = lane // edge
    return (group == 0) | (group == 5), (group == 1) | (group == 4)


def first_kernel(
    blocks,
    devices,
    table_hbm,
    state_hbm,
    velocity_hbm,
    porosity_hbm,
    post_ref,
    faces_ref,
    sources_ref,
    state_ref,
    velocity_ref,
    porosity_ref,
    lines_ref,
    table_ref,
    sems,
    sem,
    flow_sems,
):
    edge, plane = porosity_ref.shape[1:]
    swapped = first_partner_above()
    row = jnp.minimum(lax.axis_index("blk").astype(jnp.int32), blocks - 1)

    def copy(b):
        return pltpu.make_async_copy(state_hbm.at[b], state_ref.at[b], sems.at[b])

    lookup = pltpu.make_async_copy(table_hbm, table_ref, sem.at[0])

    def flow(b):
        return (
            pltpu.make_async_copy(velocity_hbm.at[b], velocity_ref.at[b], flow_sems.at[0, b]),
            pltpu.make_async_copy(porosity_hbm.at[b], porosity_ref.at[b], flow_sems.at[1, b]),
        )

    for b in range(blocks):
        copy(b).start()
        for other in flow(b):
            other.start()
        if b == 0:
            lookup.start()
    lookup.wait()
    per = -(-devices // blocks)

    def one(b, carry):
        copy(b).wait()
        for other in flow(b):
            other.wait()
        parts = collide_block(
            lambda p, zs, cells: state_ref[b, p, zs, cells],
            velocity_ref.at[b],
            porosity_ref.at[b],
            post_ref.at[b],
            edge,
            plane,
        )
        for (low, left), sens in parts.items():
            post_ref[b, POPS, pl.ds(low, 8), pl.ds(left, 128)] = sens
        for k in range(per):
            source_rows(jnp.minimum(b * per + k, devices - 1), row, blocks, table_ref, sources_ref, edge)
        return carry

    lax.fori_loop(0, blocks, one, 0)
    y_lines(blocks, post_ref, lines_ref, plane)
    for b in range(blocks):
        pack_faces(b, blocks, swapped, post_ref.at[b], lines_ref, faces_ref, edge, plane)


def slab_start(owner_ref, slab, devices):
    start = jnp.int32(0)
    for j in range(devices):
        start = start + jnp.where(j < slab, 2 * owner_ref[j], 0)
    return start


def second_kernel(
    blocks,
    devices,
    chunks,
    owner_hbm,
    before_ref,
    velocity_hbm,
    porosity_hbm,
    halo_ref,
    near_hbm,
    late_hbm,
    faces_ref,
    velocity_ref,
    porosity_ref,
    post_ref,
    state_ref,
    lines_ref,
    turned_ref,
    owner_ref,
    sems,
    sem,
):
    edge, plane = porosity_ref.shape[1:]
    swapped = first_partner_above()
    others = [
        pltpu.make_async_copy(velocity_hbm, velocity_ref, sem.at[1]),
        pltpu.make_async_copy(porosity_hbm, porosity_ref, sem.at[2]),
        pltpu.make_async_copy(owner_hbm, owner_ref, sem.at[0]),
    ]
    for other in others:
        other.start()

    half = blocks // 2

    def result(b, out_hbm, first):
        return pltpu.make_async_copy(post_ref.at[b], out_hbm.at[b - first], sems.at[b])

    def stream(b, carry):
        stream_block(before_ref.at[b], halo_ref.at[b], lines_ref.at[b], state_ref.at[b], edge)
        return carry

    y_halos(blocks, halo_ref, lines_ref)
    lax.fori_loop(0, blocks, stream, 0)
    for other in others:
        other.wait()

    def collide(b, carry):
        parts = collide_block(
            lambda p, zs, cells: state_ref[b, p, zs, cells],
            velocity_ref.at[b],
            porosity_ref.at[b],
            post_ref.at[b],
            edge,
            plane,
        )

        @pl.when(b < half)
        def _():
            result(b, near_hbm, 0).start()

        @pl.when(b >= half)
        def _():
            result(b, late_hbm, half).start()

        for (low, left), sens in parts.items():
            sens = before_ref[b, POPS, pl.ds(low, 8), pl.ds(left, 128)] + sens
            turned_ref[0, b * (plane // 128) + left // 128, pl.ds(low, 8), :] = sens
        return carry

    lax.fori_loop(0, blocks, collide, 0)
    y_lines(blocks, post_ref, lines_ref, plane)

    for b in range(blocks):
        pack_faces(b, blocks, swapped, post_ref.at[b], lines_ref, faces_ref, edge, plane)
    held = blocks * (plane // 128)
    for c in range(held):
        for m in range(1, 4):
            for low in (0, 8):
                turned_ref[m, c, low : low + 8, :] = shift(turned_ref[0, c, low : low + 8, :], -2 * m * edge)
    lane = lanes((edge, 128))
    start = jnp.int32(0)
    for j in range(devices):
        first = lax.div(start + 6, jnp.int32(8)) - 1
        behind = start - 2 - 8 * first
        phase = lax.div(behind, jnp.int32(2))
        turned = [turned_ref[phase, jnp.clip(first + i, 0, held - 1)] for i in range(chunks + 1)]
        kept = lane < 128 - behind * edge
        for i in range(chunks):
            value = jnp.where(kept, turned[i], turned[i + 1])
            at = FACE_ROWS + 16 * i
            if at + 16 <= faces_ref.shape[1]:
                faces_ref[j, at : at + 16, :] = value
            else:
                faces_ref[j, at : at + 8, :] = jnp.where(lane[0:8] < 64, value[0:8], shift(value[8:16], 64))
        start = start + 2 * owner_ref[j]
    for b in range(blocks):
        (result(b, near_hbm, 0) if b < half else result(b, late_hbm, half)).wait()


def last_kernel(blocks, near_ref, late_hbm, halo_ref, out_hbm, late_ref, out_ref, lines_ref, sems):
    edge = late_ref.shape[2]
    half = blocks // 2

    def late(b):
        return pltpu.make_async_copy(late_hbm.at[b - half], late_ref.at[b - half], sems.at[blocks + b - half])

    def result(b):
        return pltpu.make_async_copy(out_ref.at[b], out_hbm.at[b], sems.at[b])

    for b in range(half, blocks):
        late(b).start()

    def one(b, before_ref):
        stream_block(before_ref, halo_ref.at[b], lines_ref.at[b], out_ref.at[b], edge)
        result(b).start()

    def near_one(b, carry):
        one(b, near_ref.at[b])
        return carry

    def late_one(b, carry):
        late(b).wait()
        one(b, late_ref.at[b - half])
        return carry

    y_halos(blocks, halo_ref, lines_ref)
    lax.fori_loop(0, half, near_one, 0)
    lax.fori_loop(half, blocks, late_one, 0)
    for b in range(blocks):
        result(b).wait()


def route_kernel(devices, sources_ref, faces_ref, first_ref, second_ref, halo_ref, y_ref, above_ref, below_ref):
    edge = 16
    swapped = first_partner_above()
    lane = lanes((8, 128))
    level = lax.broadcasted_iota(jnp.int32, (8, 128), 0)
    x, group = lane % edge, lane // edge
    in_east, in_west = east_west_groups(lane, edge)
    sides = (0, 128)

    def z_tiles(own, pops):
        out = list(own)
        for i, p in enumerate(pops):
            cx, cy, _ = VELOCITIES[p]
            if cx != 0:
                face = edge - 1 if cx > 0 else 0
                for c in range(2):
                    value = jnp.where(x == face, shift(own[c], cx * (edge - 1)), shift(own[c], -cx))
                    out[c] = jnp.where(level == i, value, out[c])
            if cy != 0:
                outer = 1 if cy > 0 else 0
                face = 7 if cy > 0 else 0
                start = NORTH_POPS.index(p) * edge if cy > 0 else SOUTH + SOUTH_POPS.index(p) * edge
                turned = [shift(side, -cy * edge) for side in own]
                arrived = jnp.broadcast_to(shift(own[0][5:6], face * edge - start), (8, 128))
                inner = jnp.where(group == face, turned[outer], turned[1 - outer])
                rim = jnp.where(group == face, arrived, turned[outer])
                out[1 - outer] = jnp.where(level == i, inner, out[1 - outer])
                out[outer] = jnp.where(level == i, rim, out[outer])
        return out

    def prepare(e, carry):
        first = [first_ref[e, at : at + 8, :] for at in (0, 6)]
        second = [second_ref[e, 4:12, :], shift(second_ref[e, 8:16, :], -2, 0)]
        above = [jnp.where(swapped, a, b) for a, b in zip(first, second)]
        below = [jnp.where(swapped, b, a) for a, b in zip(first, second)]
        for own, pops, ref in ((above, UPPER_POPS, above_ref), (below, LOWER_POPS, below_ref)):
            for at, tile in zip((0, 8), z_tiles(own, pops)):
                ref[e, at : at + 8, :] = tile
        for at in (0, 8):
            own = faces_ref[e, Y_ROWS + at : Y_ROWS + at + 8, :]
            east = jnp.where(x == edge - 1, shift(own, edge - 1), shift(own, -1))
            west = jnp.where(x == 0, shift(own, 1 - edge), shift(own, 1))
            y_ref[e, at : at + 8, :] = jnp.where(in_east, east, jnp.where(in_west, west, own))
        return carry

    lax.fori_loop(0, devices, prepare, 0, unroll=2)

    def pick(index, tiles_of):
        total = None
        for e in range(devices):
            hit = index == e
            tiles = tiles_of(e)
            total = [jnp.where(hit, t, 0.0 if total is None else total[k]) for k, t in enumerate(tiles)]
        return total

    def one(d, carry):
        row = [jnp.broadcast_to(sources_ref[d, r : r + 1, :], (8, 128)) for r in range(14)]
        for at, index in zip((0, 8, 16), row):
            (halo_ref[d, at : at + 8, :],) = pick(index, lambda e: [faces_ref[e, at : at + 8, :]])
        for at, tile in zip((0, 8), pick(row[3], lambda e: [y_ref[e, at : at + 8, :] for at in (0, 8)])):
            halo_ref[d, Y_ROWS + at : Y_ROWS + at + 8, :] = tile
        for pops, base, ref, upper in ((UPPER_POPS, 4, above_ref, True), (LOWER_POPS, 9, below_ref, False)):
            index = [row[base]] * 2
            for i, p in enumerate(pops):
                cx, cy, _ = VELOCITIES[p]
                if cx != 0:
                    here = (level == i) & (x == (edge - 1 if cx > 0 else 0))
                    index = [jnp.where(here, row[base + (1 if cx > 0 else 2)], side) for side in index]
                if cy != 0:
                    outer, face = (1, 7) if cy > 0 else (0, 0)
                    here = (level == i) & (group == face)
                    index[outer] = jnp.where(here, row[base + (3 if cy > 0 else 4)], index[outer])
            for left, at, side in zip(sides, (0, 8), index):
                (tile,) = pick(side, lambda e: [ref[e, at : at + 8, :]])
                top = halo_row(upper, left, 0).start
                halo_ref[d, top : top + 6, :] = tile[0:6]
        return carry

    lax.fori_loop(0, devices, one, 0, unroll=2)


def slab_kernel(
    blocks, devices, chunks, owner_ref, column_ref, rows_ref, out_ref, first_ref, second_ref, field_ref
):
    slab = lax.axis_index("blk").astype(jnp.int32)
    swapped = first_partner_above()
    count, edge, width = out_ref.shape
    start = slab_start(owner_ref, slab, devices)
    group = lanes((edge, width)) // edge
    lane = lanes((edge, width))
    height = blocks * edge

    def chunk(i):
        top = start - 2 + 8 * i
        tiles = [jnp.zeros((edge, width), jnp.float32) for _ in range(8)]
        at = FACE_ROWS + 16 * i
        if at + 16 <= rows_ref.shape[1]:
            values = [rows_ref[e, at : at + 16, :] for e in range(devices)]
        else:
            halves = [rows_ref[e, at : at + 8, :] for e in range(devices)]
            values = [jnp.concatenate([half, shift(half, 64)], axis=0) for half in halves]
        for r in range(0, 8, 2):
            inside = (top + r >= 0) & (top + r < height)
            block_row = lax.div(jnp.clip(top + r, 0, height - 1), jnp.int32(edge))
            for e in range(devices):
                column = column_ref[0, e * blocks + block_row]
                hit = group == jnp.where(inside, column, -1)
                for k in range(r, r + 2):
                    part = pltpu.roll(values[e], lax.rem(column + (8 - k), jnp.int32(8)) * edge, 1)
                    if width > 128:
                        part = jnp.concatenate([part] * (width // 128), axis=1)
                    tiles[k] = jnp.where(hit, part, tiles[k])
        for r in range(8):
            field_ref[i * 8 + r] = tiles[r]

    for i in range(chunks):
        chunk(i)

    def row(r):
        at = r
        mixed = TAP_EDGE * (field_ref[at] + field_ref[at + 4]) + (
            TAP_NEAR * (field_ref[at + 1] + field_ref[at + 3]) + field_ref[at + 2]
        )
        value = mixed
        for step, tap in ((1, TAP_NEAR), (2, TAP_EDGE)):
            left = jnp.where(lane >= step, shift(mixed, step), 0.0)
            right = jnp.where(lane < width - step, shift(mixed, -step), 0.0)
            value = value + tap * (left + right)
        out_ref[r] = value
        low, high = value[0:2], value[edge - 2 : edge]
        first_ref[r] = jnp.where(swapped, high, low)
        second_ref[r] = jnp.where(swapped, low, high)

    by_rows(count, row)


def by_rows(count, body):
    step = 8 if count % 8 == 0 else 4 if count % 4 == 0 else 2

    def several(i, carry):
        for k in range(step):
            body(i * step + k)
        return carry

    lax.fori_loop(0, count // step, several, 0)


def depth_kernel(devices, layers, owner_ref, rows_ref, first_ref, second_ref, out_ref):
    count, edge, width = out_ref.shape
    slab, layer = lax.axis_index("blk").astype(jnp.int32), lax.axis_index("gz").astype(jnp.int32)
    own_rows = jnp.int32(0)
    for j in range(devices):
        own_rows = jnp.where(slab == j, 2 * owner_ref[j], own_rows)
    swapped = first_partner_above()
    depth = lax.broadcasted_iota(jnp.int32, (edge, width), 0)

    def row(r):
        value = rows_ref[r]
        first, second = first_ref[r], second_ref[r]
        below = jnp.where(layer > 0, jnp.where(swapped, second, first), 0.0)
        above = jnp.where(layer < layers - 1, jnp.where(swapped, first, second), 0.0)
        b0, b1, a0, a1 = below[0:1], below[1:2], above[0:1], above[1:2]
        down = jnp.where(depth == 0, b1, shift(value, 1, 0))
        up = jnp.where(depth == edge - 1, a0, shift(value, -1, 0))
        down_2 = jnp.where(depth == 0, b0, jnp.where(depth == 1, b1, shift(value, 2, 0)))
        up_2 = jnp.where(depth == edge - 1, a1, jnp.where(depth == edge - 2, a0, shift(value, -2, 0)))
        total = value + TAP_NEAR * (down + up) + TAP_EDGE * (down_2 + up_2)
        out_ref[r] = jnp.where(r < own_rows, total, 0.0)

    by_rows(count, row)


SMEM = pl.BlockSpec(memory_space=pltpu.SMEM)
VMEM = pl.BlockSpec(memory_space=pltpu.VMEM)


ANY = pl.BlockSpec(memory_space=pl.ANY)


def f32(*shape):
    return jax.ShapeDtypeStruct(shape, jnp.float32)


def hbm(*shape):
    return pltpu.HBM(shape, jnp.float32)


def vmem(*shape):
    return pltpu.VMEM(shape, jnp.float32)


def local(adjoint, velocity, porosity, block_x, neighbours, owner_map):
    blocks, _, edge, plane = adjoint.shape[1:]
    devices, layers = lax.axis_size("blk"), lax.axis_size("gz")
    table = pltpu.with_memory_space_constraint(jnp.transpose(neighbours, (2, 0, 1)), pltpu.HBM)
    state, flow, design = [pltpu.with_memory_space_constraint(x[0], pltpu.HBM) for x in (adjoint, velocity, porosity)]
    rows_cap = 2 * (3 * (blocks * edge // 2) // devices)
    chunks = -(-(rows_cap + 4) // 8)
    width = devices * edge
    first_pairs = [(g, g ^ 1) for g in range(layers)]
    second_pairs = [(g, (g + 1 if g % 2 else g - 1) % layers) for g in range(layers)]
    near_shape, late_shape = [(count,) + state.shape[1:] for count in (blocks // 2, blocks - blocks // 2)]
    faces_shape = (devices, FACE_ROWS, 128)
    row_count = 16 * chunks - (8 if 0 < (rows_cap + 4) % 8 <= 4 else 0)
    post_shape = (blocks, POPS + 1, edge, plane)
    params = pltpu.CompilerParams(vmem_limit_bytes=32 * 1024 * 1024)

    def to_halo(gathered):
        first = lax.ppermute(gathered[:, FIRST : FIRST + 16], "gz", first_pairs)
        second = lax.ppermute(gathered[:, SECOND - 4 : SECOND + 12], "gz", second_pairs)
        halo = pl.pallas_call(
            functools.partial(route_kernel, devices),
            out_shape=f32(*faces_shape),
            in_specs=[VMEM] * 4,
            out_specs=VMEM,
            scratch_shapes=[vmem(devices, 16, 128)] * 3,
            compiler_params=params,
            name="route",
        )(sources, gathered, first, second)
        return lax.all_to_all(halo, "blk", 0, 0, tiled=True)

    inputs = [vmem(*state.shape), vmem(*flow.shape), vmem(*design.shape)]
    post, faces, sources = pl.pallas_call(
        functools.partial(first_kernel, blocks, devices),
        out_shape=(
            vmem(*post_shape),
            f32(*faces_shape),
            jax.ShapeDtypeStruct((devices, SOURCES, 128), jnp.int32),
        ),
        in_specs=[ANY] * 4,
        out_specs=(VMEM,) * 3,
        scratch_shapes=inputs
        + [
            vmem(blocks, 32, 128),
            pltpu.SMEM(table.shape, jnp.int32),
            pltpu.SemaphoreType.DMA((blocks,)),
            pltpu.SemaphoreType.DMA((1,)),
            pltpu.SemaphoreType.DMA((2, blocks)),
        ],
        compiler_params=params,
        name="collide_first",
    )(table, state, flow, design)
    halo = to_halo(lax.all_to_all(faces, "blk", 0, 0, tiled=True))
    near, late, faces = pl.pallas_call(
        functools.partial(second_kernel, blocks, devices, chunks),
        out_shape=(hbm(*near_shape), hbm(*late_shape), f32(devices, FACE_ROWS + row_count, 128)),
        in_specs=[ANY, VMEM, ANY, ANY, VMEM],
        out_specs=(ANY, ANY, VMEM),
        scratch_shapes=inputs[1:]
        + [
            vmem(*state.shape),
            vmem(*state.shape),
            vmem(blocks, 32, 128),
            vmem(4, blocks * plane // 128, edge, 128),
            pltpu.SMEM(owner_map.shape, jnp.int32),
            pltpu.SemaphoreType.DMA((blocks,)),
            pltpu.SemaphoreType.DMA((3,)),
        ],
        compiler_params=params,
        name="stream_collide",
    )(owner_map, post, flow, design, halo)
    gathered = lax.all_to_all(faces, "blk", 0, 0, tiled=True)
    halo = to_halo(gathered)
    slab_shape, ends = (rows_cap, edge, width), (rows_cap, 2, width)
    slab, first, second = pl.pallas_call(
        functools.partial(slab_kernel, blocks, devices, chunks),
        out_shape=(f32(*slab_shape), f32(*ends), f32(*ends)),
        in_specs=[SMEM, SMEM, VMEM],
        out_specs=(VMEM,) * 3,
        scratch_shapes=[vmem(chunks * 8, edge, width)],
        compiler_params=params,
        name="slab_rows",
    )(owner_map, block_x, gathered)
    first = lax.ppermute(first, "gz", first_pairs)
    second = lax.ppermute(second, "gz", second_pairs)
    smoothed = pl.pallas_call(
        functools.partial(depth_kernel, devices, layers),
        out_shape=f32(*slab_shape),
        in_specs=[SMEM, VMEM, VMEM, VMEM],
        out_specs=VMEM,
        compiler_params=params,
        name="slab_depth",
    )(owner_map, slab, first, second)
    moved = pl.pallas_call(
        functools.partial(last_kernel, blocks),
        out_shape=hbm(*state.shape),
        in_specs=[VMEM, ANY, VMEM],
        out_specs=ANY,
        scratch_shapes=[
            vmem(*late_shape),
            vmem(*state.shape),
            vmem(blocks, 32, 128),
            pltpu.SemaphoreType.DMA((2 * blocks - blocks // 2,)),
        ],
        compiler_params=params,
        name="stream_last",
    )(near, pltpu.with_memory_space_constraint(late, pltpu.HBM), halo)
    return (moved[None], smoothed[None, None])


def solution(mesh):
    placed = (
        P("gz", "blk", None, None, None),
        P("gz", "blk", None, None, None),
        P("gz", "blk", None, None),
        P("gz", None),
        P("gz", None, None),
        P(),
    )
    return jax.shard_map(
        local,
        mesh=mesh,
        in_specs=placed,
        out_specs=(P("gz", "blk", None, None, None), P("gz", "blk", None, None, None)),
        check_vma=False,
    )
```

```python
import functools

import jax
import jax.numpy as jnp
import numpy as np
from jax import lax
from jax.experimental import pallas as pl
from jax.experimental.pallas import tpu as pltpu
from jax.sharding import PartitionSpec as P

STEPS = 2
VELOCITIES = [
    (0, 0, 0),
    (1, 0, 0),
    (-1, 0, 0),
    (0, 1, 0),
    (0, -1, 0),
    (0, 0, 1),
    (0, 0, -1),
    (1, 1, 0),
    (-1, -1, 0),
    (1, -1, 0),
    (-1, 1, 0),
    (1, 0, 1),
    (-1, 0, -1),
    (1, 0, -1),
    (-1, 0, 1),
    (0, 1, 1),
    (0, -1, -1),
    (0, 1, -1),
    (0, -1, 1),
]
POPS = 19
EAST_POPS = [1, 7, 9, 11, 13]
WEST_POPS = [2, 10, 8, 12, 14]
NORTH_POPS = [7, 10, 15, 17]
SOUTH_POPS = [8, 9, 16, 18]
UPPER_POPS = [5, 11, 14, 15, 18]
LOWER_POPS = [6, 12, 13, 16, 17]
RELAX_RATE = 1.25
DRAG_RATE = 0.3
TAP_EDGE, TAP_NEAR = 1.0 / 3.0, 2.0 / 3.0

FACE_ROWS = 64
Y_ROWS, FIRST, SECOND = 24, 40, 52
SOUTH = 64
OWN_PAIRS = [0, 1, 2, 4, 5]
FREE_PAIRS = [(0, 6), (1, 3), (1, 6), (1, 7), (2, 6)]
Y_SPOTS = {3: [(0, 6), (0, 7)], 4: [(2, 6), (2, 7)]}
STREAM_ORDER = [1, 2, 7, 10, 9, 8, 11, 12, 13, 14, 0, 5, 6, 15, 16, 17, 18, 3, 4]
STREAM_GROUP = 4


SOURCES = 16


def shift(value, amount, axis=1):
    amount = amount % value.shape[axis]
    return value if amount == 0 else pltpu.roll(value, amount, axis)


def lanes(shape):
    return lax.broadcasted_iota(jnp.int32, shape, len(shape) - 1)


def collide_cells(f, u, porosity):
    total, gap = {}, {}
    for i in range(1, POPS, 2):
        total[i], gap[i] = f[i] + f[i + 1], f[i] - f[i + 1]
    ux, uy, uz = u
    mx = gap[1] + gap[7] + gap[9] + gap[11] + gap[13]
    my = gap[3] + gap[7] - gap[9] + gap[15] + gap[17]
    mz = gap[5] + gap[11] - gap[13] + gap[15] - gap[17]
    xy_sum, xz_sum, yz_sum = total[7] + total[9], total[11] + total[13], total[15] + total[17]
    xx = 2.0 * total[1] + xy_sum + xz_sum
    yy = 2.0 * total[3] + xy_sum + yz_sum
    zz = 2.0 * total[5] + xz_sum + yz_sum
    xy, xz, yz = total[7] - total[9], total[11] - total[13], total[15] - total[17]
    mass = 12.0 * f[0] + 2.0 * (total[1] + total[3] + total[5]) + (xy_sum + xz_sum + yz_sum)
    speed_sq = ux * ux + uy * uy + uz * uz
    qx = xx * ux + xy * uy + xz * uz
    qy = xy * ux + yy * uy + yz * uz
    qz = xz * ux + yz * uy + zz * uz
    sens = ux * mx + uy * my + uz * mz
    drag = DRAG_RATE * porosity
    scale = RELAX_RATE / 36.0
    quad = ux * qx + uy * qy + uz * qz
    base = scale * (mass + 1.5 * (speed_sq * mass) - 4.5 * quad) + drag * sens
    gx = (3.0 * scale) * (mx + gap[1] + 3.0 * qx - ux * mass) - drag * mx
    gy = (3.0 * scale) * (my + gap[3] + 3.0 * qy - uy * mass) - drag * my
    gz = (3.0 * scale) * (mz + gap[5] + 3.0 * qz - uz * mass) - drag * mz
    along = {1: gx, 3: gy, 5: gz, 7: gx + gy, 9: gx - gy, 11: gx + gz, 13: gx - gz, 15: gy + gz, 17: gy - gz}
    keep = 1.0 - RELAX_RATE
    post = [base + keep * f[0]]
    for i in range(1, POPS, 2):
        post.append(base + along[i] + keep * f[i])
        post.append(base - along[i] + keep * f[i + 1])
    return post, sens


def collide_block(read, velocity_ref, porosity_ref, post_ref, edge, plane):
    parts = {}
    for low in range(0, edge, 8):
        for left in range(0, plane, 128):
            zs, cells = pl.ds(low, 8), pl.ds(left, 128)
            post, sens = collide_cells(
                [read(p, zs, cells) for p in range(POPS)],
                [velocity_ref[c, zs, cells] for c in range(3)],
                porosity_ref[zs, cells],
            )
            for p in range(POPS):
                post_ref[p, zs, cells] = post[p]
            parts[low, left] = sens
    return parts


def part(ref, p, low, left):
    return ref[p, low : low + 8, left : left + 128]


def x_pair(p, depth, side):
    i = EAST_POPS.index(p) if p in EAST_POPS else WEST_POPS.index(p)
    return FREE_PAIRS[i] if (depth, side) == (1, 1) else (depth * 2 + side, OWN_PAIRS[i])


def slot_source(slot, east, west, y_face):
    source = jnp.where(slot % 2 == 0, east, west)
    return source if y_face is None else jnp.where(slot % 8 >= 6, y_face, source)


def spread(values, bases, lane):
    places = [(lane - base) % 128 for base in bases]
    for bit in (2, 1, 0):
        moved = [shift(value, 15 << bit) for value in values]
        values = [jnp.where(p & (16 << bit) != 0, m, v) for p, m, v in zip(places, moved, values)]
    return values


def gathered_lanes(values, bases, lane):
    places = [(lane - base) % 128 for base in bases]
    for bit in (0, 1, 2):
        moved = [shift(value, -(15 << bit)) for value in values]
        values = [jnp.where(p & (1 << bit) != 0, m, v) for p, m, v in zip(places, moved, values)]
    return values


def end_row(tile, left, row):
    at = tile + (6 if left else 0) + row
    return slice(at, at + 1)


def halo_row(upper, left, row):
    at = FIRST + (0 if upper else 12) + (6 if left else 0) + row
    return slice(at, at + 1)


def pack_faces(block, blocks, swapped, post_ref, lines_ref, faces_ref, edge, plane):
    def put_ends(target, row, left, cells, low, high):
        faces_ref[target, end_row(FIRST, left, row), cells] = jnp.where(swapped, high, low)
        faces_ref[target, end_row(SECOND, left, row), cells] = jnp.where(swapped, low, high)

    lane = lanes((8, 128))
    slot, group = lane % edge, lane // edge
    every = slice(0, 128)
    tiles = [None] * 3
    for depth, side in ((0, 0), (0, 1), (1, 0), (1, 1)):
        for p in EAST_POPS + WEST_POPS:
            t, pair = x_pair(p, depth, side)
            east = p in EAST_POPS
            s = 2 * pair + (0 if east else 1)
            moved = shift(part(post_ref, p, depth * 8, side * 128), s - (0 if east else 2 * edge - 1))
            tiles[t] = moved if tiles[t] is None else jnp.where(slot == s, moved, tiles[t])
    for p, beyond in ((3, block + 1), (4, block - 1)):
        if 0 <= beyond < blocks:
            for depth, (t, s) in enumerate(Y_SPOTS[p]):
                at = (p - 3) * 16 + depth * 8
                tiles[t] = jnp.where((slot == s) | (slot == s + 8), lines_ref[beyond, at : at + 8, :], tiles[t])
    for t, tile in enumerate(tiles):
        faces_ref[block, t * 8 : t * 8 + 8, :] = tile
    for left in range(0, plane, 128):
        cells = slice(left, left + 128)
        for i in range(5):
            put_ends(
                block,
                i,
                left,
                every,
                post_ref[UPPER_POPS[i], 0:1, cells],
                post_ref[LOWER_POPS[i], edge - 1 : edge, cells],
            )

    def y_tiles(pops, left, first):
        tiles = []
        for low in range(0, edge, 8):
            tile = None
            for q, p in enumerate(pops):
                moved = shift(part(post_ref, p, low, left), q * edge if first == 0 else (q + 5) * edge)
                tile = moved if tile is None else jnp.where(group == first + q, moved, tile)
            tiles.append(tile)
        return tiles

    north = y_tiles(NORTH_POPS, 0, 0)
    south = y_tiles(SOUTH_POPS, plane - 128, 4)

    def put_y(target, tiles, start):
        cells = slice(start, start + 64)
        for half in range(2):
            at = Y_ROWS + half * 8
            faces_ref[target, at : at + 8, cells] = tiles[half][:, cells]
        put_ends(target, 5, 0, cells, tiles[0][0:1, cells], tiles[1][7:8, cells])

    if block > 0:
        put_y(block - 1, north, 0)
    if block < blocks - 1:
        put_y(block + 1, south, SOUTH)


def y_lines(blocks, posts_ref, lines_ref, plane):
    lane = lanes((8, 128))
    spots = [(b, p, depth) for b in range(blocks) for p in (3, 4) for depth in (0, 1)]
    bases = [0 if p == 3 else 112 for _, p, _ in spots]
    lines = [part(posts_ref.at[b], p, depth * 8, 0 if p == 3 else plane - 128) for b, p, depth in spots]
    for (b, p, depth), line, base in zip(spots, spread(lines, bases, lane), bases):
        at = (p - 3) * 16 + depth * 8
        lines_ref[b, at : at + 8, :] = shift(line, Y_SPOTS[p][depth][1] - base)


def y_halos(blocks, halo_ref, lines_ref):
    lane = lanes((8, 128))
    spots = [(b, p, depth) for b in range(blocks) for p in (3, 4) for depth in (0, 1)]
    bases = [Y_SPOTS[p][depth][1] for _, p, depth in spots]
    lines = []
    for b, p, depth in spots:
        t = Y_SPOTS[p][depth][0]
        lines.append(halo_ref[b, t * 8 : t * 8 + 8, :])
    for (b, p, depth), line, base in zip(spots, gathered_lanes(lines, bases, lane), bases):
        at = (p - 3) * 16 + depth * 8
        lines_ref[b, at : at + 8, :] = shift(line, (112 if p == 3 else 0) - base)


def first_partner_above():
    return lax.rem(lax.axis_index("gz").astype(jnp.int32), jnp.int32(2)) == 0


def stream_pop(p, source_ref, halo_ref, y_faces, x_faces, edge):
    cx, cy, cz = VELOCITIES[p]
    lane = lanes((8, 128))
    sides, depths = (0, 1), (0, 1)
    value = {(z, c): shift(part(source_ref, p, z * 8, c * 128), -(cx + edge * cy)) for z in depths for c in sides}
    at_face = lane % edge == (edge - 1 if cx > 0 else 0)
    if cx != 0:
        arrived = {}
        for z in depths:
            for c in sides:
                spot = x_pair(p, z, c)
                if spot not in x_faces:
                    t, pair = spot
                    x_faces[spot] = shift(halo_ref[t * 8 : t * 8 + 8, :], edge - 1 - 2 * pair - edge * cy)
                arrived[z, c] = x_faces[spot]
    if cy == 0:
        if cx != 0:
            value = {at: jnp.where(at_face, arrived[at], value[at]) for at in value}
    else:
        far = 7 if cy > 0 else 0
        border = lane // edge == far
        outer = 1 if cy > 0 else 0
        if p in (3, 4):
            faces = y_faces[p]
        else:
            start = NORTH_POPS.index(p) * edge if cy > 0 else SOUTH + SOUTH_POPS.index(p) * edge
            faces = [shift(halo_ref[at : at + 8, :], far * edge - start) for at in (Y_ROWS, Y_ROWS + 8)]
        moved = {}
        for z in depths:
            inner = jnp.where(border, value[z, outer], value[z, 1 - outer])
            rim = value[z, outer]
            if cx != 0:
                inner = jnp.where(at_face, jnp.where(border, arrived[z, outer], arrived[z, 1 - outer]), inner)
                rim = jnp.where(at_face, arrived[z, outer], rim)
            moved[z, 1 - outer] = inner
            moved[z, outer] = jnp.where(border, faces[z], rim)
        value = moved
    if cz != 0:
        row = UPPER_POPS.index(p) if cz > 0 else LOWER_POPS.index(p)
        outer = 1 if cz > 0 else 0
        border = lax.broadcasted_iota(jnp.int32, (8, 128), 0) == (7 if cz > 0 else 0)
        moved = {}
        for c in sides:
            turned = [shift(value[z, c], -cz, 0) for z in depths]
            moved[1 - outer, c] = jnp.where(border, turned[outer], turned[1 - outer])
            moved[outer, c] = jnp.where(border, halo_ref[halo_row(cz > 0, c * 128, row), :], turned[outer])
        value = moved
    return value


def stream_block(source_ref, halo_ref, lines_ref, out_ref, edge):
    y_faces = {3: [lines_ref[0:8, :], lines_ref[8:16, :]], 4: [lines_ref[16:24, :], lines_ref[24:32, :]]}
    x_faces = {}
    for start in range(0, POPS, STREAM_GROUP):
        pops = STREAM_ORDER[start : start + STREAM_GROUP]
        values = [stream_pop(p, source_ref, halo_ref, y_faces, x_faces, edge) for p in pops]
        for p, value in zip(pops, values):
            for (z, c), tile in value.items():
                out_ref[p, z * 8 : z * 8 + 8, c * 128 : c * 128 + 128] = tile


def source_rows(d, row, blocks, table_ref, sources_ref, edge):
    here = d * blocks + row
    west, east, south, north, below, above = [table_ref[face, 0, here] for face in range(6)]

    def beside(slot_id, face):
        return jnp.where(slot_id < 0, -1, table_ref[face, 0, jnp.maximum(slot_id, 0)])

    lane = lanes((1, 128))
    in_north = lane < SOUTH
    near = jnp.where(in_north, north, south)
    far_east = jnp.where(in_north, beside(north, 1), beside(south, 1))
    far_west = jnp.where(in_north, beside(north, 0), beside(south, 0))
    in_east, in_west = east_west_groups(lane, edge)
    rows = [
        slot_source(lane % edge, east, west, north),
        slot_source(lane % edge, east, west, None),
        slot_source(lane % edge, east, west, south),
        jnp.where(
            in_east & (lane % edge == edge - 1),
            far_east,
            jnp.where(in_west & (lane % edge == 0), far_west, near),
        ),
    ]
    for face, own in ((5, above), (4, below)):
        rows += [own, beside(east, face), beside(west, face), beside(north, face), beside(south, face)]
    for r, slot_id in enumerate(rows):
        device = lax.shift_right_arithmetic(slot_id, jnp.int32(blocks.bit_length() - 1))
        sources_ref[d, r : r + 1, :] = jnp.broadcast_to(device, (1, 128))


def east_west_groups(lane, edge):
    group = lane // edge
    return (group == 0) | (group == 5), (group == 1) | (group == 4)


def first_kernel(
    blocks,
    devices,
    table_hbm,
    state_hbm,
    velocity_hbm,
    porosity_hbm,
    post_ref,
    faces_ref,
    sources_ref,
    state_ref,
    velocity_ref,
    porosity_ref,
    lines_ref,
    table_ref,
    sems,
    sem,
    flow_sems,
):
    edge, plane = porosity_ref.shape[1:]
    swapped = first_partner_above()
    row = jnp.minimum(lax.axis_index("blk").astype(jnp.int32), blocks - 1)

    def copy(b):
        return pltpu.make_async_copy(state_hbm.at[b], state_ref.at[b], sems.at[b])

    lookup = pltpu.make_async_copy(table_hbm, table_ref, sem.at[0])

    def flow(b):
        return (
            pltpu.make_async_copy(velocity_hbm.at[b], velocity_ref.at[b], flow_sems.at[0, b]),
            pltpu.make_async_copy(porosity_hbm.at[b], porosity_ref.at[b], flow_sems.at[1, b]),
        )

    for b in range(blocks):
        copy(b).start()
        for other in flow(b):
            other.start()
        if b == 0:
            lookup.start()
    lookup.wait()
    per = -(-devices // blocks)

    def one(b, carry):
        copy(b).wait()
        for other in flow(b):
            other.wait()
        parts = collide_block(
            lambda p, zs, cells: state_ref[b, p, zs, cells],
            velocity_ref.at[b],
            porosity_ref.at[b],
            post_ref.at[b],
            edge,
            plane,
        )
        for (low, left), sens in parts.items():
            post_ref[b, POPS, pl.ds(low, 8), pl.ds(left, 128)] = sens
        for k in range(per):
            source_rows(jnp.minimum(b * per + k, devices - 1), row, blocks, table_ref, sources_ref, edge)
        return carry

    lax.fori_loop(0, blocks, one, 0)
    y_lines(blocks, post_ref, lines_ref, plane)
    for b in range(blocks):
        pack_faces(b, blocks, swapped, post_ref.at[b], lines_ref, faces_ref, edge, plane)


def slab_start(owner_ref, slab, devices):
    start = jnp.int32(0)
    for j in range(devices):
        start = start + jnp.where(j < slab, 2 * owner_ref[j], 0)
    return start


def second_kernel(
    blocks,
    devices,
    chunks,
    owner_hbm,
    before_ref,
    velocity_hbm,
    porosity_hbm,
    halo_ref,
    near_hbm,
    late_hbm,
    faces_ref,
    velocity_ref,
    porosity_ref,
    post_ref,
    state_ref,
    lines_ref,
    turned_ref,
    owner_ref,
    sems,
    sem,
):
    edge, plane = porosity_ref.shape[1:]
    swapped = first_partner_above()
    others = [
        pltpu.make_async_copy(velocity_hbm, velocity_ref, sem.at[1]),
        pltpu.make_async_copy(porosity_hbm, porosity_ref, sem.at[2]),
        pltpu.make_async_copy(owner_hbm, owner_ref, sem.at[0]),
    ]
    for other in others:
        other.start()

    half = blocks // 2

    def result(b, out_hbm, first):
        return pltpu.make_async_copy(post_ref.at[b], out_hbm.at[b - first], sems.at[b])

    def stream(b, carry):
        stream_block(before_ref.at[b], halo_ref.at[b], lines_ref.at[b], state_ref.at[b], edge)
        return carry

    y_halos(blocks, halo_ref, lines_ref)
    lax.fori_loop(0, blocks, stream, 0)
    for other in others:
        other.wait()

    def collide(b, carry):
        parts = collide_block(
            lambda p, zs, cells: state_ref[b, p, zs, cells],
            velocity_ref.at[b],
            porosity_ref.at[b],
            post_ref.at[b],
            edge,
            plane,
        )

        @pl.when(b < half)
        def _():
            result(b, near_hbm, 0).start()

        @pl.when(b >= half)
        def _():
            result(b, late_hbm, half).start()

        for (low, left), sens in parts.items():
            sens = before_ref[b, POPS, pl.ds(low, 8), pl.ds(left, 128)] + sens
            turned_ref[0, b * (plane // 128) + left // 128, pl.ds(low, 8), :] = sens
        return carry

    lax.fori_loop(0, blocks, collide, 0)
    y_lines(blocks, post_ref, lines_ref, plane)

    for b in range(blocks):
        pack_faces(b, blocks, swapped, post_ref.at[b], lines_ref, faces_ref, edge, plane)
    held = blocks * (plane // 128)
    for c in range(held):
        for m in range(1, 4):
            for low in (0, 8):
                turned_ref[m, c, low : low + 8, :] = shift(turned_ref[0, c, low : low + 8, :], -2 * m * edge)
    lane = lanes((edge, 128))
    start = jnp.int32(0)
    for j in range(devices):
        first = lax.div(start + 6, jnp.int32(8)) - 1
        behind = start - 2 - 8 * first
        phase = lax.div(behind, jnp.int32(2))
        turned = [turned_ref[phase, jnp.clip(first + i, 0, held - 1)] for i in range(chunks + 1)]
        kept = lane < 128 - behind * edge
        for i in range(chunks):
            value = jnp.where(kept, turned[i], turned[i + 1])
            at = FACE_ROWS + 16 * i
            if at + 16 <= faces_ref.shape[1]:
                faces_ref[j, at : at + 16, :] = value
            else:
                faces_ref[j, at : at + 8, :] = jnp.where(lane[0:8] < 64, value[0:8], shift(value[8:16], 64))
        start = start + 2 * owner_ref[j]
    for b in range(blocks):
        (result(b, near_hbm, 0) if b < half else result(b, late_hbm, half)).wait()


def last_kernel(blocks, near_ref, late_hbm, halo_ref, out_hbm, late_ref, out_ref, lines_ref, sems):
    edge = late_ref.shape[2]
    half = blocks // 2

    def late(b):
        return pltpu.make_async_copy(late_hbm.at[b - half], late_ref.at[b - half], sems.at[blocks + b - half])

    def result(b):
        return pltpu.make_async_copy(out_ref.at[b], out_hbm.at[b], sems.at[b])

    for b in range(half, blocks):
        late(b).start()

    def one(b, before_ref):
        stream_block(before_ref, halo_ref.at[b], lines_ref.at[b], out_ref.at[b], edge)
        result(b).start()

    def near_one(b, carry):
        one(b, near_ref.at[b])
        return carry

    def late_one(b, carry):
        late(b).wait()
        one(b, late_ref.at[b - half])
        return carry

    y_halos(blocks, halo_ref, lines_ref)
    lax.fori_loop(0, half, near_one, 0)
    lax.fori_loop(half, blocks, late_one, 0)
    for b in range(blocks):
        result(b).wait()


def route_kernel(devices, sources_ref, faces_ref, first_ref, second_ref, halo_ref, y_ref, above_ref, below_ref):
    edge = 16
    swapped = first_partner_above()
    lane = lanes((8, 128))
    level = lax.broadcasted_iota(jnp.int32, (8, 128), 0)
    x, group = lane % edge, lane // edge
    in_east, in_west = east_west_groups(lane, edge)
    sides = (0, 128)

    def z_tiles(own, pops):
        out = list(own)
        for i, p in enumerate(pops):
            cx, cy, _ = VELOCITIES[p]
            if cx != 0:
                face = edge - 1 if cx > 0 else 0
                for c in range(2):
                    value = jnp.where(x == face, shift(own[c], cx * (edge - 1)), shift(own[c], -cx))
                    out[c] = jnp.where(level == i, value, out[c])
            if cy != 0:
                outer = 1 if cy > 0 else 0
                face = 7 if cy > 0 else 0
                start = NORTH_POPS.index(p) * edge if cy > 0 else SOUTH + SOUTH_POPS.index(p) * edge
                turned = [shift(side, -cy * edge) for side in own]
                arrived = jnp.broadcast_to(shift(own[0][5:6], face * edge - start), (8, 128))
                inner = jnp.where(group == face, turned[outer], turned[1 - outer])
                rim = jnp.where(group == face, arrived, turned[outer])
                out[1 - outer] = jnp.where(level == i, inner, out[1 - outer])
                out[outer] = jnp.where(level == i, rim, out[outer])
        return out

    def prepare(e, carry):
        first = [first_ref[e, at : at + 8, :] for at in (0, 6)]
        second = [second_ref[e, 4:12, :], shift(second_ref[e, 8:16, :], -2, 0)]
        above = [jnp.where(swapped, a, b) for a, b in zip(first, second)]
        below = [jnp.where(swapped, b, a) for a, b in zip(first, second)]
        for own, pops, ref in ((above, UPPER_POPS, above_ref), (below, LOWER_POPS, below_ref)):
            for at, tile in zip((0, 8), z_tiles(own, pops)):
                ref[e, at : at + 8, :] = tile
        for at in (0, 8):
            own = faces_ref[e, Y_ROWS + at : Y_ROWS + at + 8, :]
            east = jnp.where(x == edge - 1, shift(own, edge - 1), shift(own, -1))
            west = jnp.where(x == 0, shift(own, 1 - edge), shift(own, 1))
            y_ref[e, at : at + 8, :] = jnp.where(in_east, east, jnp.where(in_west, west, own))
        return carry

    lax.fori_loop(0, devices, prepare, 0, unroll=8)

    def pick(index, tiles_of):
        total = None
        for e in range(devices):
            hit = index == e
            tiles = tiles_of(e)
            total = [jnp.where(hit, t, 0.0 if total is None else total[k]) for k, t in enumerate(tiles)]
        return total

    def one(d, carry):
        row = [jnp.broadcast_to(sources_ref[d, r : r + 1, :], (8, 128)) for r in range(14)]
        for at, index in zip((0, 8, 16), row):
            (halo_ref[d, at : at + 8, :],) = pick(index, lambda e: [faces_ref[e, at : at + 8, :]])
        for at, tile in zip((0, 8), pick(row[3], lambda e: [y_ref[e, at : at + 8, :] for at in (0, 8)])):
            halo_ref[d, Y_ROWS + at : Y_ROWS + at + 8, :] = tile
        for pops, base, ref, upper in ((UPPER_POPS, 4, above_ref, True), (LOWER_POPS, 9, below_ref, False)):
            index = [row[base]] * 2
            for i, p in enumerate(pops):
                cx, cy, _ = VELOCITIES[p]
                if cx != 0:
                    here = (level == i) & (x == (edge - 1 if cx > 0 else 0))
                    index = [jnp.where(here, row[base + (1 if cx > 0 else 2)], side) for side in index]
                if cy != 0:
                    outer, face = (1, 7) if cy > 0 else (0, 0)
                    here = (level == i) & (group == face)
                    index[outer] = jnp.where(here, row[base + (3 if cy > 0 else 4)], index[outer])
            for left, at, side in zip(sides, (0, 8), index):
                (tile,) = pick(side, lambda e: [ref[e, at : at + 8, :]])
                top = halo_row(upper, left, 0).start
                halo_ref[d, top : top + 6, :] = tile[0:6]
        return carry

    lax.fori_loop(0, devices, one, 0, unroll=8)


def slab_kernel(
    blocks, devices, chunks, owner_ref, column_ref, rows_ref, out_ref, first_ref, second_ref, field_ref
):
    slab = lax.axis_index("blk").astype(jnp.int32)
    swapped = first_partner_above()
    count, edge, width = out_ref.shape
    start = slab_start(owner_ref, slab, devices)
    group = lanes((edge, width)) // edge
    lane = lanes((edge, width))
    height = blocks * edge

    def chunk(i):
        top = start - 2 + 8 * i
        tiles = [jnp.zeros((edge, width), jnp.float32) for _ in range(8)]
        at = FACE_ROWS + 16 * i
        if at + 16 <= rows_ref.shape[1]:
            values = [rows_ref[e, at : at + 16, :] for e in range(devices)]
        else:
            halves = [rows_ref[e, at : at + 8, :] for e in range(devices)]
            values = [jnp.concatenate([half, shift(half, 64)], axis=0) for half in halves]
        for r in range(0, 8, 2):
            inside = (top + r >= 0) & (top + r < height)
            block_row = lax.div(jnp.clip(top + r, 0, height - 1), jnp.int32(edge))
            for e in range(devices):
                column = column_ref[0, e * blocks + block_row]
                hit = group == jnp.where(inside, column, -1)
                for k in range(r, r + 2):
                    part = pltpu.roll(values[e], lax.rem(column + (8 - k), jnp.int32(8)) * edge, 1)
                    if width > 128:
                        part = jnp.concatenate([part] * (width // 128), axis=1)
                    tiles[k] = jnp.where(hit, part, tiles[k])
        for r in range(8):
            field_ref[i * 8 + r] = tiles[r]

    for i in range(chunks):
        chunk(i)

    def row(r):
        at = r
        mixed = TAP_EDGE * (field_ref[at] + field_ref[at + 4]) + (
            TAP_NEAR * (field_ref[at + 1] + field_ref[at + 3]) + field_ref[at + 2]
        )
        value = mixed
        for step, tap in ((1, TAP_NEAR), (2, TAP_EDGE)):
            left = jnp.where(lane >= step, shift(mixed, step), 0.0)
            right = jnp.where(lane < width - step, shift(mixed, -step), 0.0)
            value = value + tap * (left + right)
        out_ref[r] = value
        low, high = value[0:2], value[edge - 2 : edge]
        first_ref[r] = jnp.where(swapped, high, low)
        second_ref[r] = jnp.where(swapped, low, high)

    by_rows(count, row)


def by_rows(count, body):
    step = 8 if count % 8 == 0 else 4 if count % 4 == 0 else 2

    def several(i, carry):
        for k in range(step):
            body(i * step + k)
        return carry

    lax.fori_loop(0, count // step, several, 0)


def depth_kernel(devices, layers, owner_ref, rows_ref, first_ref, second_ref, out_ref):
    count, edge, width = out_ref.shape
    slab, layer = lax.axis_index("blk").astype(jnp.int32), lax.axis_index("gz").astype(jnp.int32)
    own_rows = jnp.int32(0)
    for j in range(devices):
        own_rows = jnp.where(slab == j, 2 * owner_ref[j], own_rows)
    swapped = first_partner_above()
    depth = lax.broadcasted_iota(jnp.int32, (edge, width), 0)

    def row(r):
        value = rows_ref[r]
        first, second = first_ref[r], second_ref[r]
        below = jnp.where(layer > 0, jnp.where(swapped, second, first), 0.0)
        above = jnp.where(layer < layers - 1, jnp.where(swapped, first, second), 0.0)
        b0, b1, a0, a1 = below[0:1], below[1:2], above[0:1], above[1:2]
        down = jnp.where(depth == 0, b1, shift(value, 1, 0))
        up = jnp.where(depth == edge - 1, a0, shift(value, -1, 0))
        down_2 = jnp.where(depth == 0, b0, jnp.where(depth == 1, b1, shift(value, 2, 0)))
        up_2 = jnp.where(depth == edge - 1, a1, jnp.where(depth == edge - 2, a0, shift(value, -2, 0)))
        total = value + TAP_NEAR * (down + up) + TAP_EDGE * (down_2 + up_2)
        out_ref[r] = jnp.where(r < own_rows, total, 0.0)

    by_rows(count, row)


SMEM = pl.BlockSpec(memory_space=pltpu.SMEM)
VMEM = pl.BlockSpec(memory_space=pltpu.VMEM)


ANY = pl.BlockSpec(memory_space=pl.ANY)


def f32(*shape):
    return jax.ShapeDtypeStruct(shape, jnp.float32)


def hbm(*shape):
    return pltpu.HBM(shape, jnp.float32)


def vmem(*shape):
    return pltpu.VMEM(shape, jnp.float32)


def local(adjoint, velocity, porosity, block_x, neighbours, owner_map):
    blocks, _, edge, plane = adjoint.shape[1:]
    devices, layers = lax.axis_size("blk"), lax.axis_size("gz")
    table = pltpu.with_memory_space_constraint(jnp.transpose(neighbours, (2, 0, 1)), pltpu.HBM)
    state, flow, design = [pltpu.with_memory_space_constraint(x[0], pltpu.HBM) for x in (adjoint, velocity, porosity)]
    rows_cap = 2 * (3 * (blocks * edge // 2) // devices)
    chunks = -(-(rows_cap + 4) // 8)
    width = devices * edge
    first_pairs = [(g, g ^ 1) for g in range(layers)]
    second_pairs = [(g, (g + 1 if g % 2 else g - 1) % layers) for g in range(layers)]
    near_shape, late_shape = [(count,) + state.shape[1:] for count in (blocks // 2, blocks - blocks // 2)]
    faces_shape = (devices, FACE_ROWS, 128)
    row_count = 16 * chunks - (8 if 0 < (rows_cap + 4) % 8 <= 4 else 0)
    post_shape = (blocks, POPS + 1, edge, plane)
    params = pltpu.CompilerParams(vmem_limit_bytes=32 * 1024 * 1024)

    def to_halo(gathered):
        first = lax.ppermute(gathered[:, FIRST : FIRST + 16], "gz", first_pairs)
        second = lax.ppermute(gathered[:, SECOND - 4 : SECOND + 12], "gz", second_pairs)
        halo = pl.pallas_call(
            functools.partial(route_kernel, devices),
            out_shape=f32(*faces_shape),
            in_specs=[VMEM] * 4,
            out_specs=VMEM,
            scratch_shapes=[vmem(devices, 16, 128)] * 3,
            compiler_params=params,
            name="route",
        )(sources, gathered, first, second)
        return lax.all_to_all(halo, "blk", 0, 0, tiled=True)

    inputs = [vmem(*state.shape), vmem(*flow.shape), vmem(*design.shape)]
    post, faces, sources = pl.pallas_call(
        functools.partial(first_kernel, blocks, devices),
        out_shape=(
            vmem(*post_shape),
            f32(*faces_shape),
            jax.ShapeDtypeStruct((devices, SOURCES, 128), jnp.int32),
        ),
        in_specs=[ANY] * 4,
        out_specs=(VMEM,) * 3,
        scratch_shapes=inputs
        + [
            vmem(blocks, 32, 128),
            pltpu.SMEM(table.shape, jnp.int32),
            pltpu.SemaphoreType.DMA((blocks,)),
            pltpu.SemaphoreType.DMA((1,)),
            pltpu.SemaphoreType.DMA((2, blocks)),
        ],
        compiler_params=params,
        name="collide_first",
    )(table, state, flow, design)
    halo = to_halo(lax.all_to_all(faces, "blk", 0, 0, tiled=True))
    near, late, faces = pl.pallas_call(
        functools.partial(second_kernel, blocks, devices, chunks),
        out_shape=(hbm(*near_shape), hbm(*late_shape), f32(devices, FACE_ROWS + row_count, 128)),
        in_specs=[ANY, VMEM, ANY, ANY, VMEM],
        out_specs=(ANY, ANY, VMEM),
        scratch_shapes=inputs[1:]
        + [
            vmem(*state.shape),
            vmem(*state.shape),
            vmem(blocks, 32, 128),
            vmem(4, blocks * plane // 128, edge, 128),
            pltpu.SMEM(owner_map.shape, jnp.int32),
            pltpu.SemaphoreType.DMA((blocks,)),
            pltpu.SemaphoreType.DMA((3,)),
        ],
        compiler_params=params,
        name="stream_collide",
    )(owner_map, post, flow, design, halo)
    gathered = lax.all_to_all(faces, "blk", 0, 0, tiled=True)
    halo = to_halo(gathered)
    slab_shape, ends = (rows_cap, edge, width), (rows_cap, 2, width)
    slab, first, second = pl.pallas_call(
        functools.partial(slab_kernel, blocks, devices, chunks),
        out_shape=(f32(*slab_shape), f32(*ends), f32(*ends)),
        in_specs=[SMEM, SMEM, VMEM],
        out_specs=(VMEM,) * 3,
        scratch_shapes=[vmem(chunks * 8, edge, width)],
        compiler_params=params,
        name="slab_rows",
    )(owner_map, block_x, gathered)
    first = lax.ppermute(first, "gz", first_pairs)
    second = lax.ppermute(second, "gz", second_pairs)
    smoothed = pl.pallas_call(
        functools.partial(depth_kernel, devices, layers),
        out_shape=f32(*slab_shape),
        in_specs=[SMEM, VMEM, VMEM, VMEM],
        out_specs=VMEM,
        compiler_params=params,
        name="slab_depth",
    )(owner_map, slab, first, second)
    moved = pl.pallas_call(
        functools.partial(last_kernel, blocks),
        out_shape=hbm(*state.shape),
        in_specs=[VMEM, ANY, VMEM],
        out_specs=ANY,
        scratch_shapes=[
            vmem(*late_shape),
            vmem(*state.shape),
            vmem(blocks, 32, 128),
            pltpu.SemaphoreType.DMA((2 * blocks - blocks // 2,)),
        ],
        compiler_params=params,
        name="stream_last",
    )(near, pltpu.with_memory_space_constraint(late, pltpu.HBM), halo)
    return (moved[None], smoothed[None, None])


def solution(mesh):
    placed = (
        P("gz", "blk", None, None, None),
        P("gz", "blk", None, None, None),
        P("gz", "blk", None, None),
        P("gz", None),
        P("gz", None, None),
        P(),
    )
    return jax.shard_map(
        local,
        mesh=mesh,
        in_specs=placed,
        out_specs=(P("gz", "blk", None, None, None), P("gz", "blk", None, None, None)),
        check_vma=False,
    )
```

```python
import functools

import jax
import jax.numpy as jnp
import numpy as np
from jax import lax
from jax.experimental import pallas as pl
from jax.experimental.pallas import tpu as pltpu
from jax.sharding import PartitionSpec as P

STEPS = 2
VELOCITIES = [
    (0, 0, 0),
    (1, 0, 0),
    (-1, 0, 0),
    (0, 1, 0),
    (0, -1, 0),
    (0, 0, 1),
    (0, 0, -1),
    (1, 1, 0),
    (-1, -1, 0),
    (1, -1, 0),
    (-1, 1, 0),
    (1, 0, 1),
    (-1, 0, -1),
    (1, 0, -1),
    (-1, 0, 1),
    (0, 1, 1),
    (0, -1, -1),
    (0, 1, -1),
    (0, -1, 1),
]
POPS = 19
EAST_POPS = [1, 7, 9, 11, 13]
WEST_POPS = [2, 10, 8, 12, 14]
NORTH_POPS = [7, 10, 15, 17]
SOUTH_POPS = [8, 9, 16, 18]
UPPER_POPS = [5, 11, 14, 15, 18]
LOWER_POPS = [6, 12, 13, 16, 17]
RELAX_RATE = 1.25
DRAG_RATE = 0.3
TAP_EDGE, TAP_NEAR = 1.0 / 3.0, 2.0 / 3.0

FACE_ROWS = 64
Y_ROWS, FIRST, SECOND = 24, 40, 52
SOUTH = 64
OWN_PAIRS = [0, 1, 2, 4, 5]
FREE_PAIRS = [(0, 6), (1, 3), (1, 6), (1, 7), (2, 6)]
Y_SPOTS = {3: [(0, 6), (0, 7)], 4: [(2, 6), (2, 7)]}
STREAM_ORDER = [1, 2, 7, 10, 9, 8, 11, 12, 13, 14, 0, 5, 6, 15, 16, 17, 18, 3, 4]
STREAM_GROUP = 4


SOURCES = 16


def shift(value, amount, axis=1):
    amount = amount % value.shape[axis]
    return value if amount == 0 else pltpu.roll(value, amount, axis)


def lanes(shape):
    return lax.broadcasted_iota(jnp.int32, shape, len(shape) - 1)


def collide_cells(f, u, porosity):
    total, gap = {}, {}
    for i in range(1, POPS, 2):
        total[i], gap[i] = f[i] + f[i + 1], f[i] - f[i + 1]
    ux, uy, uz = u
    mx = gap[1] + gap[7] + gap[9] + gap[11] + gap[13]
    my = gap[3] + gap[7] - gap[9] + gap[15] + gap[17]
    mz = gap[5] + gap[11] - gap[13] + gap[15] - gap[17]
    xy_sum, xz_sum, yz_sum = total[7] + total[9], total[11] + total[13], total[15] + total[17]
    xx = 2.0 * total[1] + xy_sum + xz_sum
    yy = 2.0 * total[3] + xy_sum + yz_sum
    zz = 2.0 * total[5] + xz_sum + yz_sum
    xy, xz, yz = total[7] - total[9], total[11] - total[13], total[15] - total[17]
    mass = 12.0 * f[0] + 2.0 * (total[1] + total[3] + total[5]) + (xy_sum + xz_sum + yz_sum)
    speed_sq = ux * ux + uy * uy + uz * uz
    qx = xx * ux + xy * uy + xz * uz
    qy = xy * ux + yy * uy + yz * uz
    qz = xz * ux + yz * uy + zz * uz
    sens = ux * mx + uy * my + uz * mz
    drag = DRAG_RATE * porosity
    scale = RELAX_RATE / 36.0
    quad = ux * qx + uy * qy + uz * qz
    base = scale * (mass + 1.5 * (speed_sq * mass) - 4.5 * quad) + drag * sens
    gx = (3.0 * scale) * (mx + gap[1] + 3.0 * qx - ux * mass) - drag * mx
    gy = (3.0 * scale) * (my + gap[3] + 3.0 * qy - uy * mass) - drag * my
    gz = (3.0 * scale) * (mz + gap[5] + 3.0 * qz - uz * mass) - drag * mz
    along = {1: gx, 3: gy, 5: gz, 7: gx + gy, 9: gx - gy, 11: gx + gz, 13: gx - gz, 15: gy + gz, 17: gy - gz}
    keep = 1.0 - RELAX_RATE
    post = [base + keep * f[0]]
    for i in range(1, POPS, 2):
        post.append(base + along[i] + keep * f[i])
        post.append(base - along[i] + keep * f[i + 1])
    return post, sens


def collide_block(read, velocity_ref, porosity_ref, post_ref, edge, plane):
    parts = {}
    for low in range(0, edge, 8):
        for left in range(0, plane, 128):
            zs, cells = pl.ds(low, 8), pl.ds(left, 128)
            post, sens = collide_cells(
                [read(p, zs, cells) for p in range(POPS)],
                [velocity_ref[c, zs, cells] for c in range(3)],
                porosity_ref[zs, cells],
            )
            for p in range(POPS):
                post_ref[p, zs, cells] = post[p]
            parts[low, left] = sens
    return parts


def part(ref, p, low, left):
    return ref[p, low : low + 8, left : left + 128]


def x_pair(p, depth, side):
    i = EAST_POPS.index(p) if p in EAST_POPS else WEST_POPS.index(p)
    return FREE_PAIRS[i] if (depth, side) == (1, 1) else (depth * 2 + side, OWN_PAIRS[i])


def slot_source(slot, east, west, y_face):
    source = jnp.where(slot % 2 == 0, east, west)
    return source if y_face is None else jnp.where(slot % 8 >= 6, y_face, source)


def spread(values, bases, lane):
    places = [(lane - base) % 128 for base in bases]
    for bit in (2, 1, 0):
        moved = [shift(value, 15 << bit) for value in values]
        values = [jnp.where(p & (16 << bit) != 0, m, v) for p, m, v in zip(places, moved, values)]
    return values


def gathered_lanes(values, bases, lane):
    places = [(lane - base) % 128 for base in bases]
    for bit in (0, 1, 2):
        moved = [shift(value, -(15 << bit)) for value in values]
        values = [jnp.where(p & (1 << bit) != 0, m, v) for p, m, v in zip(places, moved, values)]
    return values


def end_row(tile, left, row):
    at = tile + (6 if left else 0) + row
    return slice(at, at + 1)


def halo_row(upper, left, row):
    at = FIRST + (0 if upper else 12) + (6 if left else 0) + row
    return slice(at, at + 1)


def pack_faces(block, blocks, swapped, post_ref, lines_ref, faces_ref, edge, plane):
    def put_ends(target, row, left, cells, low, high):
        faces_ref[target, end_row(FIRST, left, row), cells] = jnp.where(swapped, high, low)
        faces_ref[target, end_row(SECOND, left, row), cells] = jnp.where(swapped, low, high)

    lane = lanes((8, 128))
    slot, group = lane % edge, lane // edge
    every = slice(0, 128)
    tiles = [None] * 3
    for depth, side in ((0, 0), (0, 1), (1, 0), (1, 1)):
        for p in EAST_POPS + WEST_POPS:
            t, pair = x_pair(p, depth, side)
            east = p in EAST_POPS
            s = 2 * pair + (0 if east else 1)
            moved = shift(part(post_ref, p, depth * 8, side * 128), s - (0 if east else 2 * edge - 1))
            tiles[t] = moved if tiles[t] is None else jnp.where(slot == s, moved, tiles[t])
    for p, beyond in ((3, block + 1), (4, block - 1)):
        if 0 <= beyond < blocks:
            for depth, (t, s) in enumerate(Y_SPOTS[p]):
                at = (p - 3) * 16 + depth * 8
                tiles[t] = jnp.where((slot == s) | (slot == s + 8), lines_ref[beyond, at : at + 8, :], tiles[t])
    for t, tile in enumerate(tiles):
        faces_ref[block, t * 8 : t * 8 + 8, :] = tile
    for left in range(0, plane, 128):
        cells = slice(left, left + 128)
        for i in range(5):
            put_ends(
                block,
                i,
                left,
                every,
                post_ref[UPPER_POPS[i], 0:1, cells],
                post_ref[LOWER_POPS[i], edge - 1 : edge, cells],
            )

    def y_tiles(pops, left, first):
        tiles = []
        for low in range(0, edge, 8):
            tile = None
            for q, p in enumerate(pops):
                moved = shift(part(post_ref, p, low, left), q * edge if first == 0 else (q + 5) * edge)
                tile = moved if tile is None else jnp.where(group == first + q, moved, tile)
            tiles.append(tile)
        return tiles

    north = y_tiles(NORTH_POPS, 0, 0)
    south = y_tiles(SOUTH_POPS, plane - 128, 4)

    def put_y(target, tiles, start):
        cells = slice(start, start + 64)
        for half in range(2):
            at = Y_ROWS + half * 8
            faces_ref[target, at : at + 8, cells] = tiles[half][:, cells]
        put_ends(target, 5, 0, cells, tiles[0][0:1, cells], tiles[1][7:8, cells])

    if block > 0:
        put_y(block - 1, north, 0)
    if block < blocks - 1:
        put_y(block + 1, south, SOUTH)


def y_lines(blocks, posts_ref, lines_ref, plane):
    lane = lanes((8, 128))
    spots = [(b, p, depth) for b in range(blocks) for p in (3, 4) for depth in (0, 1)]
    bases = [0 if p == 3 else 112 for _, p, _ in spots]
    lines = [part(posts_ref.at[b], p, depth * 8, 0 if p == 3 else plane - 128) for b, p, depth in spots]
    for (b, p, depth), line, base in zip(spots, spread(lines, bases, lane), bases):
        at = (p - 3) * 16 + depth * 8
        lines_ref[b, at : at + 8, :] = shift(line, Y_SPOTS[p][depth][1] - base)


def y_halos(blocks, halo_ref, lines_ref):
    lane = lanes((8, 128))
    spots = [(b, p, depth) for b in range(blocks) for p in (3, 4) for depth in (0, 1)]
    bases = [Y_SPOTS[p][depth][1] for _, p, depth in spots]
    lines = []
    for b, p, depth in spots:
        t = Y_SPOTS[p][depth][0]
        lines.append(halo_ref[b, t * 8 : t * 8 + 8, :])
    for (b, p, depth), line, base in zip(spots, gathered_lanes(lines, bases, lane), bases):
        at = (p - 3) * 16 + depth * 8
        lines_ref[b, at : at + 8, :] = shift(line, (112 if p == 3 else 0) - base)


def first_partner_above():
    return lax.rem(lax.axis_index("gz").astype(jnp.int32), jnp.int32(2)) == 0


def stream_pop(p, source_ref, halo_ref, y_faces, x_faces, edge):
    cx, cy, cz = VELOCITIES[p]
    lane = lanes((8, 128))
    sides, depths = (0, 1), (0, 1)
    value = {(z, c): shift(part(source_ref, p, z * 8, c * 128), -(cx + edge * cy)) for z in depths for c in sides}
    at_face = lane % edge == (edge - 1 if cx > 0 else 0)
    if cx != 0:
        arrived = {}
        for z in depths:
            for c in sides:
                spot = x_pair(p, z, c)
                if spot not in x_faces:
                    t, pair = spot
                    x_faces[spot] = shift(halo_ref[t * 8 : t * 8 + 8, :], edge - 1 - 2 * pair - edge * cy)
                arrived[z, c] = x_faces[spot]
    if cy == 0:
        if cx != 0:
            value = {at: jnp.where(at_face, arrived[at], value[at]) for at in value}
    else:
        far = 7 if cy > 0 else 0
        border = lane // edge == far
        outer = 1 if cy > 0 else 0
        if p in (3, 4):
            faces = y_faces[p]
        else:
            start = NORTH_POPS.index(p) * edge if cy > 0 else SOUTH + SOUTH_POPS.index(p) * edge
            faces = [shift(halo_ref[at : at + 8, :], far * edge - start) for at in (Y_ROWS, Y_ROWS + 8)]
        moved = {}
        for z in depths:
            inner = jnp.where(border, value[z, outer], value[z, 1 - outer])
            rim = value[z, outer]
            if cx != 0:
                inner = jnp.where(at_face, jnp.where(border, arrived[z, outer], arrived[z, 1 - outer]), inner)
                rim = jnp.where(at_face, arrived[z, outer], rim)
            moved[z, 1 - outer] = inner
            moved[z, outer] = jnp.where(border, faces[z], rim)
        value = moved
    if cz != 0:
        row = UPPER_POPS.index(p) if cz > 0 else LOWER_POPS.index(p)
        outer = 1 if cz > 0 else 0
        border = lax.broadcasted_iota(jnp.int32, (8, 128), 0) == (7 if cz > 0 else 0)
        moved = {}
        for c in sides:
            turned = [shift(value[z, c], -cz, 0) for z in depths]
            moved[1 - outer, c] = jnp.where(border, turned[outer], turned[1 - outer])
            moved[outer, c] = jnp.where(border, halo_ref[halo_row(cz > 0, c * 128, row), :], turned[outer])
        value = moved
    return value


def shift_inside(p, source_ref, edge):
    cx, cy, cz = VELOCITIES[p]
    value = {(z, c): shift(part(source_ref, p, z * 8, c * 128), -(cx + edge * cy)) for z in (0, 1) for c in (0, 1)}
    if cy != 0:
        outer, far = (1, 7) if cy > 0 else (0, 0)
        border = lanes((8, 128)) // edge == far
        for z in (0, 1):
            value[z, 1 - outer] = jnp.where(border, value[z, outer], value[z, 1 - outer])
    return shift_depth(value, cz)


def shift_depth(value, cz):
    if cz == 0:
        return value
    outer = 1 if cz > 0 else 0
    border = lax.broadcasted_iota(jnp.int32, (8, 128), 0) == (7 if cz > 0 else 0)
    turned = {at: shift(tile, -cz, 0) for at, tile in value.items()}
    return {
        (z, c): tile if z == outer else jnp.where(border, turned[outer, c], tile) for (z, c), tile in turned.items()
    }


def insert_halo(p, source_ref, halo_ref, y_faces, x_faces, edge):
    cx, cy, cz = VELOCITIES[p]
    lane = lanes((8, 128))
    sides, depths = (0, 1), (0, 1)
    value = {(z, c): part(source_ref, p, z * 8, c * 128) for z in depths for c in sides}
    if cx != 0:
        at_face = lane % edge == (edge - 1 if cx > 0 else 0)
        arrived = {}
        for z in depths:
            for c in sides:
                spot = x_pair(p, z, c)
                if spot not in x_faces:
                    t, pair = spot
                    x_faces[spot] = shift(halo_ref[t * 8 : t * 8 + 8, :], edge - 1 - 2 * pair - edge * cy)
                arrived[z, c] = x_faces[spot]
    if cy != 0:
        outer, far = (1, 7) if cy > 0 else (0, 0)
        border = lane // edge == far
        if cx != 0:
            for z in depths:
                arrived[z, 1 - outer] = jnp.where(border, arrived[z, outer], arrived[z, 1 - outer])
    if cx != 0:
        arrived = shift_depth(arrived, cz)
        value = {at: jnp.where(at_face, arrived[at], tile) for at, tile in value.items()}
    if cy != 0:
        if p in y_faces:
            faces = y_faces[p]
        else:
            start = NORTH_POPS.index(p) * edge if cy > 0 else SOUTH + SOUTH_POPS.index(p) * edge
            faces = [shift(halo_ref[at : at + 8, :], far * edge - start) for at in (Y_ROWS, Y_ROWS + 8)]
        faces = shift_depth({(z, 0): face for z, face in enumerate(faces)}, cz)
        for z in depths:
            value[z, outer] = jnp.where(border, faces[z, 0], value[z, outer])
    if cz != 0:
        row = UPPER_POPS.index(p) if cz > 0 else LOWER_POPS.index(p)
        last = 1 if cz > 0 else 0
        end = lax.broadcasted_iota(jnp.int32, (8, 128), 0) == (7 if cz > 0 else 0)
        for c in sides:
            value[last, c] = jnp.where(end, halo_ref[halo_row(cz > 0, c * 128, row), :], value[last, c])
    return value


def put_tiles(ref, p, value):
    for (z, c), tile in value.items():
        ref[p, z * 8 : z * 8 + 8, c * 128 : c * 128 + 128] = tile


def ahead_kernel(blocks, before_ref, gathered_ref, after_ref):
    edge = before_ref.shape[2]

    def one(b, carry):
        source_ref, out_ref = before_ref.at[b], after_ref.at[b]
        out_ref[POPS] = source_ref[POPS]
        for start in range(0, POPS, STREAM_GROUP):
            pops = STREAM_ORDER[start : start + STREAM_GROUP]
            values = [shift_inside(p, source_ref, edge) for p in pops]
            for p, value in zip(pops, values):
                put_tiles(out_ref, p, value)
        return carry

    lax.fori_loop(0, blocks, one, 0)


def stream_block(source_ref, halo_ref, lines_ref, out_ref, edge, one_pop=None):
    one_pop = one_pop or stream_pop
    y_faces = {3: [lines_ref[0:8, :], lines_ref[8:16, :]], 4: [lines_ref[16:24, :], lines_ref[24:32, :]]}
    x_faces = {}
    for start in range(0, POPS, STREAM_GROUP):
        pops = STREAM_ORDER[start : start + STREAM_GROUP]
        values = [one_pop(p, source_ref, halo_ref, y_faces, x_faces, edge) for p in pops]
        for p, value in zip(pops, values):
            for (z, c), tile in value.items():
                out_ref[p, z * 8 : z * 8 + 8, c * 128 : c * 128 + 128] = tile


def source_rows(d, row, blocks, table_ref, sources_ref, edge):
    here = d * blocks + row
    west, east, south, north, below, above = [table_ref[face, 0, here] for face in range(6)]

    def beside(slot_id, face):
        return jnp.where(slot_id < 0, -1, table_ref[face, 0, jnp.maximum(slot_id, 0)])

    lane = lanes((1, 128))
    in_north = lane < SOUTH
    near = jnp.where(in_north, north, south)
    far_east = jnp.where(in_north, beside(north, 1), beside(south, 1))
    far_west = jnp.where(in_north, beside(north, 0), beside(south, 0))
    in_east, in_west = east_west_groups(lane, edge)
    rows = [
        slot_source(lane % edge, east, west, north),
        slot_source(lane % edge, east, west, None),
        slot_source(lane % edge, east, west, south),
        jnp.where(
            in_east & (lane % edge == edge - 1),
            far_east,
            jnp.where(in_west & (lane % edge == 0), far_west, near),
        ),
    ]
    for face, own in ((5, above), (4, below)):
        rows += [own, beside(east, face), beside(west, face), beside(north, face), beside(south, face)]
    for r, slot_id in enumerate(rows):
        device = lax.shift_right_arithmetic(slot_id, jnp.int32(blocks.bit_length() - 1))
        sources_ref[d, r : r + 1, :] = jnp.broadcast_to(device, (1, 128))


def east_west_groups(lane, edge):
    group = lane // edge
    return (group == 0) | (group == 5), (group == 1) | (group == 4)


def first_kernel(
    blocks,
    devices,
    table_hbm,
    state_hbm,
    velocity_hbm,
    porosity_hbm,
    post_ref,
    faces_ref,
    sources_ref,
    state_ref,
    velocity_ref,
    porosity_ref,
    lines_ref,
    table_ref,
    sems,
    sem,
    flow_sems,
):
    edge, plane = porosity_ref.shape[1:]
    swapped = first_partner_above()
    row = jnp.minimum(lax.axis_index("blk").astype(jnp.int32), blocks - 1)

    def copy(b):
        return pltpu.make_async_copy(state_hbm.at[b], state_ref.at[b], sems.at[b])

    lookup = pltpu.make_async_copy(table_hbm, table_ref, sem.at[0])

    def flow(b):
        return (
            pltpu.make_async_copy(velocity_hbm.at[b], velocity_ref.at[b], flow_sems.at[0, b]),
            pltpu.make_async_copy(porosity_hbm.at[b], porosity_ref.at[b], flow_sems.at[1, b]),
        )

    for b in range(blocks):
        copy(b).start()
        for other in flow(b):
            other.start()
        if b == 0:
            lookup.start()
    lookup.wait()
    per = -(-devices // blocks)

    def one(b, carry):
        copy(b).wait()
        for other in flow(b):
            other.wait()
        parts = collide_block(
            lambda p, zs, cells: state_ref[b, p, zs, cells],
            velocity_ref.at[b],
            porosity_ref.at[b],
            post_ref.at[b],
            edge,
            plane,
        )
        for (low, left), sens in parts.items():
            post_ref[b, POPS, pl.ds(low, 8), pl.ds(left, 128)] = sens
        for k in range(per):
            source_rows(jnp.minimum(b * per + k, devices - 1), row, blocks, table_ref, sources_ref, edge)
        return carry

    lax.fori_loop(0, blocks, one, 0)
    y_lines(blocks, post_ref, lines_ref, plane)
    for b in range(blocks):
        pack_faces(b, blocks, swapped, post_ref.at[b], lines_ref, faces_ref, edge, plane)


def slab_start(owner_ref, slab, devices):
    start = jnp.int32(0)
    for j in range(devices):
        start = start + jnp.where(j < slab, 2 * owner_ref[j], 0)
    return start


def second_kernel(
    blocks,
    devices,
    chunks,
    owner_hbm,
    before_ref,
    velocity_hbm,
    porosity_hbm,
    halo_ref,
    near_hbm,
    late_hbm,
    faces_ref,
    velocity_ref,
    porosity_ref,
    post_ref,
    state_ref,
    lines_ref,
    turned_ref,
    owner_ref,
    sems,
    sem,
):
    edge, plane = porosity_ref.shape[1:]
    swapped = first_partner_above()
    others = [
        pltpu.make_async_copy(velocity_hbm, velocity_ref, sem.at[1]),
        pltpu.make_async_copy(porosity_hbm, porosity_ref, sem.at[2]),
        pltpu.make_async_copy(owner_hbm, owner_ref, sem.at[0]),
    ]
    for other in others:
        other.start()

    half = blocks // 2

    def result(b, out_hbm, first):
        return pltpu.make_async_copy(post_ref.at[b], out_hbm.at[b - first], sems.at[b])

    def stream(b, carry):
        stream_block(before_ref.at[b], halo_ref.at[b], lines_ref.at[b], state_ref.at[b], edge, insert_halo)
        return carry

    y_halos(blocks, halo_ref, lines_ref)
    lax.fori_loop(0, blocks, stream, 0)
    for other in others:
        other.wait()

    def collide(b, carry):
        parts = collide_block(
            lambda p, zs, cells: state_ref[b, p, zs, cells],
            velocity_ref.at[b],
            porosity_ref.at[b],
            post_ref.at[b],
            edge,
            plane,
        )

        @pl.when(b < half)
        def _():
            result(b, near_hbm, 0).start()

        @pl.when(b >= half)
        def _():
            result(b, late_hbm, half).start()

        for (low, left), sens in parts.items():
            sens = before_ref[b, POPS, pl.ds(low, 8), pl.ds(left, 128)] + sens
            turned_ref[0, b * (plane // 128) + left // 128, pl.ds(low, 8), :] = sens
        return carry

    lax.fori_loop(0, blocks, collide, 0)
    y_lines(blocks, post_ref, lines_ref, plane)

    for b in range(blocks):
        pack_faces(b, blocks, swapped, post_ref.at[b], lines_ref, faces_ref, edge, plane)
    held = blocks * (plane // 128)
    for c in range(held):
        for m in range(1, 4):
            for low in (0, 8):
                turned_ref[m, c, low : low + 8, :] = shift(turned_ref[0, c, low : low + 8, :], -2 * m * edge)
    lane = lanes((edge, 128))
    start = jnp.int32(0)
    for j in range(devices):
        first = lax.div(start + 6, jnp.int32(8)) - 1
        behind = start - 2 - 8 * first
        phase = lax.div(behind, jnp.int32(2))
        turned = [turned_ref[phase, jnp.clip(first + i, 0, held - 1)] for i in range(chunks + 1)]
        kept = lane < 128 - behind * edge
        for i in range(chunks):
            value = jnp.where(kept, turned[i], turned[i + 1])
            at = FACE_ROWS + 16 * i
            if at + 16 <= faces_ref.shape[1]:
                faces_ref[j, at : at + 16, :] = value
            else:
                faces_ref[j, at : at + 8, :] = jnp.where(lane[0:8] < 64, value[0:8], shift(value[8:16], 64))
        start = start + 2 * owner_ref[j]
    for b in range(blocks):
        (result(b, near_hbm, 0) if b < half else result(b, late_hbm, half)).wait()


def last_kernel(blocks, near_ref, late_hbm, halo_ref, out_hbm, late_ref, out_ref, lines_ref, sems):
    edge = late_ref.shape[2]
    half = blocks // 2

    def late(b):
        return pltpu.make_async_copy(late_hbm.at[b - half], late_ref.at[b - half], sems.at[blocks + b - half])

    def result(b):
        return pltpu.make_async_copy(out_ref.at[b], out_hbm.at[b], sems.at[b])

    for b in range(half, blocks):
        late(b).start()

    def one(b, before_ref):
        stream_block(before_ref, halo_ref.at[b], lines_ref.at[b], out_ref.at[b], edge)
        result(b).start()

    def near_one(b, carry):
        one(b, near_ref.at[b])
        return carry

    def late_one(b, carry):
        late(b).wait()
        one(b, late_ref.at[b - half])
        return carry

    y_halos(blocks, halo_ref, lines_ref)
    lax.fori_loop(0, half, near_one, 0)
    lax.fori_loop(half, blocks, late_one, 0)
    for b in range(blocks):
        result(b).wait()


def route_kernel(devices, sources_ref, faces_ref, first_ref, second_ref, *refs):
    halo_ref, y_ref, above_ref, below_ref = refs[-4:]
    edge = 16
    swapped = first_partner_above()
    lane = lanes((8, 128))
    level = lax.broadcasted_iota(jnp.int32, (8, 128), 0)
    x, group = lane % edge, lane // edge
    in_east, in_west = east_west_groups(lane, edge)
    sides = (0, 128)

    def z_tiles(own, pops):
        out = list(own)
        for i, p in enumerate(pops):
            cx, cy, _ = VELOCITIES[p]
            if cx != 0:
                face = edge - 1 if cx > 0 else 0
                for c in range(2):
                    value = jnp.where(x == face, shift(own[c], cx * (edge - 1)), shift(own[c], -cx))
                    out[c] = jnp.where(level == i, value, out[c])
            if cy != 0:
                outer = 1 if cy > 0 else 0
                face = 7 if cy > 0 else 0
                start = NORTH_POPS.index(p) * edge if cy > 0 else SOUTH + SOUTH_POPS.index(p) * edge
                turned = [shift(side, -cy * edge) for side in own]
                arrived = jnp.broadcast_to(shift(own[0][5:6], face * edge - start), (8, 128))
                inner = jnp.where(group == face, turned[outer], turned[1 - outer])
                rim = jnp.where(group == face, arrived, turned[outer])
                out[1 - outer] = jnp.where(level == i, inner, out[1 - outer])
                out[outer] = jnp.where(level == i, rim, out[outer])
        return out

    def prepare(e, carry):
        first = [first_ref[e, at : at + 8, :] for at in (0, 6)]
        second = [second_ref[e, 4:12, :], shift(second_ref[e, 8:16, :], -2, 0)]
        above = [jnp.where(swapped, a, b) for a, b in zip(first, second)]
        below = [jnp.where(swapped, b, a) for a, b in zip(first, second)]
        for own, pops, ref in ((above, UPPER_POPS, above_ref), (below, LOWER_POPS, below_ref)):
            for at, tile in zip((0, 8), z_tiles(own, pops)):
                ref[e, at : at + 8, :] = tile
        for at in (0, 8):
            own = faces_ref[e, Y_ROWS + at : Y_ROWS + at + 8, :]
            east = jnp.where(x == edge - 1, shift(own, edge - 1), shift(own, -1))
            west = jnp.where(x == 0, shift(own, 1 - edge), shift(own, 1))
            y_ref[e, at : at + 8, :] = jnp.where(in_east, east, jnp.where(in_west, west, own))
        return carry

    lax.fori_loop(0, devices, prepare, 0, unroll=8)

    def pick(index, tiles_of):
        total = None
        for e in range(devices):
            hit = index == e
            tiles = tiles_of(e)
            total = [jnp.where(hit, t, 0.0 if total is None else total[k]) for k, t in enumerate(tiles)]
        return total

    def one(d, carry):
        row = [jnp.broadcast_to(sources_ref[d, r : r + 1, :], (8, 128)) for r in range(14)]
        for at, index in zip((0, 8, 16), row):
            (halo_ref[d, at : at + 8, :],) = pick(index, lambda e: [faces_ref[e, at : at + 8, :]])
        for at, tile in zip((0, 8), pick(row[3], lambda e: [y_ref[e, at : at + 8, :] for at in (0, 8)])):
            halo_ref[d, Y_ROWS + at : Y_ROWS + at + 8, :] = tile
        for pops, base, ref, upper in ((UPPER_POPS, 4, above_ref, True), (LOWER_POPS, 9, below_ref, False)):
            index = [row[base]] * 2
            for i, p in enumerate(pops):
                cx, cy, _ = VELOCITIES[p]
                if cx != 0:
                    here = (level == i) & (x == (edge - 1 if cx > 0 else 0))
                    index = [jnp.where(here, row[base + (1 if cx > 0 else 2)], side) for side in index]
                if cy != 0:
                    outer, face = (1, 7) if cy > 0 else (0, 0)
                    here = (level == i) & (group == face)
                    index[outer] = jnp.where(here, row[base + (3 if cy > 0 else 4)], index[outer])
            for left, at, side in zip(sides, (0, 8), index):
                (tile,) = pick(side, lambda e: [ref[e, at : at + 8, :]])
                top = halo_row(upper, left, 0).start
                halo_ref[d, top : top + 6, :] = tile[0:6]
        return carry

    lax.fori_loop(0, devices, one, 0, unroll=8)


def slab_kernel(
    blocks, devices, chunks, owner_ref, column_ref, rows_ref, out_ref, first_ref, second_ref, field_ref
):
    slab = lax.axis_index("blk").astype(jnp.int32)
    swapped = first_partner_above()
    count, edge, width = out_ref.shape
    start = slab_start(owner_ref, slab, devices)
    group = lanes((edge, width)) // edge
    lane = lanes((edge, width))
    height = blocks * edge

    def chunk(i):
        top = start - 2 + 8 * i
        tiles = [jnp.zeros((edge, width), jnp.float32) for _ in range(8)]
        at = FACE_ROWS + 16 * i
        if at + 16 <= rows_ref.shape[1]:
            values = [rows_ref[e, at : at + 16, :] for e in range(devices)]
        else:
            halves = [rows_ref[e, at : at + 8, :] for e in range(devices)]
            values = [jnp.concatenate([half, shift(half, 64)], axis=0) for half in halves]
        for r in range(0, 8, 2):
            inside = (top + r >= 0) & (top + r < height)
            block_row = lax.div(jnp.clip(top + r, 0, height - 1), jnp.int32(edge))
            for e in range(devices):
                column = column_ref[0, e * blocks + block_row]
                hit = group == jnp.where(inside, column, -1)
                for k in range(r, r + 2):
                    part = pltpu.roll(values[e], lax.rem(column + (8 - k), jnp.int32(8)) * edge, 1)
                    if width > 128:
                        part = jnp.concatenate([part] * (width // 128), axis=1)
                    tiles[k] = jnp.where(hit, part, tiles[k])
        for r in range(8):
            field_ref[i * 8 + r] = tiles[r]

    for i in range(chunks):
        chunk(i)

    def row(r):
        at = r
        mixed = TAP_EDGE * (field_ref[at] + field_ref[at + 4]) + (
            TAP_NEAR * (field_ref[at + 1] + field_ref[at + 3]) + field_ref[at + 2]
        )
        value = mixed
        for step, tap in ((1, TAP_NEAR), (2, TAP_EDGE)):
            left = jnp.where(lane >= step, shift(mixed, step), 0.0)
            right = jnp.where(lane < width - step, shift(mixed, -step), 0.0)
            value = value + tap * (left + right)
        out_ref[r] = value
        low, high = value[0:2], value[edge - 2 : edge]
        first_ref[r] = jnp.where(swapped, high, low)
        second_ref[r] = jnp.where(swapped, low, high)

    by_rows(count, row)


def by_rows(count, body):
    step = 8 if count % 8 == 0 else 4 if count % 4 == 0 else 2

    def several(i, carry):
        for k in range(step):
            body(i * step + k)
        return carry

    lax.fori_loop(0, count // step, several, 0)


def depth_kernel(devices, layers, owner_ref, rows_ref, first_ref, second_ref, out_ref):
    count, edge, width = out_ref.shape
    slab, layer = lax.axis_index("blk").astype(jnp.int32), lax.axis_index("gz").astype(jnp.int32)
    own_rows = jnp.int32(0)
    for j in range(devices):
        own_rows = jnp.where(slab == j, 2 * owner_ref[j], own_rows)
    swapped = first_partner_above()
    depth = lax.broadcasted_iota(jnp.int32, (edge, width), 0)

    def row(r):
        value = rows_ref[r]
        first, second = first_ref[r], second_ref[r]
        below = jnp.where(layer > 0, jnp.where(swapped, second, first), 0.0)
        above = jnp.where(layer < layers - 1, jnp.where(swapped, first, second), 0.0)
        b0, b1, a0, a1 = below[0:1], below[1:2], above[0:1], above[1:2]
        down = jnp.where(depth == 0, b1, shift(value, 1, 0))
        up = jnp.where(depth == edge - 1, a0, shift(value, -1, 0))
        down_2 = jnp.where(depth == 0, b0, jnp.where(depth == 1, b1, shift(value, 2, 0)))
        up_2 = jnp.where(depth == edge - 1, a1, jnp.where(depth == edge - 2, a0, shift(value, -2, 0)))
        total = value + TAP_NEAR * (down + up) + TAP_EDGE * (down_2 + up_2)
        out_ref[r] = jnp.where(r < own_rows, total, 0.0)

    by_rows(count, row)


SMEM = pl.BlockSpec(memory_space=pltpu.SMEM)
VMEM = pl.BlockSpec(memory_space=pltpu.VMEM)


ANY = pl.BlockSpec(memory_space=pl.ANY)


def f32(*shape):
    return jax.ShapeDtypeStruct(shape, jnp.float32)


def hbm(*shape):
    return pltpu.HBM(shape, jnp.float32)


def vmem(*shape):
    return pltpu.VMEM(shape, jnp.float32)


def local(adjoint, velocity, porosity, block_x, neighbours, owner_map):
    blocks, _, edge, plane = adjoint.shape[1:]
    devices, layers = lax.axis_size("blk"), lax.axis_size("gz")
    table = pltpu.with_memory_space_constraint(jnp.transpose(neighbours, (2, 0, 1)), pltpu.HBM)
    state, flow, design = [pltpu.with_memory_space_constraint(x[0], pltpu.HBM) for x in (adjoint, velocity, porosity)]
    rows_cap = 2 * (3 * (blocks * edge // 2) // devices)
    chunks = -(-(rows_cap + 4) // 8)
    width = devices * edge
    first_pairs = [(g, g ^ 1) for g in range(layers)]
    second_pairs = [(g, (g + 1 if g % 2 else g - 1) % layers) for g in range(layers)]
    near_shape, late_shape = [(count,) + state.shape[1:] for count in (blocks // 2, blocks - blocks // 2)]
    faces_shape = (devices, FACE_ROWS, 128)
    row_count = 16 * chunks - (8 if 0 < (rows_cap + 4) % 8 <= 4 else 0)
    post_shape = (blocks, POPS + 1, edge, plane)
    params = pltpu.CompilerParams(vmem_limit_bytes=32 * 1024 * 1024)

    def to_halo(gathered, *others):
        first = lax.ppermute(gathered[:, FIRST : FIRST + 16], "gz", first_pairs)
        second = lax.ppermute(gathered[:, SECOND - 4 : SECOND + 12], "gz", second_pairs)
        halo = pl.pallas_call(
            functools.partial(route_kernel, devices),
            out_shape=f32(*faces_shape),
            in_specs=[VMEM] * 4 + [ANY] * len(others),
            out_specs=VMEM,
            scratch_shapes=[vmem(devices, 16, 128)] * 3,
            compiler_params=params,
            name="route",
        )(sources, gathered, first, second, *others)
        return lax.all_to_all(halo, "blk", 0, 0, tiled=True)

    inputs = [vmem(*state.shape), vmem(*flow.shape), vmem(*design.shape)]
    post, faces, sources = pl.pallas_call(
        functools.partial(first_kernel, blocks, devices),
        out_shape=(
            vmem(*post_shape),
            f32(*faces_shape),
            jax.ShapeDtypeStruct((devices, SOURCES, 128), jnp.int32),
        ),
        in_specs=[ANY] * 4,
        out_specs=(VMEM,) * 3,
        scratch_shapes=inputs
        + [
            vmem(blocks, 32, 128),
            pltpu.SMEM(table.shape, jnp.int32),
            pltpu.SemaphoreType.DMA((blocks,)),
            pltpu.SemaphoreType.DMA((1,)),
            pltpu.SemaphoreType.DMA((2, blocks)),
        ],
        compiler_params=params,
        name="collide_first",
    )(table, state, flow, design)
    gathered = lax.all_to_all(faces, "blk", 0, 0, tiled=True)
    post = pl.pallas_call(
        functools.partial(ahead_kernel, blocks),
        out_shape=vmem(*post_shape),
        in_specs=[VMEM, ANY],
        out_specs=VMEM,
        compiler_params=params,
        name="shift_inside",
    )(post, gathered)
    halo = to_halo(gathered, post)
    near, late, faces = pl.pallas_call(
        functools.partial(second_kernel, blocks, devices, chunks),
        out_shape=(hbm(*near_shape), hbm(*late_shape), f32(devices, FACE_ROWS + row_count, 128)),
        in_specs=[ANY, VMEM, ANY, ANY, VMEM],
        out_specs=(ANY, ANY, VMEM),
        scratch_shapes=inputs[1:]
        + [
            vmem(*state.shape),
            vmem(*state.shape),
            vmem(blocks, 32, 128),
            vmem(4, blocks * plane // 128, edge, 128),
            pltpu.SMEM(owner_map.shape, jnp.int32),
            pltpu.SemaphoreType.DMA((blocks,)),
            pltpu.SemaphoreType.DMA((3,)),
        ],
        compiler_params=params,
        name="stream_collide",
    )(owner_map, post, flow, design, halo)
    gathered = lax.all_to_all(faces, "blk", 0, 0, tiled=True)
    halo = to_halo(gathered)
    slab_shape, ends = (rows_cap, edge, width), (rows_cap, 2, width)
    slab, first, second = pl.pallas_call(
        functools.partial(slab_kernel, blocks, devices, chunks),
        out_shape=(f32(*slab_shape), f32(*ends), f32(*ends)),
        in_specs=[SMEM, SMEM, VMEM],
        out_specs=(VMEM,) * 3,
        scratch_shapes=[vmem(chunks * 8, edge, width)],
        compiler_params=params,
        name="slab_rows",
    )(owner_map, block_x, gathered)
    first = lax.ppermute(first, "gz", first_pairs)
    second = lax.ppermute(second, "gz", second_pairs)
    smoothed = pl.pallas_call(
        functools.partial(depth_kernel, devices, layers),
        out_shape=f32(*slab_shape),
        in_specs=[SMEM, VMEM, VMEM, VMEM],
        out_specs=VMEM,
        compiler_params=params,
        name="slab_depth",
    )(owner_map, slab, first, second)
    moved = pl.pallas_call(
        functools.partial(last_kernel, blocks),
        out_shape=hbm(*state.shape),
        in_specs=[VMEM, ANY, VMEM],
        out_specs=ANY,
        scratch_shapes=[
            vmem(*late_shape),
            vmem(*state.shape),
            vmem(blocks, 32, 128),
            pltpu.SemaphoreType.DMA((2 * blocks - blocks // 2,)),
        ],
        compiler_params=params,
        name="stream_last",
    )(near, pltpu.with_memory_space_constraint(late, pltpu.HBM), halo)
    return (moved[None], smoothed[None, None])


def solution(mesh):
    placed = (
        P("gz", "blk", None, None, None),
        P("gz", "blk", None, None, None),
        P("gz", "blk", None, None),
        P("gz", None),
        P("gz", None, None),
        P(),
    )
    return jax.shard_map(
        local,
        mesh=mesh,
        in_specs=placed,
        out_specs=(P("gz", "blk", None, None, None), P("gz", "blk", None, None, None)),
        check_vma=False,
    )
```

```python
import functools

import jax
import jax.numpy as jnp
import numpy as np
from jax import lax
from jax.experimental import pallas as pl
from jax.experimental.pallas import tpu as pltpu
from jax.sharding import PartitionSpec as P

STEPS = 2
VELOCITIES = [
    (0, 0, 0),
    (1, 0, 0),
    (-1, 0, 0),
    (0, 1, 0),
    (0, -1, 0),
    (0, 0, 1),
    (0, 0, -1),
    (1, 1, 0),
    (-1, -1, 0),
    (1, -1, 0),
    (-1, 1, 0),
    (1, 0, 1),
    (-1, 0, -1),
    (1, 0, -1),
    (-1, 0, 1),
    (0, 1, 1),
    (0, -1, -1),
    (0, 1, -1),
    (0, -1, 1),
]
POPS = 19
EAST_POPS = [1, 7, 9, 11, 13]
WEST_POPS = [2, 10, 8, 12, 14]
NORTH_POPS = [7, 10, 15, 17]
SOUTH_POPS = [8, 9, 16, 18]
UPPER_POPS = [5, 11, 14, 15, 18]
LOWER_POPS = [6, 12, 13, 16, 17]
RELAX_RATE = 1.25
DRAG_RATE = 0.3
TAP_EDGE, TAP_NEAR = 1.0 / 3.0, 2.0 / 3.0

FACE_ROWS = 64
Y_ROWS, FIRST, SECOND = 24, 40, 52
SOUTH = 64
OWN_PAIRS = [0, 1, 2, 4, 5]
FREE_PAIRS = [(0, 6), (1, 3), (1, 6), (1, 7), (2, 6)]
Y_SPOTS = {3: [(0, 6), (0, 7)], 4: [(2, 6), (2, 7)]}
STREAM_ORDER = [1, 2, 7, 10, 9, 8, 11, 12, 13, 14, 0, 5, 6, 15, 16, 17, 18, 3, 4]
STREAM_GROUP = 4


SOURCES = 16


def shift(value, amount, axis=1):
    amount = amount % value.shape[axis]
    return value if amount == 0 else pltpu.roll(value, amount, axis)


def lanes(shape):
    return lax.broadcasted_iota(jnp.int32, shape, len(shape) - 1)


def collide_cells(f, u, porosity):
    total, gap = {}, {}
    for i in range(1, POPS, 2):
        total[i], gap[i] = f[i] + f[i + 1], f[i] - f[i + 1]
    ux, uy, uz = u
    mx = gap[1] + gap[7] + gap[9] + gap[11] + gap[13]
    my = gap[3] + gap[7] - gap[9] + gap[15] + gap[17]
    mz = gap[5] + gap[11] - gap[13] + gap[15] - gap[17]
    xy_sum, xz_sum, yz_sum = total[7] + total[9], total[11] + total[13], total[15] + total[17]
    xx = 2.0 * total[1] + xy_sum + xz_sum
    yy = 2.0 * total[3] + xy_sum + yz_sum
    zz = 2.0 * total[5] + xz_sum + yz_sum
    xy, xz, yz = total[7] - total[9], total[11] - total[13], total[15] - total[17]
    mass = 12.0 * f[0] + 2.0 * (total[1] + total[3] + total[5]) + (xy_sum + xz_sum + yz_sum)
    speed_sq = ux * ux + uy * uy + uz * uz
    qx = xx * ux + xy * uy + xz * uz
    qy = xy * ux + yy * uy + yz * uz
    qz = xz * ux + yz * uy + zz * uz
    sens = ux * mx + uy * my + uz * mz
    drag = DRAG_RATE * porosity
    scale = RELAX_RATE / 36.0
    quad = ux * qx + uy * qy + uz * qz
    base = scale * (mass + 1.5 * (speed_sq * mass) - 4.5 * quad) + drag * sens
    gx = (3.0 * scale) * (mx + gap[1] + 3.0 * qx - ux * mass) - drag * mx
    gy = (3.0 * scale) * (my + gap[3] + 3.0 * qy - uy * mass) - drag * my
    gz = (3.0 * scale) * (mz + gap[5] + 3.0 * qz - uz * mass) - drag * mz
    along = {1: gx, 3: gy, 5: gz, 7: gx + gy, 9: gx - gy, 11: gx + gz, 13: gx - gz, 15: gy + gz, 17: gy - gz}
    keep = 1.0 - RELAX_RATE
    post = [base + keep * f[0]]
    for i in range(1, POPS, 2):
        post.append(base + along[i] + keep * f[i])
        post.append(base - along[i] + keep * f[i + 1])
    return post, sens


def collide_block(read, velocity_ref, porosity_ref, post_ref, edge, plane):
    parts = {}
    for low in range(0, edge, 8):
        for left in range(0, plane, 128):
            zs, cells = pl.ds(low, 8), pl.ds(left, 128)
            post, sens = collide_cells(
                [read(p, zs, cells) for p in range(POPS)],
                [velocity_ref[c, zs, cells] for c in range(3)],
                porosity_ref[zs, cells],
            )
            for p in range(POPS):
                post_ref[p, zs, cells] = post[p]
            parts[low, left] = sens
    return parts


def part(ref, p, low, left):
    return ref[p, low : low + 8, left : left + 128]


def x_pair(p, depth, side):
    i = EAST_POPS.index(p) if p in EAST_POPS else WEST_POPS.index(p)
    return FREE_PAIRS[i] if (depth, side) == (1, 1) else (depth * 2 + side, OWN_PAIRS[i])


def slot_source(slot, east, west, y_face):
    source = jnp.where(slot % 2 == 0, east, west)
    return source if y_face is None else jnp.where(slot % 8 >= 6, y_face, source)


def spread(values, bases, lane):
    places = [(lane - base) % 128 for base in bases]
    for bit in (2, 1, 0):
        moved = [shift(value, 15 << bit) for value in values]
        values = [jnp.where(p & (16 << bit) != 0, m, v) for p, m, v in zip(places, moved, values)]
    return values


def gathered_lanes(values, bases, lane):
    places = [(lane - base) % 128 for base in bases]
    for bit in (0, 1, 2):
        moved = [shift(value, -(15 << bit)) for value in values]
        values = [jnp.where(p & (1 << bit) != 0, m, v) for p, m, v in zip(places, moved, values)]
    return values


def end_row(tile, left, row):
    at = tile + (6 if left else 0) + row
    return slice(at, at + 1)


def halo_row(upper, left, row):
    at = FIRST + (0 if upper else 12) + (6 if left else 0) + row
    return slice(at, at + 1)


def pack_faces(block, blocks, swapped, post_ref, lines_ref, faces_ref, edge, plane):
    def put_ends(target, row, left, cells, low, high):
        faces_ref[target, end_row(FIRST, left, row), cells] = jnp.where(swapped, high, low)
        faces_ref[target, end_row(SECOND, left, row), cells] = jnp.where(swapped, low, high)

    lane = lanes((8, 128))
    slot, group = lane % edge, lane // edge
    every = slice(0, 128)
    tiles = [None] * 3
    for depth, side in ((0, 0), (0, 1), (1, 0), (1, 1)):
        for p in EAST_POPS + WEST_POPS:
            t, pair = x_pair(p, depth, side)
            east = p in EAST_POPS
            s = 2 * pair + (0 if east else 1)
            moved = shift(part(post_ref, p, depth * 8, side * 128), s - (0 if east else 2 * edge - 1))
            tiles[t] = moved if tiles[t] is None else jnp.where(slot == s, moved, tiles[t])
    for p, beyond in ((3, block + 1), (4, block - 1)):
        if 0 <= beyond < blocks:
            for depth, (t, s) in enumerate(Y_SPOTS[p]):
                at = (p - 3) * 16 + depth * 8
                tiles[t] = jnp.where((slot == s) | (slot == s + 8), lines_ref[beyond, at : at + 8, :], tiles[t])
    for t, tile in enumerate(tiles):
        faces_ref[block, t * 8 : t * 8 + 8, :] = tile
    for left in range(0, plane, 128):
        cells = slice(left, left + 128)
        for i in range(5):
            put_ends(
                block,
                i,
                left,
                every,
                post_ref[UPPER_POPS[i], 0:1, cells],
                post_ref[LOWER_POPS[i], edge - 1 : edge, cells],
            )

    def y_tiles(pops, left, first):
        tiles = []
        for low in range(0, edge, 8):
            tile = None
            for q, p in enumerate(pops):
                moved = shift(part(post_ref, p, low, left), q * edge if first == 0 else (q + 5) * edge)
                tile = moved if tile is None else jnp.where(group == first + q, moved, tile)
            tiles.append(tile)
        return tiles

    north = y_tiles(NORTH_POPS, 0, 0)
    south = y_tiles(SOUTH_POPS, plane - 128, 4)

    def put_y(target, tiles, start):
        cells = slice(start, start + 64)
        for half in range(2):
            at = Y_ROWS + half * 8
            faces_ref[target, at : at + 8, cells] = tiles[half][:, cells]
        put_ends(target, 5, 0, cells, tiles[0][0:1, cells], tiles[1][7:8, cells])

    if block > 0:
        put_y(block - 1, north, 0)
    if block < blocks - 1:
        put_y(block + 1, south, SOUTH)


def y_lines(blocks, posts_ref, lines_ref, plane):
    lane = lanes((8, 128))
    spots = [(b, p, depth) for b in range(blocks) for p in (3, 4) for depth in (0, 1)]
    bases = [0 if p == 3 else 112 for _, p, _ in spots]
    lines = [part(posts_ref.at[b], p, depth * 8, 0 if p == 3 else plane - 128) for b, p, depth in spots]
    for (b, p, depth), line, base in zip(spots, spread(lines, bases, lane), bases):
        at = (p - 3) * 16 + depth * 8
        lines_ref[b, at : at + 8, :] = shift(line, Y_SPOTS[p][depth][1] - base)


def y_halos(blocks, halo_ref, lines_ref):
    lane = lanes((8, 128))
    spots = [(b, p, depth) for b in range(blocks) for p in (3, 4) for depth in (0, 1)]
    bases = [Y_SPOTS[p][depth][1] for _, p, depth in spots]
    lines = []
    for b, p, depth in spots:
        t = Y_SPOTS[p][depth][0]
        lines.append(halo_ref[b, t * 8 : t * 8 + 8, :])
    for (b, p, depth), line, base in zip(spots, gathered_lanes(lines, bases, lane), bases):
        at = (p - 3) * 16 + depth * 8
        lines_ref[b, at : at + 8, :] = shift(line, (112 if p == 3 else 0) - base)


def first_partner_above():
    return lax.rem(lax.axis_index("gz").astype(jnp.int32), jnp.int32(2)) == 0


def stream_pop(p, source_ref, halo_ref, y_faces, x_faces, edge):
    cx, cy, cz = VELOCITIES[p]
    lane = lanes((8, 128))
    sides, depths = (0, 1), (0, 1)
    value = {(z, c): shift(part(source_ref, p, z * 8, c * 128), -(cx + edge * cy)) for z in depths for c in sides}
    at_face = lane % edge == (edge - 1 if cx > 0 else 0)
    if cx != 0:
        arrived = {}
        for z in depths:
            for c in sides:
                spot = x_pair(p, z, c)
                if spot not in x_faces:
                    t, pair = spot
                    x_faces[spot] = shift(halo_ref[t * 8 : t * 8 + 8, :], edge - 1 - 2 * pair - edge * cy)
                arrived[z, c] = x_faces[spot]
    if cy == 0:
        if cx != 0:
            value = {at: jnp.where(at_face, arrived[at], value[at]) for at in value}
    else:
        far = 7 if cy > 0 else 0
        border = lane // edge == far
        outer = 1 if cy > 0 else 0
        if p in (3, 4):
            faces = y_faces[p]
        else:
            start = NORTH_POPS.index(p) * edge if cy > 0 else SOUTH + SOUTH_POPS.index(p) * edge
            faces = [shift(halo_ref[at : at + 8, :], far * edge - start) for at in (Y_ROWS, Y_ROWS + 8)]
        moved = {}
        for z in depths:
            inner = jnp.where(border, value[z, outer], value[z, 1 - outer])
            rim = value[z, outer]
            if cx != 0:
                inner = jnp.where(at_face, jnp.where(border, arrived[z, outer], arrived[z, 1 - outer]), inner)
                rim = jnp.where(at_face, arrived[z, outer], rim)
            moved[z, 1 - outer] = inner
            moved[z, outer] = jnp.where(border, faces[z], rim)
        value = moved
    if cz != 0:
        row = UPPER_POPS.index(p) if cz > 0 else LOWER_POPS.index(p)
        outer = 1 if cz > 0 else 0
        border = lax.broadcasted_iota(jnp.int32, (8, 128), 0) == (7 if cz > 0 else 0)
        moved = {}
        for c in sides:
            turned = [shift(value[z, c], -cz, 0) for z in depths]
            moved[1 - outer, c] = jnp.where(border, turned[outer], turned[1 - outer])
            moved[outer, c] = jnp.where(border, halo_ref[halo_row(cz > 0, c * 128, row), :], turned[outer])
        value = moved
    return value


def shift_inside(p, source_ref, edge):
    cx, cy, cz = VELOCITIES[p]
    value = {(z, c): shift(part(source_ref, p, z * 8, c * 128), -(cx + edge * cy)) for z in (0, 1) for c in (0, 1)}
    if cy != 0:
        outer, far = (1, 7) if cy > 0 else (0, 0)
        border = lanes((8, 128)) // edge == far
        for z in (0, 1):
            value[z, 1 - outer] = jnp.where(border, value[z, outer], value[z, 1 - outer])
    return shift_depth(value, cz)


def shift_depth(value, cz):
    if cz == 0:
        return value
    outer = 1 if cz > 0 else 0
    border = lax.broadcasted_iota(jnp.int32, (8, 128), 0) == (7 if cz > 0 else 0)
    turned = {at: shift(tile, -cz, 0) for at, tile in value.items()}
    return {
        (z, c): tile if z == outer else jnp.where(border, turned[outer, c], tile) for (z, c), tile in turned.items()
    }


def insert_halo(p, source_ref, halo_ref, y_faces, x_faces, edge):
    cx, cy, cz = VELOCITIES[p]
    lane = lanes((8, 128))
    sides, depths = (0, 1), (0, 1)
    value = {(z, c): part(source_ref, p, z * 8, c * 128) for z in depths for c in sides}
    if cx != 0:
        at_face = lane % edge == (edge - 1 if cx > 0 else 0)
        arrived = {}
        for z in depths:
            for c in sides:
                spot = x_pair(p, z, c)
                if spot not in x_faces:
                    t, pair = spot
                    x_faces[spot] = shift(halo_ref[t * 8 : t * 8 + 8, :], edge - 1 - 2 * pair - edge * cy)
                arrived[z, c] = x_faces[spot]
    if cy != 0:
        outer, far = (1, 7) if cy > 0 else (0, 0)
        border = lane // edge == far
        if cx != 0:
            for z in depths:
                arrived[z, 1 - outer] = jnp.where(border, arrived[z, outer], arrived[z, 1 - outer])
    if cx != 0:
        arrived = shift_depth(arrived, cz)
        value = {at: jnp.where(at_face, arrived[at], tile) for at, tile in value.items()}
    if cy != 0:
        if p in y_faces:
            faces = y_faces[p]
        else:
            start = NORTH_POPS.index(p) * edge if cy > 0 else SOUTH + SOUTH_POPS.index(p) * edge
            faces = [shift(halo_ref[at : at + 8, :], far * edge - start) for at in (Y_ROWS, Y_ROWS + 8)]
        faces = shift_depth({(z, 0): face for z, face in enumerate(faces)}, cz)
        for z in depths:
            value[z, outer] = jnp.where(border, faces[z, 0], value[z, outer])
    if cz != 0:
        row = UPPER_POPS.index(p) if cz > 0 else LOWER_POPS.index(p)
        last = 1 if cz > 0 else 0
        end = lax.broadcasted_iota(jnp.int32, (8, 128), 0) == (7 if cz > 0 else 0)
        for c in sides:
            value[last, c] = jnp.where(end, halo_ref[halo_row(cz > 0, c * 128, row), :], value[last, c])
    return value


def put_tiles(ref, p, value):
    for (z, c), tile in value.items():
        ref[p, z * 8 : z * 8 + 8, c * 128 : c * 128 + 128] = tile


def ahead_kernel(blocks, before_ref, gathered_ref, after_ref):
    edge = before_ref.shape[2]

    def one(b, carry):
        source_ref, out_ref = before_ref.at[b], after_ref.at[b]
        if before_ref.shape[1] > POPS:
            out_ref[POPS] = source_ref[POPS]
        for start in range(0, POPS, STREAM_GROUP):
            pops = STREAM_ORDER[start : start + STREAM_GROUP]
            values = [shift_inside(p, source_ref, edge) for p in pops]
            for p, value in zip(pops, values):
                put_tiles(out_ref, p, value)
        return carry

    lax.fori_loop(0, blocks, one, 0)


def stream_block(source_ref, halo_ref, lines_ref, out_ref, edge, one_pop=None):
    one_pop = one_pop or stream_pop
    y_faces = {3: [lines_ref[0:8, :], lines_ref[8:16, :]], 4: [lines_ref[16:24, :], lines_ref[24:32, :]]}
    x_faces = {}
    for start in range(0, POPS, STREAM_GROUP):
        pops = STREAM_ORDER[start : start + STREAM_GROUP]
        values = [one_pop(p, source_ref, halo_ref, y_faces, x_faces, edge) for p in pops]
        for p, value in zip(pops, values):
            for (z, c), tile in value.items():
                out_ref[p, z * 8 : z * 8 + 8, c * 128 : c * 128 + 128] = tile


def source_rows(d, row, blocks, table_ref, sources_ref, edge):
    here = d * blocks + row
    west, east, south, north, below, above = [table_ref[face, 0, here] for face in range(6)]

    def beside(slot_id, face):
        return jnp.where(slot_id < 0, -1, table_ref[face, 0, jnp.maximum(slot_id, 0)])

    lane = lanes((1, 128))
    in_north = lane < SOUTH
    near = jnp.where(in_north, north, south)
    far_east = jnp.where(in_north, beside(north, 1), beside(south, 1))
    far_west = jnp.where(in_north, beside(north, 0), beside(south, 0))
    in_east, in_west = east_west_groups(lane, edge)
    rows = [
        slot_source(lane % edge, east, west, north),
        slot_source(lane % edge, east, west, None),
        slot_source(lane % edge, east, west, south),
        jnp.where(
            in_east & (lane % edge == edge - 1),
            far_east,
            jnp.where(in_west & (lane % edge == 0), far_west, near),
        ),
    ]
    for face, own in ((5, above), (4, below)):
        rows += [own, beside(east, face), beside(west, face), beside(north, face), beside(south, face)]
    for r, slot_id in enumerate(rows):
        device = lax.shift_right_arithmetic(slot_id, jnp.int32(blocks.bit_length() - 1))
        sources_ref[d, r : r + 1, :] = jnp.broadcast_to(device, (1, 128))


def east_west_groups(lane, edge):
    group = lane // edge
    return (group == 0) | (group == 5), (group == 1) | (group == 4)


def first_kernel(
    blocks,
    devices,
    table_hbm,
    state_hbm,
    velocity_hbm,
    porosity_hbm,
    post_ref,
    faces_ref,
    sources_ref,
    state_ref,
    velocity_ref,
    porosity_ref,
    lines_ref,
    table_ref,
    sems,
    sem,
    flow_sems,
):
    edge, plane = porosity_ref.shape[1:]
    swapped = first_partner_above()
    row = jnp.minimum(lax.axis_index("blk").astype(jnp.int32), blocks - 1)

    def copy(b):
        return pltpu.make_async_copy(state_hbm.at[b], state_ref.at[b], sems.at[b])

    lookup = pltpu.make_async_copy(table_hbm, table_ref, sem.at[0])

    def flow(b):
        return (
            pltpu.make_async_copy(velocity_hbm.at[b], velocity_ref.at[b], flow_sems.at[0, b]),
            pltpu.make_async_copy(porosity_hbm.at[b], porosity_ref.at[b], flow_sems.at[1, b]),
        )

    for b in range(blocks):
        copy(b).start()
        for other in flow(b):
            other.start()
        if b == 0:
            lookup.start()
    lookup.wait()
    per = -(-devices // blocks)

    def one(b, carry):
        copy(b).wait()
        for other in flow(b):
            other.wait()
        parts = collide_block(
            lambda p, zs, cells: state_ref[b, p, zs, cells],
            velocity_ref.at[b],
            porosity_ref.at[b],
            post_ref.at[b],
            edge,
            plane,
        )
        for (low, left), sens in parts.items():
            post_ref[b, POPS, pl.ds(low, 8), pl.ds(left, 128)] = sens
        for k in range(per):
            source_rows(jnp.minimum(b * per + k, devices - 1), row, blocks, table_ref, sources_ref, edge)
        return carry

    lax.fori_loop(0, blocks, one, 0)
    y_lines(blocks, post_ref, lines_ref, plane)
    for b in range(blocks):
        pack_faces(b, blocks, swapped, post_ref.at[b], lines_ref, faces_ref, edge, plane)


def slab_start(owner_ref, slab, devices):
    start = jnp.int32(0)
    for j in range(devices):
        start = start + jnp.where(j < slab, 2 * owner_ref[j], 0)
    return start


def second_kernel(
    blocks,
    devices,
    chunks,
    owner_hbm,
    before_ref,
    velocity_hbm,
    porosity_hbm,
    halo_ref,
    near_hbm,
    late_hbm,
    faces_ref,
    velocity_ref,
    porosity_ref,
    post_ref,
    state_ref,
    lines_ref,
    turned_ref,
    owner_ref,
    sems,
    sem,
):
    edge, plane = porosity_ref.shape[1:]
    swapped = first_partner_above()
    others = [
        pltpu.make_async_copy(velocity_hbm, velocity_ref, sem.at[1]),
        pltpu.make_async_copy(porosity_hbm, porosity_ref, sem.at[2]),
        pltpu.make_async_copy(owner_hbm, owner_ref, sem.at[0]),
    ]
    for other in others:
        other.start()

    half = blocks // 2

    def result(b, out_hbm, first):
        return pltpu.make_async_copy(post_ref.at[b], out_hbm.at[b - first], sems.at[b])

    def stream(b, carry):
        stream_block(before_ref.at[b], halo_ref.at[b], lines_ref.at[b], state_ref.at[b], edge, insert_halo)
        return carry

    y_halos(blocks, halo_ref, lines_ref)
    lax.fori_loop(0, blocks, stream, 0)
    for other in others:
        other.wait()

    def collide(b, carry):
        parts = collide_block(
            lambda p, zs, cells: state_ref[b, p, zs, cells],
            velocity_ref.at[b],
            porosity_ref.at[b],
            post_ref.at[b],
            edge,
            plane,
        )

        @pl.when(b < half)
        def _():
            result(b, near_hbm, 0).start()

        @pl.when(b >= half)
        def _():
            result(b, late_hbm, half).start()

        for (low, left), sens in parts.items():
            sens = before_ref[b, POPS, pl.ds(low, 8), pl.ds(left, 128)] + sens
            turned_ref[0, b * (plane // 128) + left // 128, pl.ds(low, 8), :] = sens
        return carry

    lax.fori_loop(0, blocks, collide, 0)
    y_lines(blocks, post_ref, lines_ref, plane)

    for b in range(blocks):
        pack_faces(b, blocks, swapped, post_ref.at[b], lines_ref, faces_ref, edge, plane)
    held = blocks * (plane // 128)
    for c in range(held):
        for m in range(1, 4):
            for low in (0, 8):
                turned_ref[m, c, low : low + 8, :] = shift(turned_ref[0, c, low : low + 8, :], -2 * m * edge)
    lane = lanes((edge, 128))
    start = jnp.int32(0)
    for j in range(devices):
        first = lax.div(start + 6, jnp.int32(8)) - 1
        behind = start - 2 - 8 * first
        phase = lax.div(behind, jnp.int32(2))
        turned = [turned_ref[phase, jnp.clip(first + i, 0, held - 1)] for i in range(chunks + 1)]
        kept = lane < 128 - behind * edge
        for i in range(chunks):
            value = jnp.where(kept, turned[i], turned[i + 1])
            at = FACE_ROWS + 16 * i
            if at + 16 <= faces_ref.shape[1]:
                faces_ref[j, at : at + 16, :] = value
            else:
                faces_ref[j, at : at + 8, :] = jnp.where(lane[0:8] < 64, value[0:8], shift(value[8:16], 64))
        start = start + 2 * owner_ref[j]
    for b in range(blocks):
        (result(b, near_hbm, 0) if b < half else result(b, late_hbm, half)).wait()


def last_kernel(blocks, near_ref, late_hbm, halo_ref, out_hbm, late_ref, out_ref, lines_ref, sems):
    edge = late_ref.shape[2]
    half = blocks // 2

    def late(b):
        return pltpu.make_async_copy(late_hbm.at[b - half], late_ref.at[b - half], sems.at[blocks + b - half])

    def result(b):
        return pltpu.make_async_copy(out_ref.at[b], out_hbm.at[b], sems.at[b])

    for b in range(half, blocks):
        late(b).start()

    def one(b, before_ref, one_pop):
        stream_block(before_ref, halo_ref.at[b], lines_ref.at[b], out_ref.at[b], edge, one_pop)
        result(b).start()

    def near_one(b, carry):
        one(b, near_ref.at[b], insert_halo)
        return carry

    def late_one(b, carry):
        late(b).wait()
        one(b, late_ref.at[b - half], stream_pop)
        return carry

    y_halos(blocks, halo_ref, lines_ref)
    lax.fori_loop(0, half, near_one, 0)
    lax.fori_loop(half, blocks, late_one, 0)
    for b in range(blocks):
        result(b).wait()


def route_kernel(devices, sources_ref, faces_ref, first_ref, second_ref, *refs):
    halo_ref, y_ref, above_ref, below_ref = refs[-4:]
    edge = 16
    swapped = first_partner_above()
    lane = lanes((8, 128))
    level = lax.broadcasted_iota(jnp.int32, (8, 128), 0)
    x, group = lane % edge, lane // edge
    in_east, in_west = east_west_groups(lane, edge)
    sides = (0, 128)

    def z_tiles(own, pops):
        out = list(own)
        for i, p in enumerate(pops):
            cx, cy, _ = VELOCITIES[p]
            if cx != 0:
                face = edge - 1 if cx > 0 else 0
                for c in range(2):
                    value = jnp.where(x == face, shift(own[c], cx * (edge - 1)), shift(own[c], -cx))
                    out[c] = jnp.where(level == i, value, out[c])
            if cy != 0:
                outer = 1 if cy > 0 else 0
                face = 7 if cy > 0 else 0
                start = NORTH_POPS.index(p) * edge if cy > 0 else SOUTH + SOUTH_POPS.index(p) * edge
                turned = [shift(side, -cy * edge) for side in own]
                arrived = jnp.broadcast_to(shift(own[0][5:6], face * edge - start), (8, 128))
                inner = jnp.where(group == face, turned[outer], turned[1 - outer])
                rim = jnp.where(group == face, arrived, turned[outer])
                out[1 - outer] = jnp.where(level == i, inner, out[1 - outer])
                out[outer] = jnp.where(level == i, rim, out[outer])
        return out

    def prepare(e, carry):
        first = [first_ref[e, at : at + 8, :] for at in (0, 6)]
        second = [second_ref[e, 4:12, :], shift(second_ref[e, 8:16, :], -2, 0)]
        above = [jnp.where(swapped, a, b) for a, b in zip(first, second)]
        below = [jnp.where(swapped, b, a) for a, b in zip(first, second)]
        for own, pops, ref in ((above, UPPER_POPS, above_ref), (below, LOWER_POPS, below_ref)):
            for at, tile in zip((0, 8), z_tiles(own, pops)):
                ref[e, at : at + 8, :] = tile
        for at in (0, 8):
            own = faces_ref[e, Y_ROWS + at : Y_ROWS + at + 8, :]
            east = jnp.where(x == edge - 1, shift(own, edge - 1), shift(own, -1))
            west = jnp.where(x == 0, shift(own, 1 - edge), shift(own, 1))
            y_ref[e, at : at + 8, :] = jnp.where(in_east, east, jnp.where(in_west, west, own))
        return carry

    lax.fori_loop(0, devices, prepare, 0, unroll=8)

    def pick(index, tiles_of):
        total = None
        for e in range(devices):
            hit = index == e
            tiles = tiles_of(e)
            total = [jnp.where(hit, t, 0.0 if total is None else total[k]) for k, t in enumerate(tiles)]
        return total

    def one(d, carry):
        row = [jnp.broadcast_to(sources_ref[d, r : r + 1, :], (8, 128)) for r in range(14)]
        for at, index in zip((0, 8, 16), row):
            (halo_ref[d, at : at + 8, :],) = pick(index, lambda e: [faces_ref[e, at : at + 8, :]])
        for at, tile in zip((0, 8), pick(row[3], lambda e: [y_ref[e, at : at + 8, :] for at in (0, 8)])):
            halo_ref[d, Y_ROWS + at : Y_ROWS + at + 8, :] = tile
        for pops, base, ref, upper in ((UPPER_POPS, 4, above_ref, True), (LOWER_POPS, 9, below_ref, False)):
            index = [row[base]] * 2
            for i, p in enumerate(pops):
                cx, cy, _ = VELOCITIES[p]
                if cx != 0:
                    here = (level == i) & (x == (edge - 1 if cx > 0 else 0))
                    index = [jnp.where(here, row[base + (1 if cx > 0 else 2)], side) for side in index]
                if cy != 0:
                    outer, face = (1, 7) if cy > 0 else (0, 0)
                    here = (level == i) & (group == face)
                    index[outer] = jnp.where(here, row[base + (3 if cy > 0 else 4)], index[outer])
            for left, at, side in zip(sides, (0, 8), index):
                (tile,) = pick(side, lambda e: [ref[e, at : at + 8, :]])
                top = halo_row(upper, left, 0).start
                halo_ref[d, top : top + 6, :] = tile[0:6]
        return carry

    lax.fori_loop(0, devices, one, 0, unroll=8)


def slab_kernel(
    blocks, devices, chunks, owner_ref, column_ref, rows_ref, out_ref, first_ref, second_ref, field_ref
):
    slab = lax.axis_index("blk").astype(jnp.int32)
    swapped = first_partner_above()
    count, edge, width = out_ref.shape
    start = slab_start(owner_ref, slab, devices)
    group = lanes((edge, width)) // edge
    lane = lanes((edge, width))
    height = blocks * edge

    def chunk(i):
        top = start - 2 + 8 * i
        tiles = [jnp.zeros((edge, width), jnp.float32) for _ in range(8)]
        at = FACE_ROWS + 16 * i
        if at + 16 <= rows_ref.shape[1]:
            values = [rows_ref[e, at : at + 16, :] for e in range(devices)]
        else:
            halves = [rows_ref[e, at : at + 8, :] for e in range(devices)]
            values = [jnp.concatenate([half, shift(half, 64)], axis=0) for half in halves]
        for r in range(0, 8, 2):
            inside = (top + r >= 0) & (top + r < height)
            block_row = lax.div(jnp.clip(top + r, 0, height - 1), jnp.int32(edge))
            for e in range(devices):
                column = column_ref[0, e * blocks + block_row]
                hit = group == jnp.where(inside, column, -1)
                for k in range(r, r + 2):
                    part = pltpu.roll(values[e], lax.rem(column + (8 - k), jnp.int32(8)) * edge, 1)
                    if width > 128:
                        part = jnp.concatenate([part] * (width // 128), axis=1)
                    tiles[k] = jnp.where(hit, part, tiles[k])
        for r in range(8):
            field_ref[i * 8 + r] = tiles[r]

    for i in range(chunks):
        chunk(i)

    def row(r):
        at = r
        mixed = TAP_EDGE * (field_ref[at] + field_ref[at + 4]) + (
            TAP_NEAR * (field_ref[at + 1] + field_ref[at + 3]) + field_ref[at + 2]
        )
        value = mixed
        for step, tap in ((1, TAP_NEAR), (2, TAP_EDGE)):
            left = jnp.where(lane >= step, shift(mixed, step), 0.0)
            right = jnp.where(lane < width - step, shift(mixed, -step), 0.0)
            value = value + tap * (left + right)
        out_ref[r] = value
        low, high = value[0:2], value[edge - 2 : edge]
        first_ref[r] = jnp.where(swapped, high, low)
        second_ref[r] = jnp.where(swapped, low, high)

    by_rows(count, row)


def by_rows(count, body):
    step = 8 if count % 8 == 0 else 4 if count % 4 == 0 else 2

    def several(i, carry):
        for k in range(step):
            body(i * step + k)
        return carry

    lax.fori_loop(0, count // step, several, 0)


def depth_kernel(devices, layers, owner_ref, rows_ref, first_ref, second_ref, out_ref):
    count, edge, width = out_ref.shape
    slab, layer = lax.axis_index("blk").astype(jnp.int32), lax.axis_index("gz").astype(jnp.int32)
    own_rows = jnp.int32(0)
    for j in range(devices):
        own_rows = jnp.where(slab == j, 2 * owner_ref[j], own_rows)
    swapped = first_partner_above()
    depth = lax.broadcasted_iota(jnp.int32, (edge, width), 0)

    def row(r):
        value = rows_ref[r]
        first, second = first_ref[r], second_ref[r]
        below = jnp.where(layer > 0, jnp.where(swapped, second, first), 0.0)
        above = jnp.where(layer < layers - 1, jnp.where(swapped, first, second), 0.0)
        b0, b1, a0, a1 = below[0:1], below[1:2], above[0:1], above[1:2]
        down = jnp.where(depth == 0, b1, shift(value, 1, 0))
        up = jnp.where(depth == edge - 1, a0, shift(value, -1, 0))
        down_2 = jnp.where(depth == 0, b0, jnp.where(depth == 1, b1, shift(value, 2, 0)))
        up_2 = jnp.where(depth == edge - 1, a1, jnp.where(depth == edge - 2, a0, shift(value, -2, 0)))
        total = value + TAP_NEAR * (down + up) + TAP_EDGE * (down_2 + up_2)
        out_ref[r] = jnp.where(r < own_rows, total, 0.0)

    by_rows(count, row)


SMEM = pl.BlockSpec(memory_space=pltpu.SMEM)
VMEM = pl.BlockSpec(memory_space=pltpu.VMEM)


ANY = pl.BlockSpec(memory_space=pl.ANY)


def f32(*shape):
    return jax.ShapeDtypeStruct(shape, jnp.float32)


def hbm(*shape):
    return pltpu.HBM(shape, jnp.float32)


def vmem(*shape):
    return pltpu.VMEM(shape, jnp.float32)


def local(adjoint, velocity, porosity, block_x, neighbours, owner_map):
    blocks, _, edge, plane = adjoint.shape[1:]
    devices, layers = lax.axis_size("blk"), lax.axis_size("gz")
    table = pltpu.with_memory_space_constraint(jnp.transpose(neighbours, (2, 0, 1)), pltpu.HBM)
    state, flow, design = [pltpu.with_memory_space_constraint(x[0], pltpu.HBM) for x in (adjoint, velocity, porosity)]
    rows_cap = 2 * (3 * (blocks * edge // 2) // devices)
    chunks = -(-(rows_cap + 4) // 8)
    width = devices * edge
    first_pairs = [(g, g ^ 1) for g in range(layers)]
    second_pairs = [(g, (g + 1 if g % 2 else g - 1) % layers) for g in range(layers)]
    near_shape, late_shape = [(count,) + state.shape[1:] for count in (blocks // 2, blocks - blocks // 2)]
    faces_shape = (devices, FACE_ROWS, 128)
    row_count = 16 * chunks - (8 if 0 < (rows_cap + 4) % 8 <= 4 else 0)
    post_shape = (blocks, POPS + 1, edge, plane)
    params = pltpu.CompilerParams(vmem_limit_bytes=32 * 1024 * 1024)

    def to_halo(gathered, *others):
        first = lax.ppermute(gathered[:, FIRST : FIRST + 16], "gz", first_pairs)
        second = lax.ppermute(gathered[:, SECOND - 4 : SECOND + 12], "gz", second_pairs)
        halo = pl.pallas_call(
            functools.partial(route_kernel, devices),
            out_shape=f32(*faces_shape),
            in_specs=[VMEM] * 4 + [ANY] * len(others),
            out_specs=VMEM,
            scratch_shapes=[vmem(devices, 16, 128)] * 3,
            compiler_params=params,
            name="route",
        )(sources, gathered, first, second, *others)
        return lax.all_to_all(halo, "blk", 0, 0, tiled=True)

    def ahead(before, gathered):
        return pl.pallas_call(
            functools.partial(ahead_kernel, before.shape[0]),
            out_shape=vmem(*before.shape),
            in_specs=[VMEM, ANY],
            out_specs=VMEM,
            compiler_params=params,
            name="shift_inside",
        )(before, gathered)

    inputs = [vmem(*state.shape), vmem(*flow.shape), vmem(*design.shape)]
    post, faces, sources = pl.pallas_call(
        functools.partial(first_kernel, blocks, devices),
        out_shape=(
            vmem(*post_shape),
            f32(*faces_shape),
            jax.ShapeDtypeStruct((devices, SOURCES, 128), jnp.int32),
        ),
        in_specs=[ANY] * 4,
        out_specs=(VMEM,) * 3,
        scratch_shapes=inputs
        + [
            vmem(blocks, 32, 128),
            pltpu.SMEM(table.shape, jnp.int32),
            pltpu.SemaphoreType.DMA((blocks,)),
            pltpu.SemaphoreType.DMA((1,)),
            pltpu.SemaphoreType.DMA((2, blocks)),
        ],
        compiler_params=params,
        name="collide_first",
    )(table, state, flow, design)
    gathered = lax.all_to_all(faces, "blk", 0, 0, tiled=True)
    post = ahead(post, gathered)
    halo = to_halo(gathered, post)
    near, late, faces = pl.pallas_call(
        functools.partial(second_kernel, blocks, devices, chunks),
        out_shape=(hbm(*near_shape), hbm(*late_shape), f32(devices, FACE_ROWS + row_count, 128)),
        in_specs=[ANY, VMEM, ANY, ANY, VMEM],
        out_specs=(ANY, ANY, VMEM),
        scratch_shapes=inputs[1:]
        + [
            vmem(*state.shape),
            vmem(*state.shape),
            vmem(blocks, 32, 128),
            vmem(4, blocks * plane // 128, edge, 128),
            pltpu.SMEM(owner_map.shape, jnp.int32),
            pltpu.SemaphoreType.DMA((blocks,)),
            pltpu.SemaphoreType.DMA((3,)),
        ],
        compiler_params=params,
        name="stream_collide",
    )(owner_map, post, flow, design, halo)
    gathered = lax.all_to_all(faces, "blk", 0, 0, tiled=True)
    near = ahead(near, gathered)
    halo = to_halo(gathered, near)
    slab_shape, ends = (rows_cap, edge, width), (rows_cap, 2, width)
    slab, first, second = pl.pallas_call(
        functools.partial(slab_kernel, blocks, devices, chunks),
        out_shape=(f32(*slab_shape), f32(*ends), f32(*ends)),
        in_specs=[SMEM, SMEM, VMEM],
        out_specs=(VMEM,) * 3,
        scratch_shapes=[vmem(chunks * 8, edge, width)],
        compiler_params=params,
        name="slab_rows",
    )(owner_map, block_x, gathered)
    first = lax.ppermute(first, "gz", first_pairs)
    second = lax.ppermute(second, "gz", second_pairs)
    smoothed = pl.pallas_call(
        functools.partial(depth_kernel, devices, layers),
        out_shape=f32(*slab_shape),
        in_specs=[SMEM, VMEM, VMEM, VMEM],
        out_specs=VMEM,
        compiler_params=params,
        name="slab_depth",
    )(owner_map, slab, first, second)
    moved = pl.pallas_call(
        functools.partial(last_kernel, blocks),
        out_shape=hbm(*state.shape),
        in_specs=[VMEM, ANY, VMEM],
        out_specs=ANY,
        scratch_shapes=[
            vmem(*late_shape),
            vmem(*state.shape),
            vmem(blocks, 32, 128),
            pltpu.SemaphoreType.DMA((2 * blocks - blocks // 2,)),
        ],
        compiler_params=params,
        name="stream_last",
    )(near, pltpu.with_memory_space_constraint(late, pltpu.HBM), halo)
    return (moved[None], smoothed[None, None])


def solution(mesh):
    placed = (
        P("gz", "blk", None, None, None),
        P("gz", "blk", None, None, None),
        P("gz", "blk", None, None),
        P("gz", None),
        P("gz", None, None),
        P(),
    )
    return jax.shard_map(
        local,
        mesh=mesh,
        in_specs=placed,
        out_specs=(P("gz", "blk", None, None, None), P("gz", "blk", None, None, None)),
        check_vma=False,
    )
```
